512 devices in a mesh: gen: 32 (over z_hi, x, core), tp: 16 (over y, z_lo).
Axes of the slice: x: 4, y: 4, z: 16 (z_hi: 4, z_lo: 4; z = z_hi * 4 + z_lo), core: 2. Of those that a mesh axis runs over, the one named last changes fastest.
Arguments:
- embeddings: bfloat16 [2, 2048, 5120], P(None, 'gen', 'tp'), may hold values from -6 to 6
- cache: bfloat16 [2048, 128, 1024], P(('gen', 'tp'))
- lengths: int32 [2048], P(('gen', 'tp')), may hold values from 1 to 128, as said below
- attn_gain: bfloat16 [5120], P('tp'), may hold values from 0.099609375 to 1.8984375
- wqkv: bfloat16 [5120, 3584], P('tp', 'gen'), may hold values from -0.078125 to 0.078125
- wout: bfloat16 [2560, 5120], P('gen', 'tp'), may hold values from -0.125 to 0.125
- final_gain: bfloat16 [5120], replicated, may hold values from 0.099609375 to 1.8984375
- head: bfloat16 [5120, 131072], P(None, ('gen', 'tp'))
- kept: int32 [16, 2048, 2], P('tp', 'gen'), may hold values from 0 to 63, all different within a row; in each aligned block of 64 rows (0 to 63, 64 to 127, ..., all dimensions but the last counted through in order) at most 2 rows name the same one
- chosen: int32 [2, 2048], P(None, 'gen'), may hold values from 0 to 4095
Outputs:
- logprobs: float32 [2, 2048], P(None, ('gen', 'tp'))
- last_hidden: bfloat16 [2048, 5120], P('gen', 'tp')
- new_entries: bfloat16 [2, 2048, 1024], P(None, ('gen', 'tp'))
The draws below stay inside these ranges and needn't reach their ends.
Inputs may be any that keep to these rules, and one draw needn't show every extreme that they name: Entries of one row within a slice are distinct; among the rows of one generator replica no block of a slice is kept by more than 2 rows, and some block is kept by exactly 2. `lengths`: some row has a full cache of 128 positions.
All inputs are finite; a program needn't handle non-finite values.
Results may differ from the reference program's by a relative error of at most 0.0083.
Values may be sent and summed in bfloat16 or wider, within the bound.
No kernel may reach another device: no remote copies, remote signals or barrier semaphores. Data moves between devices by JAX's collectives and lax.ppermute only.
A program may use at most 64 MiB of HBM per device.

```python
import math
import jax
import jax.numpy as jnp
import numpy as np
from jax import lax

D = 5120
QUERY_HEADS = 20
KEY_VALUE_HEADS = 4
HEAD_SIZE = 128
VOC_DEV = 256
BLOCK = 128
KPS = 2
STEPS = 2
ROWS_GEN = 64
STORED_PLACES = 128
MOST = 2
SEQUENCES_ALL = 2048
QKV = 3584
VOCAB = 131072
N_GEN = 32
N_TP = 16


def draw_cache(key, part):
    key = jax.random.fold_in(key, 11)
    array_shape = (SEQUENCES_ALL, STORED_PLACES, 2 * KEY_VALUE_HEADS * HEAD_SIZE)
    return jax.random.normal(key, array_shape, jnp.float32).astype(jnp.bfloat16)


def draw_head(key, part):
    key = jax.random.fold_in(key, 12)
    array_shape = (D, VOCAB)
    factor = 3.0 / math.sqrt(D)
    return (jax.random.normal(key, array_shape, jnp.float32) * factor).astype(jnp.bfloat16)


def draw_lengths(key, part):
    key = jax.random.fold_in(key, 13)
    frequency_radix = jax.random.randint(key, (SEQUENCES_ALL,), 1, STORED_PLACES + 1)
    filled = jax.random.randint(jax.random.fold_in(key, 1), (), 0, SEQUENCES_ALL)
    return jnp.where(jnp.arange(SEQUENCES_ALL) == filled, STORED_PLACES, frequency_radix).astype(jnp.int32)


def with_ends(array, key, smallest, high):
    longest = array.shape.index(max(array.shape))
    spots = []
    for shift in (0, 1):
        where = [jax.random.randint(jax.random.fold_in(key, axis), (), 0, length) for axis, length in enumerate(array.shape)]
        where[longest] = (where[longest] + shift) % array.shape[longest]
        spots.append(tuple(where))
    return array.at[spots[0]].set(smallest).at[spots[1]].set(high)


def block_levels(own_key, shape, cuts, least, largest):
    level = 1.0
    for dim, blocks in cuts:
        draws = jax.random.uniform(jax.random.fold_in(jax.random.fold_in(own_key, 6), dim), (blocks,), jnp.float32, least / len(cuts), largest / len(cuts))
        level = level * jnp.repeat(jnp.exp(draws), shape[dim] // blocks).reshape((-1,) + (1,) * (len(shape) - 1 - dim))
    return level


def routed_block(rng, own, number, rows, number_of, top, bound, slope):
    ranking = jax.random.permutation(rng, number_of)
    crowded, usual = shares(number_of, rows * top, bound, slope, True), shares(number_of, rows * top, bound, slope, False)
    places = jnp.arange(number_of)

    def named(sizes, turn):
        used = int((sizes > 0).sum())
        fixed = max(1, used // 4)
        shifted = fixed + (places - fixed + turn * (used - fixed)) % max(1, number_of - fixed)
        return jnp.zeros((number_of,), jnp.int32).at[ranking[jnp.where(places < fixed, places, shifted)]].set(jnp.asarray(sizes, jnp.int32))

    sizes = jnp.where(number % 4 == 0, named(crowded, number // 4), named(usual, number - number // 4 - 1))
    mixed = jax.random.permutation(jax.random.fold_in(own, 3), number_of)
    source_of, taker = mixed[0:number_of // 2 * 2:2], mixed[1:number_of // 2 * 2:2]
    margin = jnp.minimum(sizes[source_of] - 1, bound - sizes[taker]) // 2
    margin = jnp.where((source_of == ranking[0]) | (taker == ranking[0]) | (sizes[taker] == 0), 0, jnp.maximum(margin, 0))
    shifted = jax.random.randint(jax.random.fold_in(own, 4), (number_of // 2,), 0, 1 << 20) % (margin + 1)
    sizes = sizes.at[source_of].add(-shifted).at[taker].add(shifted)
    items = jnp.searchsorted(jnp.cumsum(sizes), jnp.arange(rows * top), side="right").astype(jnp.int32)
    table = items.reshape(top, rows).T
    table = table[jax.random.permutation(jax.random.fold_in(own, 1), rows)]
    turn = jax.random.randint(jax.random.fold_in(own, 2), (rows, 1), 0, top)
    return jnp.take_along_axis(table, (jnp.arange(top)[None, :] + turn) % top, axis=1)


def shares(number_of, total, limit, lean, full):
    loads = [(1 << 20) // math.isqrt(grade ** lean) + 1 for grade in range(1, number_of + 1)]
    largest = limit if full else min(limit, max(-(-total // number_of), total * loads[0] // sum(loads)))
    least = 1 if total - largest >= number_of - 1 else 0
    holding, rest = [largest] + [least] * (number_of - 1), total - largest - least * (number_of - 1)
    while rest > 0:
        candidates = [i for i in range(1, number_of) if holding[i] < largest] or [i for i in range(1, number_of) if holding[i] < limit]
        whole, budget = sum([loads[i] for i in candidates]), rest
        for i in candidates:
            more = min(limit - holding[i], max(1, budget * loads[i] // whole), rest)
            holding[i] = holding[i] + more
            rest = rest - more
    return np.array(holding)


def normal_values(stream_key, dims, width, reach, split=(), kind=jnp.bfloat16):
    values = width * jax.random.normal(stream_key, dims, jnp.float32)
    if split:
        values = values * block_levels(stream_key, dims, split, -0.22, 0.18)
    return jnp.clip(values, -reach, reach).astype(kind)


def setup_inputs(seed: int = 0) -> dict:
    splits = jax.random.split(jax.random.key(seed), 11)
    embeddings = normal_values(splits[0], (STEPS, SEQUENCES_ALL, D), 1.0, 6.0, ((1, 32), (2, 16)))
    cache = draw_cache(jax.random.fold_in(splits[10], 71), 0)
    lengths = draw_lengths(jax.random.fold_in(splits[10], 71), 0)
    attn_gain = jnp.clip(1.0 + 0.18 * jax.random.normal(splits[3], (D,), jnp.float32), 0.099609375, 1.8984375).astype(jnp.bfloat16)
    wqkv = normal_values(splits[4], (D, QKV), D ** -0.5, 0.078125, ((0, 16), (1, 32)))
    wout = normal_values(splits[5], (QUERY_HEADS * HEAD_SIZE, D), (QUERY_HEADS * HEAD_SIZE) ** -0.5, 0.125, ((0, 32), (1, 16)))
    final_gain = jnp.clip(1.0 + 0.18 * jax.random.normal(splits[6], (D,), jnp.float32), 0.099609375, 1.8984375).astype(jnp.bfloat16)
    head = draw_head(jax.random.fold_in(splits[10], 71), 0)
    kept_keys = jax.random.split(jax.random.fold_in(splits[8], 1), N_TP * SEQUENCES_ALL // ROWS_GEN)
    kept_turns = jax.random.permutation(jax.random.fold_in(splits[8], 3), N_TP * SEQUENCES_ALL // ROWS_GEN)
    kept = jax.vmap(lambda own, number: routed_block(jax.random.fold_in(splits[8], 2), own, number, ROWS_GEN, VOC_DEV // BLOCK * N_GEN, KPS, MOST, 2))(kept_keys, kept_turns).reshape((N_TP, SEQUENCES_ALL, KPS))
    chosen = with_ends(jax.random.randint(splits[9], (STEPS, SEQUENCES_ALL), 0, N_TP * KPS * BLOCK), jax.random.fold_in(splits[9], 1), 0, (N_TP * KPS * BLOCK) - 1).astype(jnp.int32)
    return dict(embeddings=embeddings, cache=cache, lengths=lengths, attn_gain=attn_gain, wqkv=wqkv, wout=wout, final_gain=final_gain, head=head, kept=kept, chosen=chosen)


epsilon = 1e-06
rope_base = 1000000.0

def apply_rotary(vectors, token_positions):
    half_width = HEAD_SIZE // 2
    exponent = jnp.arange(half_width, dtype=jnp.float32) * (2.0 / HEAD_SIZE)
    inverse = jnp.power(jnp.float32(rope_base), -exponent)
    angles = token_positions.astype(jnp.float32)[:, None, None] * inverse[None, None, :]
    cosine = jnp.cos(angles)
    sine = jnp.sin(angles)
    first_half = vectors[..., :half_width]
    second_half = vectors[..., half_width:]
    return jnp.concatenate([first_half * cosine - second_half * sine, second_half * cosine + first_half * sine], axis=-1)

def attend(operands):
    query_rows, cache_entries_held, row_lengths, fresh_keys, fresh_values = operands
    row_number = query_rows.shape[0]
    key_value_width = KEY_VALUE_HEADS * HEAD_SIZE
    previous_keys = cache_entries_held[:, :, :key_value_width].reshape(row_number, STORED_PLACES, KEY_VALUE_HEADS, HEAD_SIZE).astype(jnp.float32)
    previous_values = cache_entries_held[:, :, key_value_width:].reshape(row_number, STORED_PLACES, KEY_VALUE_HEADS, HEAD_SIZE).astype(jnp.float32)
    grouped_queries = query_rows.reshape(row_number, KEY_VALUE_HEADS, QUERY_HEADS // KEY_VALUE_HEADS, HEAD_SIZE).astype(jnp.float32)
    scale = HEAD_SIZE ** (-0.5)
    old_scores = jnp.einsum('rkgd,rpkd->rkgp', grouped_queries, previous_keys) * scale
    visible = jnp.arange(STORED_PLACES, dtype=jnp.int32)[None, :] < row_lengths[:, None]
    old_scores = jnp.where(visible[:, None, None, :], old_scores, -jnp.inf)
    new_scores = jnp.einsum('rkgd,rnkd->rkgn', grouped_queries, fresh_keys.astype(jnp.float32)) * scale
    peak = jnp.maximum(lax.optimization_barrier(jnp.max(old_scores, axis=-1)), lax.optimization_barrier(jnp.max(new_scores, axis=-1)))[..., None]
    old_exp = jnp.exp(old_scores - peak)
    new_exp = jnp.exp(new_scores - peak)
    total = lax.optimization_barrier(jnp.sum(old_exp, axis=-1, keepdims=True)) + lax.optimization_barrier(jnp.sum(new_exp, axis=-1, keepdims=True))
    old_weights = (old_exp / total).astype(jnp.bfloat16).astype(jnp.float32)
    new_weights = (new_exp / total).astype(jnp.bfloat16).astype(jnp.float32)
    mixed = jnp.einsum('rkgp,rpkd->rkgd', old_weights, previous_values)
    mixed = mixed + jnp.einsum('rkgn,rnkd->rkgd', new_weights, fresh_values.astype(jnp.float32))
    return mixed.reshape(row_number, QUERY_HEADS * HEAD_SIZE).astype(jnp.bfloat16)

def block_stats(logits, blocks, starting_shifts, held):
    shaped = logits.reshape(logits.shape[0], held, BLOCK)
    pick = jnp.arange(held, dtype=jnp.int32)[None, :] == blocks[:, None]
    selected = lax.optimization_barrier(jnp.sum(jnp.where(pick[:, :, None], shaped, 0.0), axis=1))
    peak = lax.optimization_barrier(jnp.max(selected, axis=1))
    total = lax.optimization_barrier(jnp.sum(jnp.exp(selected - peak[:, None]), axis=1))
    hit = jnp.arange(BLOCK, dtype=jnp.int32)[None, :] == starting_shifts[:, None]
    picked = lax.optimization_barrier(jnp.sum(jnp.where(hit, selected, 0.0), axis=1))
    return (peak, total, picked)

def head_logprob(normed, head, kept, codes):
    held = VOC_DEV // BLOCK
    chosen_rows = max(2, ROWS_GEN * KPS // (held * N_GEN))
    selection = N_GEN * held * chosen_rows
    row_total = normed.shape[0]
    pair_total = row_total * KPS
    code_slice = codes // (KPS * BLOCK)
    code_entry = codes // BLOCK % KPS
    code_offset = codes % BLOCK
    pair_row = jnp.arange(pair_total, dtype=jnp.int32) // KPS
    pair_entry = jnp.arange(pair_total, dtype=jnp.int32) % KPS

    def owner_work(flat_index):
        slice_index = flat_index % N_TP
        owner_index = flat_index // N_TP
        blocks = lax.dynamic_index_in_dim(kept, slice_index, 0, keepdims=False).reshape(pair_total)
        owned = blocks // held == owner_index
        order = jnp.argsort(jnp.where(owned, 0, 1).astype(jnp.int32), stable=True)[:selection].astype(jnp.int32)
        rows_of = pair_row[order]
        weights = lax.dynamic_slice_in_dim(head, ((owner_index * N_TP + slice_index) * VOC_DEV).astype(jnp.int32), VOC_DEV, 1)
        logits = jnp.dot(jnp.take(normed, rows_of, axis=0), weights, preferred_element_type=jnp.float32)
        starting_shifts = jnp.where((code_slice[rows_of] == slice_index) & (code_entry[rows_of] == pair_entry[order]), code_offset[rows_of], -1)
        peak, total, picked = block_stats(logits, blocks[order] % held, starting_shifts, held)
        target = jnp.where(owned[order], slice_index * pair_total + order, N_TP * pair_total).astype(jnp.int32)
        return (target, peak, total, picked)
    target, peak, total, picked = lax.map(owner_work, jnp.arange(N_GEN * N_TP, dtype=jnp.int32))
    target = target.reshape(-1)
    peaks = jnp.zeros((N_TP * pair_total,), jnp.float32).at[target].set(peak.reshape(-1), mode='drop')
    totals = jnp.zeros((N_TP * pair_total,), jnp.float32).at[target].set(total.reshape(-1), mode='drop')
    picks = jnp.zeros((N_TP * pair_total,), jnp.float32).at[target].set(picked.reshape(-1), mode='drop')
    peaks = peaks.reshape(N_TP, row_total, KPS)
    totals = totals.reshape(N_TP, row_total, KPS)
    picks = picks.reshape(N_TP, row_total, KPS)
    best = lax.optimization_barrier(jnp.max(peaks, axis=(0, 2)))
    probability_grand = lax.optimization_barrier(jnp.sum(totals * jnp.exp(peaks - best[None, :, None]), axis=(0, 2)))
    return lax.optimization_barrier(jnp.sum(picks, axis=(0, 2))) - best - jnp.log(probability_grand)

def reference(embeddings, cache, lengths, attn_gain, wqkv, wout, final_gain, head, kept, chosen):
    total_row_count = embeddings.shape[1]
    query_width = QUERY_HEADS * HEAD_SIZE
    key_value_width = KEY_VALUE_HEADS * HEAD_SIZE
    gain_wide = attn_gain.astype(jnp.float32)
    final_wide = final_gain.astype(jnp.float32)
    key_list = []
    value_list = []
    entry_list = []
    prob_list = []
    layer_out = embeddings[0]

    def grouped_rows(tensor_in):
        return tensor_in.reshape((N_GEN, total_row_count // N_GEN) + tensor_in.shape[1:])
    for step_index in range(STEPS):
        wide_in = embeddings[step_index].astype(jnp.float32)
        mean_square = lax.optimization_barrier(jnp.mean(wide_in * wide_in, axis=1))
        scaled = (wide_in * gain_wide).astype(jnp.bfloat16)
        projected_hidden = jnp.dot(scaled, wqkv, preferred_element_type=jnp.float32) * lax.rsqrt(mean_square + epsilon)[:, None]
        token_positions = lengths + step_index
        query_rows = apply_rotary(projected_hidden[:, :query_width].reshape(total_row_count, QUERY_HEADS, HEAD_SIZE), token_positions).astype(jnp.bfloat16)
        appended_keys = apply_rotary(projected_hidden[:, query_width:query_width + key_value_width].reshape(total_row_count, KEY_VALUE_HEADS, HEAD_SIZE), token_positions).astype(jnp.bfloat16)
        appended_values = projected_hidden[:, query_width + key_value_width:].reshape(total_row_count, KEY_VALUE_HEADS, HEAD_SIZE).astype(jnp.bfloat16)
        key_list.append(appended_keys)
        value_list.append(appended_values)
        entry_list.append(jnp.concatenate([appended_keys.reshape(total_row_count, key_value_width), appended_values.reshape(total_row_count, key_value_width)], axis=1))
        stacked_keys = jnp.stack(key_list, axis=1)
        stacked_values = jnp.stack(value_list, axis=1)
        mixed = lax.map(attend, (grouped_rows(query_rows), grouped_rows(cache), grouped_rows(lengths), grouped_rows(stacked_keys), grouped_rows(stacked_values)))
        mixed = mixed.reshape(total_row_count, query_width)
        layer_out = (wide_in + jnp.dot(mixed, wout, preferred_element_type=jnp.float32)).astype(jnp.bfloat16)
        hidden = lax.optimization_barrier(layer_out).astype(jnp.float32)
        normed = (hidden * lax.rsqrt(lax.optimization_barrier(jnp.mean(hidden * hidden, axis=1)) + epsilon)[:, None] * final_wide).astype(jnp.bfloat16)
        prob_list.append(head_logprob(normed, head, kept, chosen[step_index]))
    return (jnp.stack(prob_list, axis=0), layer_out, jnp.stack(entry_list, axis=0))
```

```python
import jax
import jax.numpy as jnp
from jax import lax
from jax.experimental import pallas as pl
from jax.experimental.pallas import tpu as pltpu
from jax.sharding import PartitionSpec as P

D = 5120
QUERY_HEADS = 20
KEY_VALUE_HEADS = 4
GROUP = QUERY_HEADS // KEY_VALUE_HEADS
HEAD_SIZE = 128
BLOCK = 128
KPS = 2
STEPS = 2
QKV = 3584
GEN = 32
TP = 16
ROWS = 64
OWN = ROWS // TP
PLACES = 128

epsilon = 1e-06
rope_base = 1000000.0

bf16 = jnp.bfloat16
f32 = jnp.float32
i32 = jnp.int32
VMEM_BYTES = 48 * 1024 * 1024


def call(kernel, out_shape, *args, scalars=0, scratch=()):
    specs = [pl.BlockSpec(memory_space=pltpu.SMEM)] * scalars
    specs += [pl.BlockSpec(memory_space=pltpu.VMEM)] * (len(args) - scalars)
    return pl.pallas_call(
        kernel,
        out_shape=out_shape,
        in_specs=specs,
        out_specs=jax.tree.map(lambda _: pl.BlockSpec(memory_space=pltpu.VMEM), out_shape),
        scratch_shapes=list(scratch),
        compiler_params=pltpu.CompilerParams(vmem_limit_bytes=VMEM_BYTES),
    )(*args)


def shape(dims, dtype):
    return jax.ShapeDtypeStruct(dims, dtype)


def nt_dot(a, b):
    return lax.dot_general(a, b, (((1,), (1,)), ((), ())), preferred_element_type=f32)


def project_kernel(me_ref, x_ref, gain_ref, own_ref, other_ref, out_ref):
    me = me_ref[0]
    core = lax.rem(me, 2)
    wide = x_ref[...].astype(f32)
    scaled = (wide * gain_ref[...].astype(f32)).astype(bf16)
    for z in range(4):
        pieces = []
        for x in range(4):
            spot = jnp.bitwise_xor(z * 4 + x, me // 2)
            place = lax.rem(spot, 4) * 4 + spot // 4
            a = own_ref[place]
            b = other_ref[place]
            pieces.append(jnp.where(core == 0, a, b))
            pieces.append(jnp.where(core == 0, b, a))
        part = nt_dot(scaled, jnp.concatenate(pieces, axis=0))
        out_ref[:, z * 896 : (z + 1) * 896] = part.astype(bf16)
    squares = jnp.sum(wide * wide, axis=1, keepdims=True)
    high = squares.astype(bf16)
    low = (squares - high.astype(f32)).astype(bf16)
    lane = lax.broadcasted_iota(i32, (TP * 8, 128), 1)
    extra = jnp.where(lane == 0, high.astype(f32), jnp.where(lane == 1, low.astype(f32), 0.0))
    out_ref[:, QKV:] = extra.astype(bf16)


def attend_kernel(parts_ref, cache_ref, lengths_ref, cos_ref, sin_ref, mixed_ref, entry_ref):
    total = parts_ref[0].astype(f32)
    for t in range(1, TP):
        total = total + parts_ref[t].astype(f32)
    squares = total[:, QKV : QKV + 1] + total[:, QKV + 1 : QKV + 2]
    total = total[:, :QKV] * lax.rsqrt(squares / D + epsilon)
    cosine, sine = cos_ref[...], sin_ref[...]

    def head(index):
        return total[:, index * HEAD_SIZE : (index + 1) * HEAD_SIZE]

    def rotated(index):
        vec = head(index)
        swapped = jnp.concatenate([vec[:, HEAD_SIZE // 2 :], vec[:, : HEAD_SIZE // 2]], axis=1)
        return vec * cosine + swapped * sine

    rows = 8 * GROUP
    row = lax.rem(lax.broadcasted_iota(i32, (8, OWN * PLACES), 0), OWN)
    lane = lax.broadcasted_iota(i32, (8, OWN * PLACES), 1)
    old_ok = jnp.logical_and(lane // PLACES == row, lax.rem(lane, PLACES) < lengths_ref[:, :1])
    old_bias = jnp.tile(jnp.where(old_ok, 0.0, -jnp.inf), (GROUP, 1))
    slot = lax.broadcasted_iota(i32, (8, 8), 1)
    fresh = lax.broadcasted_iota(i32, (8, 8), 0)
    new_ok = jnp.logical_and(lax.rem(slot, OWN) == lax.rem(fresh, OWN), slot // OWN <= fresh // OWN)
    new_bias = jnp.tile(jnp.where(new_ok, 0.0, -jnp.inf), (GROUP, 1))
    scale = HEAD_SIZE ** (-0.5)
    width = KEY_VALUE_HEADS * HEAD_SIZE
    for k in range(KEY_VALUE_HEADS):
        at = k * HEAD_SIZE
        new_k = rotated(QUERY_HEADS + k).astype(bf16)
        new_v = head(QUERY_HEADS + KEY_VALUE_HEADS + k).astype(bf16)
        entry_ref[:, at : at + HEAD_SIZE] = new_k
        entry_ref[:, width + at : width + at + HEAD_SIZE] = new_v
        query = jnp.concatenate([rotated(k * GROUP + h) for h in range(GROUP)], axis=0).astype(bf16)
        old_k = cache_ref[:, :, at : at + HEAD_SIZE].reshape(OWN * PLACES, HEAD_SIZE)
        old_v = cache_ref[:, :, width + at : width + at + HEAD_SIZE].reshape(OWN * PLACES, HEAD_SIZE)
        old_s = nt_dot(query, old_k) * scale + old_bias
        new_s = nt_dot(query, new_k) * scale + new_bias
        peak = jnp.maximum(
            jnp.max(old_s, axis=1, keepdims=True), jnp.max(new_s, axis=1, keepdims=True)
        )
        old_e, new_e = jnp.exp(old_s - peak), jnp.exp(new_s - peak)
        whole = jnp.sum(old_e, axis=1, keepdims=True) + jnp.sum(new_e, axis=1, keepdims=True)
        old_w, new_w = (old_e / whole).astype(bf16), (new_e / whole).astype(bf16)
        mixed = jnp.dot(old_w, old_v, preferred_element_type=f32)
        mixed = mixed + jnp.dot(new_w, new_v, preferred_element_type=f32)
        for h in range(GROUP):
            to = (k * GROUP + h) * HEAD_SIZE
            mixed_ref[:, to : to + HEAD_SIZE] = mixed[8 * h : 8 * h + 8].astype(bf16)


def logits_kernel(me_ref, own_ref, other_ref, gain_ref, spot_ref, head_ref, out_ref, pairs_ref):
    me = me_ref[0]
    lane = lax.broadcasted_iota(i32, (256, 256), 1)
    for pair in range(GEN // 2):
        where = jnp.bitwise_xor(pair, me // 2)
        place = lax.rem(where, 4) * 4 + where // 4
        rows = jnp.concatenate([own_ref[place], other_ref[place]], axis=0)
        pick = (spot_ref[:, pair : pair + 1] == lane).astype(f32).astype(bf16)
        taken = jnp.dot(pick, rows, preferred_element_type=f32)
        for b in range(2 * TP):
            pairs_ref[b, 8 * pair : 8 * pair + 8, :] = taken[8 * b : 8 * b + 8]
    gain = gain_ref[...].astype(f32)
    column = lax.broadcasted_iota(i32, (128, 128), 1)
    squares = jnp.zeros((128, 128), f32)
    for t in range(TP):
        for j in range(2):
            raw = pairs_ref[2 * t + j]
            squares = jnp.where(
                column == 2 * t + j, jnp.sum(raw * raw, axis=1, keepdims=True), squares
            )
            part = jnp.dot(
                (raw * gain).astype(bf16),
                head_ref[t, :, j * BLOCK : (j + 1) * BLOCK],
                preferred_element_type=f32,
            )
            out_ref[t, j * 128 : (j + 1) * 128, :] = part.astype(bf16)
    squares = squares.T
    high = squares.astype(bf16).astype(f32)
    low = squares - high
    line = lax.broadcasted_iota(i32, (16, 128), 0)
    for t in range(TP):
        extra = jnp.zeros((16, 128), f32)
        for j in range(2):
            b = 2 * t + j
            extra = jnp.where(line == 2 * j, high[b : b + 1], extra)
            extra = jnp.where(line == 2 * j + 1, low[b : b + 1], extra)
        out_ref[t, 256:272, :] = extra.astype(bf16)


def stats_kernel(parts_ref, offset_ref, out_ref):
    total = parts_ref[0].astype(f32)
    for t in range(1, TP):
        total = total + parts_ref[t].astype(f32)
    token = lax.broadcasted_iota(i32, (BLOCK, 128), 0)
    line = lax.broadcasted_iota(i32, (8, 128), 0)
    out = jnp.zeros((8, 128), f32)
    for j in range(2):
        squares = total[256 + 2 * j : 257 + 2 * j] + total[257 + 2 * j : 258 + 2 * j]
        logits = total[j * 128 : (j + 1) * 128].T * lax.rsqrt(squares / D + epsilon)
        peak = jnp.max(logits, axis=0, keepdims=True)
        mass = jnp.sum(jnp.exp(logits - peak), axis=0, keepdims=True)
        hit = jnp.where(token == offset_ref[j : j + 1] - 1, logits, 0.0)
        picked = jnp.sum(hit, axis=0, keepdims=True)
        for at, value in enumerate((peak, mass, picked)):
            out = jnp.where(line == 3 * j + at, value, out)
    out_ref[...] = out


def rows_kernel(stats_ref, row_ref, out_ref):
    mine = lax.broadcasted_iota(i32, (ROWS, GEN), 0)
    lane = lax.broadcasted_iota(i32, (ROWS, 128), 1)
    out = jnp.zeros((ROWS, 128), f32)
    for s in range(STEPS):
        best = jnp.full((ROWS, 1), -jnp.inf, f32)
        combos = [(j, slot) for j in range(2) for slot in range(2)]
        masks = [row_ref[2 * j + slot : 2 * j + slot + 1, :] == mine for j, slot in combos]

        def stat(which, j, slot):
            at = (3 * j + which) * 4 + slot * 2 + s
            return stats_ref[at : at + 1, :]

        for mask, (j, slot) in zip(masks, combos):
            peak = jnp.where(mask, stat(0, j, slot), -jnp.inf)
            best = jnp.maximum(best, jnp.max(peak, axis=1, keepdims=True))
        mass = jnp.zeros((ROWS, 1), f32)
        picked = jnp.zeros((ROWS, 1), f32)
        for mask, (j, slot) in zip(masks, combos):
            grown = stat(1, j, slot) * jnp.exp(jnp.where(mask, stat(0, j, slot), best) - best)
            mass = mass + jnp.sum(jnp.where(mask, grown, 0.0), axis=1, keepdims=True)
            picked = picked + jnp.sum(
                jnp.where(mask, stat(2, j, slot), 0.0), axis=1, keepdims=True
            )
        for at, value in enumerate((best, mass, picked)):
            out = jnp.where(lane == 3 * s + at, value, out)
    out_ref[...] = out


def gen_index(z, x, core):
    return (z * 4 + x) * 2 + core


def exchange(value, axis, k):
    pairs = []
    for g in range(GEN):
        z, x, core = g // 8, g // 2 % 4, g % 2
        if axis == "z":
            z ^= k
        elif axis == "x":
            x ^= k
        else:
            core ^= k
        pairs.append((g, gen_index(z, x, core)))
    return lax.ppermute(value, "gen", pairs)


def gather_gen(piece):
    along_z = jnp.stack([piece] + [exchange(piece, "z", k) for k in range(1, 4)])
    along_x = jnp.stack([along_z] + [exchange(along_z, "x", k) for k in range(1, 4)])
    own = along_x.reshape((16,) + piece.shape)
    return own, exchange(own, "core", 1)


def all_to_all(value, axis):
    return lax.all_to_all(value, axis, split_axis=0, concat_axis=0, tiled=True)


def spread(value, axis, count):
    return all_to_all(jnp.broadcast_to(value[None], (count,) + value.shape), axis)


def rotary_tables(lengths):
    half = HEAD_SIZE // 2
    exponent = jnp.arange(half, dtype=f32) * (2.0 / HEAD_SIZE)
    inverse = jnp.power(f32(rope_base), -exponent)
    positions = (jnp.arange(STEPS, dtype=i32)[:, None] + lengths[None, :]).reshape(-1)
    angles = positions.astype(f32)[:, None] * inverse[None, :]
    cosine, sine = jnp.cos(angles), jnp.sin(angles)
    return (
        jnp.concatenate([cosine, cosine], axis=1),
        jnp.concatenate([-sine, sine], axis=1),
    )


def routing(kept, chosen, rank):
    row = jnp.arange(ROWS, dtype=i32)
    named = kept[:, :, None] == jnp.arange(ROWS, dtype=i32)
    match = jnp.any(named, axis=1)
    first = jnp.min(jnp.where(match, row[:, None], ROWS - 1), axis=0)
    last = jnp.max(jnp.where(match, row[:, None], 0), axis=0)
    entry = jnp.arange(KPS, dtype=i32)
    codes = chosen[:, :, None]
    here = (codes // (KPS * BLOCK) == rank) & (codes // BLOCK % KPS == entry)
    offset = jnp.where(here, codes % BLOCK + 1, 0)
    both = jnp.array([1, 256], i32)
    packed = jnp.sum(offset * both[:, None, None], axis=0)
    packed = jnp.sum(jnp.where(named, packed[:, :, None], 0), axis=1)
    rows_of = jnp.stack([first, last], axis=1)
    taken = jnp.where(row[:, None, None] == rows_of[None], packed[:, :, None], 0)
    return rows_of, rows_of + ROWS * jnp.sum(taken, axis=0)


def body(embeddings, cache, lengths, attn_gain, wqkv, wout, final_gain, head, kept, chosen):
    rank = lax.axis_index("tp")
    me = lax.axis_index("gen").astype(i32)
    me_ref = me.reshape(1)
    features = D // TP

    head_part = all_to_all(head.reshape(TP, features, 2 * BLOCK), "tp")
    own_w, other_w = gather_gen(wqkv.T)
    out_whole = lax.all_gather(wout, "gen", axis=0, tiled=True)

    rows_of, packed = routing(kept[0], chosen, rank)
    mine = all_to_all(packed.reshape(GEN, 1, 4), "gen").reshape(GEN, 4)
    routes = spread(mine.reshape(1, GEN * 4), "tp", TP).reshape(TP, GEN // 2, 2, 2, 2)
    row = jnp.bitwise_and(routes, ROWS - 1).transpose(0, 3, 2, 4, 1)
    side = jnp.bitwise_xor(jnp.arange(2, dtype=i32), jnp.bitwise_and(me, 1))
    spot = side[:, None, None] * 128 + row // OWN * 8 + row % OWN
    spot = spot[:, :, :, :, None, :] + jnp.arange(STEPS, dtype=i32)[:, None] * OWN
    spot = spot.reshape(256, GEN // 2)
    sampled = jnp.stack([mine // ROWS % 256, mine // (ROWS * 256)], axis=-1)
    offset = sampled.reshape(GEN, 2, 4).transpose(1, 0, 2).reshape(2, 128)

    x = embeddings.reshape(STEPS, TP, OWN, features).transpose(1, 0, 2, 3).reshape(128, features)
    parts = call(
        project_kernel,
        shape((128, QKV + 128), bf16),
        me_ref,
        x,
        attn_gain.reshape(1, features),
        own_w,
        other_w,
        scalars=1,
    )
    parts = all_to_all(parts.reshape(TP, 8, QKV + 128), "tp")
    cosine, sine = rotary_tables(lengths)
    wide_lengths = jnp.broadcast_to(jnp.tile(lengths, STEPS)[:, None], (8, 128))
    mixed, entries = call(
        attend_kernel,
        (shape((8, QUERY_HEADS * HEAD_SIZE), bf16), shape((8, 1024), bf16)),
        parts,
        cache,
        wide_lengths,
        cosine,
        sine,
    )
    mixed = spread(mixed, "tp", TP).reshape(128, QUERY_HEADS * HEAD_SIZE)
    layer_out = (
        x.astype(f32) + jnp.dot(mixed, out_whole, preferred_element_type=f32)
    ).astype(bf16)
    last_hidden = layer_out.reshape(TP, STEPS, OWN, features)[:, -1].reshape(ROWS, features)

    own_rows, other_rows = gather_gen(layer_out)
    gain = lax.dynamic_slice_in_dim(final_gain, rank * features, features, 0)
    logits = call(
        logits_kernel,
        shape((TP, 272, 128), bf16),
        me_ref,
        own_rows,
        other_rows,
        gain.reshape(1, features),
        spot,
        head_part,
        scalars=1,
        scratch=[pltpu.VMEM((2 * TP, 128, features), f32)],
    )
    logits = all_to_all(logits, "tp")
    stats = call(stats_kernel, shape((8, 128), f32), logits, offset)
    stats = stats.reshape(8, GEN, 4).transpose(1, 0, 2).reshape(GEN, 1, 32)
    stats = all_to_all(stats, "gen").reshape(GEN, 32).T
    row_stats = call(
        rows_kernel, shape((ROWS, 128), f32), stats, rows_of.reshape(GEN, 4).T
    )
    row_stats = all_to_all(row_stats.reshape(TP, OWN, 128)[:, :, :8], "tp")
    peak, mass, picked = (row_stats[:, :, i : 3 * STEPS : 3] for i in range(3))
    best = jnp.max(peak, axis=0)
    mass = jnp.sum(mass * jnp.exp(peak - best), axis=0)
    logprobs = jnp.sum(picked, axis=0) - best - jnp.log(mass)
    return logprobs.T, last_hidden, entries.reshape(STEPS, OWN, 1024)


def solution(mesh):
    return jax.shard_map(
        body,
        mesh=mesh,
        in_specs=(
            P(None, "gen", "tp"),
            P(("gen", "tp"), None, None),
            P(("gen", "tp")),
            P("tp"),
            P("tp", "gen"),
            P("gen", "tp"),
            P(),
            P(None, ("gen", "tp")),
            P("tp", "gen", None),
            P(None, "gen"),
        ),
        out_specs=(P(None, ("gen", "tp")), P("gen", "tp"), P(None, ("gen", "tp"), None)),
        check_vma=False,
    )
```

```python
import jax
import jax.numpy as jnp
from jax import lax
from jax.experimental import pallas as pl
from jax.experimental.pallas import tpu as pltpu
from jax.sharding import PartitionSpec as P

D = 5120
QUERY_HEADS = 20
KEY_VALUE_HEADS = 4
GROUP = QUERY_HEADS // KEY_VALUE_HEADS
HEAD_SIZE = 128
BLOCK = 128
KPS = 2
STEPS = 2
QKV = 3584
GEN = 32
TP = 16
ROWS = 64
OWN = ROWS // TP
PLACES = 128

epsilon = 1e-06
rope_base = 1000000.0

bf16 = jnp.bfloat16
f32 = jnp.float32
i32 = jnp.int32
VMEM_BYTES = 48 * 1024 * 1024


def call(kernel, out_shape, *args, scalars=0, scratch=()):
    specs = [pl.BlockSpec(memory_space=pltpu.SMEM)] * scalars
    specs += [pl.BlockSpec(memory_space=pltpu.VMEM)] * (len(args) - scalars)
    return pl.pallas_call(
        kernel,
        out_shape=out_shape,
        in_specs=specs,
        out_specs=jax.tree.map(lambda _: pl.BlockSpec(memory_space=pltpu.VMEM), out_shape),
        scratch_shapes=list(scratch),
        compiler_params=pltpu.CompilerParams(vmem_limit_bytes=VMEM_BYTES),
    )(*args)


def shape(dims, dtype):
    return jax.ShapeDtypeStruct(dims, dtype)


def nt_dot(a, b):
    return lax.dot_general(a, b, (((1,), (1,)), ((), ())), preferred_element_type=f32)


def swap_halves(value):
    return jnp.concatenate([value[:, 64:], value[:, :64]], axis=1)


def unpack(piece, rows):
    tail = piece[2 * rows :]
    other = swap_halves(tail.astype(f32)).astype(bf16)
    tail = jnp.concatenate([tail, other[: rows - 64]], axis=0)
    return jnp.concatenate([piece[:rows], piece[rows : 2 * rows], tail], axis=1)


def pack_kernel(rank_ref, weights_ref, table_ref, out_ref):
    turned = weights_ref[...].astype(f32).T
    out_ref[0:112, :] = turned[:, 0:128].astype(bf16)
    out_ref[112:224, :] = turned[:, 128:256].astype(bf16)
    block = lax.broadcasted_iota(i32, (ROWS, ROWS), 1)
    row = lax.broadcasted_iota(i32, (ROWS, ROWS), 0)
    named = [table_ref[:, k : k + 1] == block for k in range(KPS)]
    match = jnp.logical_or(named[0], named[1])
    first = jnp.min(jnp.where(match, row, ROWS - 1), axis=0, keepdims=True)
    last = jnp.max(jnp.where(match, row, 0), axis=0, keepdims=True)
    line = lax.broadcasted_iota(i32, (16, ROWS), 0)
    meta = jnp.where(line == 0, first, jnp.where(line == 1, last, 0))
    for s in range(STEPS):
        code = table_ref[:, KPS + s : KPS + s + 1]
        offset = jnp.zeros((ROWS, ROWS), i32)
        for k in range(KPS):
            here = jnp.logical_and(code // BLOCK == rank_ref[0] * KPS + k, named[k])
            offset = jnp.where(here, lax.rem(code, BLOCK) + 1, offset)
        for slot, target in enumerate((first, last)):
            value = jnp.sum(jnp.where(row == target, offset, 0), axis=0, keepdims=True)
            meta = jnp.where(line == 2 + 2 * s + slot, value, meta)
    side = jnp.concatenate([turned[64:112, 256:320], meta.astype(f32)], axis=0)
    out_ref[224:288, :] = jnp.concatenate([turned[0:64, 256:320], side], axis=1).astype(bf16)


def project_kernel(me_ref, x_ref, gain_ref, pieces_ref, out_ref, meta_ref):
    me = me_ref[0]
    wide = x_ref[...].astype(f32)
    scaled = (wide * gain_ref[...].astype(f32)).astype(bf16)
    scaled = jnp.concatenate([scaled, jnp.zeros((128, 64), bf16)], axis=1)
    lane = lax.broadcasted_iota(i32, (16, 128), 1)
    metas = [jnp.zeros((16, 128), f32), jnp.zeros((16, 128), f32)]
    for z in range(4):
        pieces = []
        for g in range(8 * z, 8 * z + 8):
            piece = pieces_ref[g]
            pieces.append(unpack(piece, 112))
            table = piece[272:288].astype(f32)
            for j in range(2):
                mine = jnp.where(lane == 64 + 2 * me + j, table, 0.0)
                column = jnp.sum(mine, axis=1, keepdims=True)
                metas[j] = jnp.where(lane == 32 + g, column, metas[j])
        part = nt_dot(scaled, jnp.concatenate(pieces, axis=0))
        out_ref[:, z * 896 : (z + 1) * 896] = part.astype(bf16)
    for j in range(2):
        meta_ref[16 * j : 16 * j + 16, :] = metas[j]
    squares = jnp.sum(wide * wide, axis=1, keepdims=True)
    high = squares.astype(bf16).astype(f32)
    low = squares - high
    line = lax.rem(lax.broadcasted_iota(i32, (TP * 8, 128), 0), 8)
    lane = lax.broadcasted_iota(i32, (TP * 8, 128), 1)
    extra = jnp.zeros((TP * 8, 128), f32)
    for j in range(2):
        for slot in range(2):
            extra = jnp.where(line == 2 * j + slot, metas[j][slot : slot + 1], extra)
    extra = jnp.where(lane == 0, high, jnp.where(lane == 1, low, extra))
    out_ref[:, QKV:] = extra.astype(bf16)


def output_kernel(me_ref, mixed_ref, own_ref, other_ref, x_ref, rows_ref, packed_ref):
    core = lax.rem(me_ref[0], 2)
    total = x_ref[...].astype(f32)
    for z in range(4):
        pieces = []
        for x in range(4):
            a = own_ref[x * 4 + z]
            b = other_ref[x * 4 + z]
            pieces += [jnp.where(core == 0, a, b), jnp.where(core == 0, b, a)]
        depth = 8 * pieces[0].shape[0]
        total = total + jnp.dot(
            mixed_ref[:, z * depth : (z + 1) * depth],
            jnp.concatenate(pieces, axis=0),
            preferred_element_type=f32,
        )
    rows = total.astype(bf16)
    rows_ref[...] = rows
    packed_ref[0:128, :] = rows[:, 0:128]
    packed_ref[128:256, :] = rows[:, 128:256]
    tail = rows[:, 256:320].astype(f32)
    packed_ref[256:320, :] = jnp.concatenate([tail[0:64], tail[64:128]], axis=1).astype(bf16)


def attend_kernel(parts_ref, cache_ref, lengths_ref, cos_ref, sin_ref, mixed_ref, entry_ref):
    total = parts_ref[0].astype(f32)
    for t in range(1, TP):
        total = total + parts_ref[t].astype(f32)
    squares = total[:, QKV : QKV + 1] + total[:, QKV + 1 : QKV + 2]
    total = total[:, :QKV] * lax.rsqrt(squares / D + epsilon)
    cosine, sine = cos_ref[...], sin_ref[...]

    def head(index):
        return total[:, index * HEAD_SIZE : (index + 1) * HEAD_SIZE]

    def rotated(index):
        vec = head(index)
        swapped = jnp.concatenate([vec[:, HEAD_SIZE // 2 :], vec[:, : HEAD_SIZE // 2]], axis=1)
        return vec * cosine + swapped * sine

    rows = 8 * GROUP
    row = lax.rem(lax.broadcasted_iota(i32, (8, OWN * PLACES), 0), OWN)
    lane = lax.broadcasted_iota(i32, (8, OWN * PLACES), 1)
    old_ok = jnp.logical_and(lane // PLACES == row, lax.rem(lane, PLACES) < lengths_ref[:, :1])
    old_bias = jnp.tile(jnp.where(old_ok, 0.0, -jnp.inf), (GROUP, 1))
    slot = lax.broadcasted_iota(i32, (8, 8), 1)
    fresh = lax.broadcasted_iota(i32, (8, 8), 0)
    new_ok = jnp.logical_and(lax.rem(slot, OWN) == lax.rem(fresh, OWN), slot // OWN <= fresh // OWN)
    new_bias = jnp.tile(jnp.where(new_ok, 0.0, -jnp.inf), (GROUP, 1))
    scale = HEAD_SIZE ** (-0.5)
    width = KEY_VALUE_HEADS * HEAD_SIZE
    for k in range(KEY_VALUE_HEADS):
        at = k * HEAD_SIZE
        new_k = rotated(QUERY_HEADS + k).astype(bf16)
        new_v = head(QUERY_HEADS + KEY_VALUE_HEADS + k).astype(bf16)
        entry_ref[:, at : at + HEAD_SIZE] = new_k
        entry_ref[:, width + at : width + at + HEAD_SIZE] = new_v
        query = jnp.concatenate([rotated(k * GROUP + h) for h in range(GROUP)], axis=0).astype(bf16)
        old_k = cache_ref[:, :, at : at + HEAD_SIZE].reshape(OWN * PLACES, HEAD_SIZE)
        old_v = cache_ref[:, :, width + at : width + at + HEAD_SIZE].reshape(OWN * PLACES, HEAD_SIZE)
        old_s = nt_dot(query, old_k) * scale + old_bias
        new_s = nt_dot(query, new_k) * scale + new_bias
        peak = jnp.maximum(
            jnp.max(old_s, axis=1, keepdims=True), jnp.max(new_s, axis=1, keepdims=True)
        )
        old_e, new_e = jnp.exp(old_s - peak), jnp.exp(new_s - peak)
        whole = jnp.sum(old_e, axis=1, keepdims=True) + jnp.sum(new_e, axis=1, keepdims=True)
        old_w, new_w = (old_e / whole).astype(bf16), (new_e / whole).astype(bf16)
        mixed = jnp.dot(old_w, old_v, preferred_element_type=f32)
        mixed = mixed + jnp.dot(new_w, new_v, preferred_element_type=f32)
        for h in range(GROUP):
            to = (k * GROUP + h) * HEAD_SIZE
            mixed_ref[:, to : to + HEAD_SIZE] = mixed[8 * h : 8 * h + 8].astype(bf16)


def logits_kernel(own_ref, other_ref, gain_ref, spot_ref, head_ref, out_ref, pairs_ref):
    lane = lax.broadcasted_iota(i32, (256, 256), 1)
    features = gain_ref.shape[1]
    for pair in range(GEN // 2):
        place = pair % 4 * 4 + pair // 4
        rows = [unpack(ref[place], 128) for ref in (own_ref, other_ref)]
        pick = (spot_ref[:, pair : pair + 1] == lane).astype(f32).astype(bf16)
        taken = jnp.dot(pick, jnp.concatenate(rows, axis=0), preferred_element_type=f32)
        for b in range(2 * TP):
            pairs_ref[b, 8 * pair : 8 * pair + 8, :] = taken[8 * b : 8 * b + 8, :features]
    gain = gain_ref[...].astype(f32)
    column = lax.broadcasted_iota(i32, (128, 128), 1)
    squares = jnp.zeros((128, 128), f32)
    for t in range(TP):
        for j in range(2):
            raw = pairs_ref[2 * t + j]
            squares = jnp.where(
                column == 2 * t + j, jnp.sum(raw * raw, axis=1, keepdims=True), squares
            )
            part = jnp.dot(
                (raw * gain).astype(bf16),
                head_ref[t, :, j * BLOCK : (j + 1) * BLOCK],
                preferred_element_type=f32,
            )
            out_ref[t, j * 128 : (j + 1) * 128, :] = part.astype(bf16)
    squares = squares.T
    high = squares.astype(bf16).astype(f32)
    low = squares - high
    line = lax.broadcasted_iota(i32, (16, 128), 0)
    for t in range(TP):
        extra = jnp.zeros((16, 128), f32)
        for j in range(2):
            b = 2 * t + j
            extra = jnp.where(line == 2 * j, high[b : b + 1], extra)
            extra = jnp.where(line == 2 * j + 1, low[b : b + 1], extra)
        out_ref[t, 256:272, :] = extra.astype(bf16)


def stats_kernel(parts_ref, offset_ref, out_ref):
    total = parts_ref[0].astype(f32)
    for t in range(1, TP):
        total = total + parts_ref[t].astype(f32)
    token = lax.broadcasted_iota(i32, (BLOCK, 128), 0)
    line = lax.broadcasted_iota(i32, (8, 128), 0)
    out = jnp.zeros((8, 128), f32)
    for j in range(2):
        squares = total[256 + 2 * j : 257 + 2 * j] + total[257 + 2 * j : 258 + 2 * j]
        logits = total[j * 128 : (j + 1) * 128].T * lax.rsqrt(squares / D + epsilon)
        peak = jnp.max(logits, axis=0, keepdims=True)
        mass = jnp.sum(jnp.exp(logits - peak), axis=0, keepdims=True)
        hit = jnp.where(token == offset_ref[j : j + 1] - 1, logits, 0.0)
        picked = jnp.sum(hit, axis=0, keepdims=True)
        for at, value in enumerate((peak, mass, picked)):
            out = jnp.where(line == 3 * j + at, value, out)
    out_ref[...] = out


def rows_kernel(stats_ref, row_ref, out_ref):
    mine = lax.broadcasted_iota(i32, (ROWS, GEN), 0)
    lane = lax.broadcasted_iota(i32, (ROWS, 128), 1)
    out = jnp.zeros((ROWS, 128), f32)
    for s in range(STEPS):
        best = jnp.full((ROWS, 1), -jnp.inf, f32)
        combos = [(j, slot) for j in range(2) for slot in range(2)]
        masks = [row_ref[2 * j + slot : 2 * j + slot + 1, :] == mine for j, slot in combos]

        def stat(which, j, slot):
            at = (3 * j + which) * 4 + slot * 2 + s
            return stats_ref[at : at + 1, :]

        for mask, (j, slot) in zip(masks, combos):
            peak = jnp.where(mask, stat(0, j, slot), -jnp.inf)
            best = jnp.maximum(best, jnp.max(peak, axis=1, keepdims=True))
        mass = jnp.zeros((ROWS, 1), f32)
        picked = jnp.zeros((ROWS, 1), f32)
        for mask, (j, slot) in zip(masks, combos):
            grown = stat(1, j, slot) * jnp.exp(jnp.where(mask, stat(0, j, slot), best) - best)
            mass = mass + jnp.sum(jnp.where(mask, grown, 0.0), axis=1, keepdims=True)
            picked = picked + jnp.sum(
                jnp.where(mask, stat(2, j, slot), 0.0), axis=1, keepdims=True
            )
        for at, value in enumerate((best, mass, picked)):
            out = jnp.where(lane == 3 * s + at, value, out)
    out_ref[...] = out


def gen_index(z, x, core):
    return (z * 4 + x) * 2 + core


Z_GROUPS = [[gen_index(z, x, c) for z in range(4)] for x in range(4) for c in range(2)]
X_GROUPS = [[gen_index(z, x, c) for x in range(4)] for z in range(4) for c in range(2)]


def gather_gen(piece):
    along_z = spread(piece, "gen", 4, Z_GROUPS)
    along_x = spread(along_z, "gen", 4, X_GROUPS)
    own = along_x.reshape((16,) + piece.shape)
    return own, lax.ppermute(own, "gen", [(g, g ^ 1) for g in range(GEN)])


def all_to_all(value, axis, groups=None):
    return lax.all_to_all(
        value, axis, split_axis=0, concat_axis=0, tiled=True, axis_index_groups=groups
    )


def spread(value, axis, count, groups=None):
    return all_to_all(jnp.broadcast_to(value[None], (count,) + value.shape), axis, groups)


def rotary_tables(lengths):
    half = HEAD_SIZE // 2
    exponent = jnp.arange(half, dtype=f32) * (2.0 / HEAD_SIZE)
    inverse = jnp.power(f32(rope_base), -exponent)
    positions = (jnp.arange(STEPS, dtype=i32)[:, None] + lengths[None, :]).reshape(-1)
    angles = positions.astype(f32)[:, None] * inverse[None, :]
    cosine, sine = jnp.cos(angles), jnp.sin(angles)
    return (
        jnp.concatenate([cosine, cosine], axis=1),
        jnp.concatenate([-sine, sine], axis=1),
    )


def row_table(kept):
    row = jnp.arange(ROWS, dtype=i32)[:, None]
    match = jnp.any(kept[:, :, None] == jnp.arange(ROWS, dtype=i32), axis=1)
    first = jnp.min(jnp.where(match, row, ROWS - 1), axis=0)
    last = jnp.max(jnp.where(match, row, 0), axis=0)
    return jnp.stack([first, last], axis=1)


def body(embeddings, cache, lengths, attn_gain, wqkv, wout, final_gain, head, kept, chosen):
    rank = lax.axis_index("tp").astype(i32)
    me = lax.axis_index("gen").astype(i32)
    features = D // TP

    table = jnp.concatenate([kept[0], chosen.T], axis=1)
    piece = call(
        pack_kernel, shape((288, 128), bf16), rank.reshape(1), wqkv, table, scalars=1
    )
    pieces = lax.all_gather(piece, "gen")
    head_part = all_to_all(head.reshape(TP, features, 2 * BLOCK), "tp")
    wout, head_part = lax.optimization_barrier((wout, head_part))
    own_out, other_out = gather_gen(wout)

    x = embeddings.reshape(STEPS, TP, OWN, features).transpose(1, 0, 2, 3).reshape(128, features)
    parts, meta = call(
        project_kernel,
        (shape((128, QKV + 128), bf16), shape((32, 128), f32)),
        me.reshape(1),
        x,
        attn_gain.reshape(1, features),
        pieces,
        scalars=1,
    )
    parts, own_out, other_out = lax.optimization_barrier((parts, own_out, other_out))
    parts = all_to_all(parts.reshape(TP, 8, QKV + 128), "tp")

    meta = meta.reshape(2, 16, 128)[:, :6, 32:64].astype(i32).reshape(2, 3, 2, GEN)
    offset = meta[:, 1:].transpose(0, 3, 2, 1).reshape(2, 128)
    routes = parts[:, :4, QKV + 32 : QKV + 64].astype(f32).astype(i32)
    row = routes.reshape(TP, 2, 2, GEN // 2, 2).transpose(0, 1, 4, 2, 3)
    side = jnp.bitwise_xor(jnp.arange(2, dtype=i32), jnp.bitwise_and(me, 1))
    spot = side[:, None, None] * 128 + row // OWN * 8 + row % OWN
    spot = spot[:, :, :, :, None, :] + jnp.arange(STEPS, dtype=i32)[:, None] * OWN
    spot = spot.reshape(256, GEN // 2)

    cosine, sine = rotary_tables(lengths)
    wide_lengths = jnp.broadcast_to(jnp.tile(lengths, STEPS)[:, None], (8, 128))
    mixed, entries = call(
        attend_kernel,
        (shape((8, QUERY_HEADS * HEAD_SIZE), bf16), shape((8, 1024), bf16)),
        parts,
        cache,
        wide_lengths,
        cosine,
        sine,
    )
    mixed = spread(mixed, "tp", TP).reshape(128, QUERY_HEADS * HEAD_SIZE)
    layer_out, packed = call(
        output_kernel,
        (shape((128, features), bf16), shape((320, 128), bf16)),
        me.reshape(1),
        mixed,
        own_out,
        other_out,
        x,
        scalars=1,
    )
    last_hidden = layer_out.reshape(TP, STEPS, OWN, features)[:, -1].reshape(ROWS, features)

    own_rows, other_rows = gather_gen(packed)
    gain = lax.dynamic_slice_in_dim(final_gain, rank * features, features, 0)
    logits = call(
        logits_kernel,
        shape((TP, 272, 128), bf16),
        own_rows,
        other_rows,
        gain.reshape(1, features),
        spot,
        head_part,
        scratch=[pltpu.VMEM((2 * TP, 128, features), f32)],
    )
    logits = all_to_all(logits, "tp")
    stats = call(stats_kernel, shape((8, 128), f32), logits, offset)
    stats = stats.reshape(8, GEN, 4).transpose(1, 0, 2).reshape(GEN, 1, 32)
    stats = all_to_all(stats, "gen").reshape(GEN, 32).T
    rows_of = row_table(kept[0]).reshape(GEN, 4).T
    row_stats = call(rows_kernel, shape((ROWS, 128), f32), stats, rows_of)
    row_stats = all_to_all(row_stats.reshape(TP, OWN, 128)[:, :, :8], "tp")
    peak, mass, picked = (row_stats[:, :, i : 3 * STEPS : 3] for i in range(3))
    best = jnp.max(peak, axis=0)
    mass = jnp.sum(mass * jnp.exp(peak - best), axis=0)
    logprobs = jnp.sum(picked, axis=0) - best - jnp.log(mass)
    return logprobs.T, last_hidden, entries.reshape(STEPS, OWN, 1024)


def solution(mesh):
    return jax.shard_map(
        body,
        mesh=mesh,
        in_specs=(
            P(None, "gen", "tp"),
            P(("gen", "tp"), None, None),
            P(("gen", "tp")),
            P("tp"),
            P("tp", "gen"),
            P("gen", "tp"),
            P(),
            P(None, ("gen", "tp")),
            P("tp", "gen", None),
            P(None, "gen"),
        ),
        out_specs=(P(None, ("gen", "tp")), P("gen", "tp"), P(None, ("gen", "tp"), None)),
        check_vma=False,
    )
```

```python
import jax
import jax.numpy as jnp
from jax import lax
from jax.experimental import pallas as pl
from jax.experimental.pallas import tpu as pltpu
from jax.sharding import PartitionSpec as P

D = 5120
QUERY_HEADS = 20
KEY_VALUE_HEADS = 4
GROUP = QUERY_HEADS // KEY_VALUE_HEADS
HEAD_SIZE = 128
BLOCK = 128
KPS = 2
STEPS = 2
QKV = 3584
GEN = 32
TP = 16
ROWS = 64
OWN = ROWS // TP
PLACES = 128

epsilon = 1e-06
rope_base = 1000000.0

bf16 = jnp.bfloat16
f32 = jnp.float32
i32 = jnp.int32
VMEM_BYTES = 48 * 1024 * 1024


def call(kernel, out_shape, *args, scalars=0, scratch=()):
    specs = [pl.BlockSpec(memory_space=pltpu.SMEM)] * scalars
    specs += [pl.BlockSpec(memory_space=pltpu.VMEM)] * (len(args) - scalars)
    return pl.pallas_call(
        kernel,
        out_shape=out_shape,
        in_specs=specs,
        out_specs=jax.tree.map(lambda _: pl.BlockSpec(memory_space=pltpu.VMEM), out_shape),
        scratch_shapes=list(scratch),
        compiler_params=pltpu.CompilerParams(vmem_limit_bytes=VMEM_BYTES),
    )(*args)


def shape(dims, dtype):
    return jax.ShapeDtypeStruct(dims, dtype)


def nt_dot(a, b):
    return lax.dot_general(a, b, (((1,), (1,)), ((), ())), preferred_element_type=f32)


def swap_halves(value):
    return jnp.concatenate([value[:, 64:], value[:, :64]], axis=1)


def unpack(piece, rows):
    tail = piece[2 * rows :]
    other = swap_halves(tail.astype(f32)).astype(bf16)
    tail = jnp.concatenate([tail, other[: rows - 64]], axis=0)
    return jnp.concatenate([piece[:rows], piece[rows : 2 * rows], tail], axis=1)


def pack_kernel(rank_ref, weights_ref, table_ref, out_ref):
    turned = weights_ref[...].astype(f32).T
    out_ref[0:112, :] = turned[:, 0:128].astype(bf16)
    out_ref[112:224, :] = turned[:, 128:256].astype(bf16)
    block = lax.broadcasted_iota(i32, (ROWS, ROWS), 1)
    row = lax.broadcasted_iota(i32, (ROWS, ROWS), 0)
    named = [table_ref[:, k : k + 1] == block for k in range(KPS)]
    match = jnp.logical_or(named[0], named[1])
    first = jnp.min(jnp.where(match, row, ROWS - 1), axis=0, keepdims=True)
    last = jnp.max(jnp.where(match, row, 0), axis=0, keepdims=True)
    line = lax.broadcasted_iota(i32, (16, ROWS), 0)
    meta = jnp.where(line == 0, first, jnp.where(line == 1, last, 0))
    for s in range(STEPS):
        code = table_ref[:, KPS + s : KPS + s + 1]
        offset = jnp.zeros((ROWS, ROWS), i32)
        for k in range(KPS):
            here = jnp.logical_and(code // BLOCK == rank_ref[0] * KPS + k, named[k])
            offset = jnp.where(here, lax.rem(code, BLOCK) + 1, offset)
        for slot, target in enumerate((first, last)):
            value = jnp.sum(jnp.where(row == target, offset, 0), axis=0, keepdims=True)
            meta = jnp.where(line == 2 + 2 * s + slot, value, meta)
    side = jnp.concatenate([turned[64:112, 256:320], meta.astype(f32)], axis=0)
    out_ref[224:288, :] = jnp.concatenate([turned[0:64, 256:320], side], axis=1).astype(bf16)


def project_kernel(me_ref, x_ref, gain_ref, own_ref, other_ref, out_ref, meta_ref):
    me = me_ref[0]
    core = lax.rem(me, 2)
    wide = x_ref[...].astype(f32)
    scaled = (wide * gain_ref[...].astype(f32)).astype(bf16)
    scaled = jnp.concatenate([scaled, jnp.zeros((128, 64), bf16)], axis=1)
    lane = lax.broadcasted_iota(i32, (16, 128), 1)
    metas = [jnp.zeros((16, 128), f32), jnp.zeros((16, 128), f32)]
    line = lax.rem(lax.broadcasted_iota(i32, (TP * 8, 128), 0), 8)
    extra = jnp.zeros((TP * 8, 128), f32)
    for z in range(4):
        pieces = []
        for x in range(4):
            a = own_ref[x * 4 + z]
            b = other_ref[x * 4 + z]
            for c, piece in enumerate((jnp.where(core == 0, a, b), jnp.where(core == 0, b, a))):
                pieces.append(unpack(piece, 112))
                table = piece[272:288].astype(f32)
                for j in range(2):
                    mine = jnp.where(lane == 64 + 2 * me + j, table, 0.0)
                    column = jnp.sum(mine, axis=1, keepdims=True)
                    at = 32 + gen_index(z, x, c)
                    metas[j] = jnp.where(lane == at, column, metas[j])
        table = own_ref[lax.rem(me // 2, 4) * 4 + z][272:288].astype(f32)
        for slot in range(2):
            extra = jnp.where(line == 2 * z + slot, table[slot : slot + 1], extra)
        part = nt_dot(scaled, jnp.concatenate(pieces, axis=0))
        out_ref[:, z * 896 : (z + 1) * 896] = part.astype(bf16)
    for j in range(2):
        meta_ref[16 * j : 16 * j + 16, :] = metas[j]
    squares = jnp.sum(wide * wide, axis=1, keepdims=True)
    high = squares.astype(bf16).astype(f32)
    low = squares - high
    lane = lax.broadcasted_iota(i32, (TP * 8, 128), 1)
    extra = jnp.where(lane < 64, 0.0, extra)
    extra = jnp.where(lane == 0, high, jnp.where(lane == 1, low, extra))
    out_ref[:, QKV:] = extra.astype(bf16)


def output_kernel(mixed_ref, weights_ref, x_ref, rows_ref, packed_ref):
    part = jnp.dot(mixed_ref[...], weights_ref[...], preferred_element_type=f32)
    rows = (x_ref[...].astype(f32) + part).astype(bf16)
    rows_ref[...] = rows
    packed_ref[0:128, :] = rows[:, 0:128]
    packed_ref[128:256, :] = rows[:, 128:256]
    tail = rows[:, 256:320].astype(f32)
    packed_ref[256:320, :] = jnp.concatenate([tail[0:64], tail[64:128]], axis=1).astype(bf16)


def attend_kernel(parts_ref, cache_ref, lengths_ref, cos_ref, sin_ref, mixed_ref, entry_ref):
    total = parts_ref[0].astype(f32)
    for t in range(1, TP):
        total = total + parts_ref[t].astype(f32)
    squares = total[:, QKV : QKV + 1] + total[:, QKV + 1 : QKV + 2]
    total = total[:, :QKV] * lax.rsqrt(squares / D + epsilon)
    cosine, sine = cos_ref[...], sin_ref[...]

    def head(index):
        return total[:, index * HEAD_SIZE : (index + 1) * HEAD_SIZE]

    def rotated(index):
        vec = head(index)
        swapped = jnp.concatenate([vec[:, HEAD_SIZE // 2 :], vec[:, : HEAD_SIZE // 2]], axis=1)
        return vec * cosine + swapped * sine

    rows = 8 * GROUP
    row = lax.rem(lax.broadcasted_iota(i32, (8, OWN * PLACES), 0), OWN)
    lane = lax.broadcasted_iota(i32, (8, OWN * PLACES), 1)
    old_ok = jnp.logical_and(lane // PLACES == row, lax.rem(lane, PLACES) < lengths_ref[:, :1])
    old_bias = jnp.tile(jnp.where(old_ok, 0.0, -jnp.inf), (GROUP, 1))
    slot = lax.broadcasted_iota(i32, (8, 8), 1)
    fresh = lax.broadcasted_iota(i32, (8, 8), 0)
    new_ok = jnp.logical_and(lax.rem(slot, OWN) == lax.rem(fresh, OWN), slot // OWN <= fresh // OWN)
    new_bias = jnp.tile(jnp.where(new_ok, 0.0, -jnp.inf), (GROUP, 1))
    scale = HEAD_SIZE ** (-0.5)
    width = KEY_VALUE_HEADS * HEAD_SIZE
    for k in range(KEY_VALUE_HEADS):
        at = k * HEAD_SIZE
        new_k = rotated(QUERY_HEADS + k).astype(bf16)
        new_v = head(QUERY_HEADS + KEY_VALUE_HEADS + k).astype(bf16)
        entry_ref[:, at : at + HEAD_SIZE] = new_k
        entry_ref[:, width + at : width + at + HEAD_SIZE] = new_v
        query = jnp.concatenate([rotated(k * GROUP + h) for h in range(GROUP)], axis=0).astype(bf16)
        old_k = cache_ref[:, :, at : at + HEAD_SIZE].reshape(OWN * PLACES, HEAD_SIZE)
        old_v = cache_ref[:, :, width + at : width + at + HEAD_SIZE].reshape(OWN * PLACES, HEAD_SIZE)
        old_s = nt_dot(query, old_k) * scale + old_bias
        new_s = nt_dot(query, new_k) * scale + new_bias
        peak = jnp.maximum(
            jnp.max(old_s, axis=1, keepdims=True), jnp.max(new_s, axis=1, keepdims=True)
        )
        old_e, new_e = jnp.exp(old_s - peak), jnp.exp(new_s - peak)
        whole = jnp.sum(old_e, axis=1, keepdims=True) + jnp.sum(new_e, axis=1, keepdims=True)
        old_w, new_w = (old_e / whole).astype(bf16), (new_e / whole).astype(bf16)
        mixed = jnp.dot(old_w, old_v, preferred_element_type=f32)
        mixed = mixed + jnp.dot(new_w, new_v, preferred_element_type=f32)
        for h in range(GROUP):
            to = (k * GROUP + h) * HEAD_SIZE
            mixed_ref[:, to : to + HEAD_SIZE] = mixed[8 * h : 8 * h + 8].astype(bf16)


def select_kernel(layer_ref, spot_ref, out_ref):
    owners = out_ref.shape[0]
    lane = lax.broadcasted_iota(i32, (16 * owners, 256), 1)
    low = lax.broadcasted_iota(i32, (256, 128), 1) < 64
    tails = jnp.zeros((16 * owners, 128), f32)
    for half in range(2):
        pieces = [layer_ref[2 * half], layer_ref[2 * half + 1]]
        sides = [jnp.concatenate([p[256:], swap_halves(p[256:].astype(f32)).astype(bf16)], axis=0) for p in pieces]
        tail = jnp.concatenate(sides, axis=0).astype(f32)
        if half:
            tail = swap_halves(tail)
        tail = jnp.where(low if half == 0 else jnp.logical_not(low), tail, 0.0).astype(bf16)
        pick = (spot_ref[:, half : half + 1] == lane).astype(f32).astype(bf16)
        for part in range(2):
            rows = jnp.concatenate([p[128 * part : 128 * part + 128] for p in pieces], axis=0)
            taken = jnp.dot(pick, rows, preferred_element_type=f32).astype(bf16)
            at = 32 * part + 16 * half
            out_ref[:, at : at + 16, :] = taken.reshape(owners, 16, 128)
        tails = tails + jnp.dot(pick, tail, preferred_element_type=f32)
    out_ref[:, 64:80, :] = tails.astype(bf16).reshape(owners, 16, 128)


def logits_kernel(rows_ref, gain_ref, head_ref, offset_ref, out_ref):
    def piece(t):
        tail = rows_ref[:, t, 64:80, :].reshape(128, 128).astype(f32)
        tail = [tail.reshape(8, 16, 128), swap_halves(tail).reshape(8, 16, 128)]
        parts = [rows_ref[:, t, 0:32, :].reshape(256, 128), rows_ref[:, t, 32:64, :].reshape(256, 128)]
        wide = [p.astype(f32) for p in parts]
        return wide + [jnp.concatenate(tail, axis=1).reshape(256, 128)[:, :64]]

    squares = jnp.zeros((256, 128), f32)
    tails = jnp.zeros((256, 64), f32)
    for t in range(TP):
        a, b, c = piece(t)
        squares = squares + (a * a + b * b)
        tails = tails + c * c
    total = jnp.sum(squares, axis=1, keepdims=True) + jnp.sum(tails, axis=1, keepdims=True)
    factor = lax.rsqrt(total / D + epsilon)
    logits = jnp.zeros((256, 2 * BLOCK), f32)
    for t in range(TP):
        at = t * 320
        for value, width in zip(piece(t), (128, 128, 64)):
            normed = (value * factor * gain_ref[:, at : at + width].astype(f32)).astype(bf16)
            weights = head_ref[at : at + width, :]
            logits = logits + jnp.dot(normed, weights, preferred_element_type=f32)
            at += width
    pair = lax.broadcasted_iota(i32, (256, BLOCK), 0)
    logits = jnp.where(lax.rem(pair // 4, 2) == 0, logits[:, :BLOCK], logits[:, BLOCK:])
    token = lax.broadcasted_iota(i32, (BLOCK, 128), 0)
    line = lax.broadcasted_iota(i32, (8, 128), 0)
    for half in range(2):
        side = logits[128 * half : 128 * half + 128].T
        peak = jnp.max(side, axis=0, keepdims=True)
        mass = jnp.sum(jnp.exp(side - peak), axis=0, keepdims=True)
        target = offset_ref[:, 128 * half : 128 * half + 128] - 1
        picked = jnp.sum(jnp.where(token == target, side, 0.0), axis=0, keepdims=True)
        out = jnp.where(line == 0, peak, jnp.where(line == 1, mass, picked))
        out_ref[:, 128 * half : 128 * half + 128] = out


def rows_kernel(stats_ref, row_ref, out_ref):
    mine = lax.broadcasted_iota(i32, (ROWS, GEN), 0)
    lane = lax.broadcasted_iota(i32, (ROWS, 128), 1)
    out = jnp.zeros((ROWS, 128), f32)
    for s in range(STEPS):
        best = jnp.full((ROWS, 1), -jnp.inf, f32)
        combos = [(j, slot) for j in range(2) for slot in range(2)]
        masks = [row_ref[2 * j + slot : 2 * j + slot + 1, :] == mine for j, slot in combos]

        def stat(which, j, slot):
            at = which * 8 + j * 4 + slot * 2 + s
            return stats_ref[at : at + 1, :]

        for mask, (j, slot) in zip(masks, combos):
            peak = jnp.where(mask, stat(0, j, slot), -jnp.inf)
            best = jnp.maximum(best, jnp.max(peak, axis=1, keepdims=True))
        mass = jnp.zeros((ROWS, 1), f32)
        picked = jnp.zeros((ROWS, 1), f32)
        for mask, (j, slot) in zip(masks, combos):
            grown = stat(1, j, slot) * jnp.exp(jnp.where(mask, stat(0, j, slot), best) - best)
            mass = mass + jnp.sum(jnp.where(mask, grown, 0.0), axis=1, keepdims=True)
            picked = picked + jnp.sum(
                jnp.where(mask, stat(2, j, slot), 0.0), axis=1, keepdims=True
            )
        for at, value in enumerate((best, mass, picked)):
            out = jnp.where(lane == 3 * s + at, value, out)
    out_ref[...] = out


def gen_index(z, x, core):
    return (z * 4 + x) * 2 + core


Z_GROUPS = [[gen_index(z, x, c) for z in range(4)] for x in range(4) for c in range(2)]
X_GROUPS = [[gen_index(z, x, c) for x in range(4)] for z in range(4) for c in range(2)]


LAYERS = [[z * 128 + i for i in range(128)] for z in range(4)]


def gather_gen(piece):
    along_z = spread(piece, "gen", 4, Z_GROUPS)
    along_x = spread(along_z, "gen", 4, X_GROUPS)
    own = along_x.reshape((16,) + piece.shape)
    return own, lax.ppermute(own, "gen", [(g, g ^ 1) for g in range(GEN)])


def all_to_all(value, axis, groups=None):
    return lax.all_to_all(
        value, axis, split_axis=0, concat_axis=0, tiled=True, axis_index_groups=groups
    )


def spread(value, axis, count, groups=None):
    return all_to_all(jnp.broadcast_to(value[None], (count,) + value.shape), axis, groups)


def rotary_tables(lengths):
    half = HEAD_SIZE // 2
    exponent = jnp.arange(half, dtype=f32) * (2.0 / HEAD_SIZE)
    inverse = jnp.power(f32(rope_base), -exponent)
    positions = (jnp.arange(STEPS, dtype=i32)[:, None] + lengths[None, :]).reshape(-1)
    angles = positions.astype(f32)[:, None] * inverse[None, :]
    cosine, sine = jnp.cos(angles), jnp.sin(angles)
    return (
        jnp.concatenate([cosine, cosine], axis=1),
        jnp.concatenate([-sine, sine], axis=1),
    )


def row_table(kept):
    row = jnp.arange(ROWS, dtype=i32)[:, None]
    match = jnp.any(kept[:, :, None] == jnp.arange(ROWS, dtype=i32), axis=1)
    first = jnp.min(jnp.where(match, row, ROWS - 1), axis=0)
    last = jnp.max(jnp.where(match, row, 0), axis=0)
    return jnp.stack([first, last], axis=1)


def body(embeddings, cache, lengths, attn_gain, wqkv, wout, final_gain, head, kept, chosen):
    rank = lax.axis_index("tp").astype(i32)
    me = lax.axis_index("gen").astype(i32)
    features = D // TP

    out_whole = lax.all_gather(wout, "gen", axis=0, tiled=True)
    table = jnp.concatenate([kept[0], chosen.T], axis=1)
    piece = call(
        pack_kernel, shape((288, 128), bf16), rank.reshape(1), wqkv, table, scalars=1
    )
    own_w, other_w = gather_gen(piece)

    x = embeddings.reshape(STEPS, TP, OWN, features).transpose(1, 0, 2, 3).reshape(128, features)
    parts, meta = call(
        project_kernel,
        (shape((128, QKV + 128), bf16), shape((32, 128), f32)),
        me.reshape(1),
        x,
        attn_gain.reshape(1, features),
        own_w,
        other_w,
        scalars=1,
    )
    parts = all_to_all(parts.reshape(TP, 8, QKV + 128), "tp")

    meta = meta.reshape(2, 16, 128)[:, :6, 32:64].astype(i32).reshape(2, 3, 2, GEN)
    offset = meta[:, 1:].reshape(2, 2, 2, 4, 8).transpose(4, 3, 0, 2, 1).reshape(1, 256)
    routes = lax.dynamic_slice_in_dim(parts[:, :, QKV + 64 :], me // 8 * 16, 16, 2)
    row = routes.astype(f32).astype(i32).reshape(TP, 2, 2, 2, 8, 2).transpose(4, 0, 2, 5, 3, 1)
    spot = jnp.arange(2, dtype=i32)[:, None, None, None] * 128 + row // OWN * 8 + row % OWN
    spot = spot[:, :, :, :, :, None, :] + jnp.arange(STEPS, dtype=i32)[:, None] * OWN
    spot = spot.reshape(16 * 128, 2)

    cosine, sine = rotary_tables(lengths)
    wide_lengths = jnp.broadcast_to(jnp.tile(lengths, STEPS)[:, None], (8, 128))
    mixed, entries = call(
        attend_kernel,
        (shape((8, QUERY_HEADS * HEAD_SIZE), bf16), shape((8, 1024), bf16)),
        parts,
        cache,
        wide_lengths,
        cosine,
        sine,
    )
    mixed = spread(mixed, "tp", TP).reshape(128, QUERY_HEADS * HEAD_SIZE)
    layer_out, packed = call(
        output_kernel,
        (shape((128, features), bf16), shape((320, 128), bf16)),
        mixed,
        out_whole,
        x,
    )
    last_hidden = layer_out.reshape(TP, STEPS, OWN, features)[:, -1].reshape(ROWS, features)

    layers = spread(packed, "gen", 4, Z_GROUPS)
    taken = call(select_kernel, shape((128, 80, 128), bf16), layers, spot)
    taken = all_to_all(taken, ("gen", "tp"), LAYERS).reshape(8, TP, 80, 128)
    stats = call(
        logits_kernel,
        shape((8, 256), f32),
        taken,
        final_gain.reshape(1, D),
        head,
        offset,
    )
    stats = stats[:3].reshape(3, 8, 4, 8).transpose(2, 1, 0, 3).reshape(GEN, 1, 24)
    stats = all_to_all(stats, "gen").reshape(GEN, 24).T
    rows_of = row_table(kept[0]).reshape(GEN, 4).T
    row_stats = call(rows_kernel, shape((ROWS, 128), f32), stats, rows_of)
    row_stats = all_to_all(row_stats.reshape(TP, OWN, 128)[:, :, :8], "tp")
    peak, mass, picked = (row_stats[:, :, i : 3 * STEPS : 3] for i in range(3))
    best = jnp.max(peak, axis=0)
    mass = jnp.sum(mass * jnp.exp(peak - best), axis=0)
    logprobs = jnp.sum(picked, axis=0) - best - jnp.log(mass)
    return logprobs.T, last_hidden, entries.reshape(STEPS, OWN, 1024)


def solution(mesh):
    return jax.shard_map(
        body,
        mesh=mesh,
        in_specs=(
            P(None, "gen", "tp"),
            P(("gen", "tp"), None, None),
            P(("gen", "tp")),
            P("tp"),
            P("tp", "gen"),
            P("gen", "tp"),
            P(),
            P(None, ("gen", "tp")),
            P("tp", "gen", None),
            P(None, "gen"),
        ),
        out_specs=(P(None, ("gen", "tp")), P("gen", "tp"), P(None, ("gen", "tp"), None)),
        check_vma=False,
    )
```

```python
import jax
import jax.numpy as jnp
from jax import lax
from jax.experimental import pallas as pl
from jax.experimental.pallas import tpu as pltpu
from jax.sharding import PartitionSpec as P

D = 5120
QUERY_HEADS = 20
KEY_VALUE_HEADS = 4
GROUP = QUERY_HEADS // KEY_VALUE_HEADS
HEAD_SIZE = 128
BLOCK = 128
KPS = 2
STEPS = 2
QKV = 3584
GEN = 32
TP = 16
ROWS = 64
OWN = ROWS // TP
PLACES = 128

epsilon = 1e-06
rope_base = 1000000.0

bf16 = jnp.bfloat16
f32 = jnp.float32
i32 = jnp.int32
VMEM_BYTES = 48 * 1024 * 1024


def call(kernel, out_shape, *args, scalars=0, scratch=()):
    specs = [pl.BlockSpec(memory_space=pltpu.SMEM)] * scalars
    specs += [pl.BlockSpec(memory_space=pltpu.VMEM)] * (len(args) - scalars)
    return pl.pallas_call(
        kernel,
        out_shape=out_shape,
        in_specs=specs,
        out_specs=jax.tree.map(lambda _: pl.BlockSpec(memory_space=pltpu.VMEM), out_shape),
        scratch_shapes=list(scratch),
        compiler_params=pltpu.CompilerParams(vmem_limit_bytes=VMEM_BYTES),
    )(*args)


def shape(dims, dtype):
    return jax.ShapeDtypeStruct(dims, dtype)


def nt_dot(a, b):
    return lax.dot_general(a, b, (((1,), (1,)), ((), ())), preferred_element_type=f32)


def swap_halves(value):
    return jnp.concatenate([value[:, 64:], value[:, :64]], axis=1)


def unpack(piece, rows):
    tail = piece[2 * rows :]
    other = swap_halves(tail.astype(f32)).astype(bf16)
    tail = jnp.concatenate([tail, other[: rows - 64]], axis=0)
    return jnp.concatenate([piece[:rows], piece[rows : 2 * rows], tail], axis=1)


def pack_kernel(rank_ref, weights_ref, table_ref, wout_ref, out_ref, rest_ref):
    few, most = wout_ref[0:16].astype(f32), wout_ref[16:80].astype(f32)
    for at, value in ((288, few), (0, most)):
        ref = rest_ref if at == 0 else out_ref
        rows = value.shape[0]
        ref[at : at + rows, :] = value[:, 0:128].astype(bf16)
        ref[at + rows : at + 2 * rows, :] = value[:, 128:256].astype(bf16)
    tail = jnp.concatenate([few[:, 256:320], jnp.zeros((16, 64), f32)], axis=1)
    out_ref[320:336, :] = tail.astype(bf16)
    tail = jnp.concatenate([most[0:32, 256:320], most[32:64, 256:320]], axis=1)
    rest_ref[128:160, :] = tail.astype(bf16)
    turned = weights_ref[...].astype(f32).T
    out_ref[0:112, :] = turned[:, 0:128].astype(bf16)
    out_ref[112:224, :] = turned[:, 128:256].astype(bf16)
    block = lax.broadcasted_iota(i32, (ROWS, ROWS), 1)
    row = lax.broadcasted_iota(i32, (ROWS, ROWS), 0)
    named = [table_ref[:, k : k + 1] == block for k in range(KPS)]
    match = jnp.logical_or(named[0], named[1])
    first = jnp.min(jnp.where(match, row, ROWS - 1), axis=0, keepdims=True)
    last = jnp.max(jnp.where(match, row, 0), axis=0, keepdims=True)
    line = lax.broadcasted_iota(i32, (16, ROWS), 0)
    meta = jnp.where(line == 0, first, jnp.where(line == 1, last, 0))
    for s in range(STEPS):
        code = table_ref[:, KPS + s : KPS + s + 1]
        offset = jnp.zeros((ROWS, ROWS), i32)
        for k in range(KPS):
            here = jnp.logical_and(code // BLOCK == rank_ref[0] * KPS + k, named[k])
            offset = jnp.where(here, lax.rem(code, BLOCK) + 1, offset)
        for slot, target in enumerate((first, last)):
            value = jnp.sum(jnp.where(row == target, offset, 0), axis=0, keepdims=True)
            meta = jnp.where(line == 2 + 2 * s + slot, value, meta)
    side = jnp.concatenate([turned[64:112, 256:320], meta.astype(f32)], axis=0)
    out_ref[224:288, :] = jnp.concatenate([turned[0:64, 256:320], side], axis=1).astype(bf16)


def project_kernel(me_ref, x_ref, gain_ref, own_ref, other_ref, out_ref, meta_ref):
    me = me_ref[0]
    core = lax.rem(me, 2)
    wide = x_ref[...].astype(f32)
    scaled = (wide * gain_ref[...].astype(f32)).astype(bf16)
    scaled = jnp.concatenate([scaled, jnp.zeros((128, 64), bf16)], axis=1)
    lane = lax.broadcasted_iota(i32, (16, 128), 1)
    metas = [jnp.zeros((16, 128), f32), jnp.zeros((16, 128), f32)]
    line = lax.rem(lax.broadcasted_iota(i32, (TP * 8, 128), 0), 8)
    extra = jnp.zeros((TP * 8, 128), f32)
    for z in range(4):
        pieces = []
        for x in range(4):
            a = own_ref[x * 4 + z]
            b = other_ref[x * 4 + z]
            for c, piece in enumerate((jnp.where(core == 0, a, b), jnp.where(core == 0, b, a))):
                pieces.append(unpack(piece[:288], 112))
                table = piece[272:288].astype(f32)
                for j in range(2):
                    mine = jnp.where(lane == 64 + 2 * me + j, table, 0.0)
                    column = jnp.sum(mine, axis=1, keepdims=True)
                    at = 32 + gen_index(z, x, c)
                    metas[j] = jnp.where(lane == at, column, metas[j])
        table = own_ref[lax.rem(me // 2, 4) * 4 + z][272:288].astype(f32)
        for slot in range(2):
            extra = jnp.where(line == 2 * z + slot, table[slot : slot + 1], extra)
        part = nt_dot(scaled, jnp.concatenate(pieces, axis=0))
        out_ref[:, z * 896 : (z + 1) * 896] = part.astype(bf16)
    for j in range(2):
        meta_ref[16 * j : 16 * j + 16, :] = metas[j]
    squares = jnp.sum(wide * wide, axis=1, keepdims=True)
    high = squares.astype(bf16).astype(f32)
    low = squares - high
    lane = lax.broadcasted_iota(i32, (TP * 8, 128), 1)
    extra = jnp.where(lane < 64, 0.0, extra)
    extra = jnp.where(lane == 0, high, jnp.where(lane == 1, low, extra))
    out_ref[:, QKV:] = extra.astype(bf16)


def output_kernel(me_ref, mixed_ref, own_ref, other_ref, rest_ref, x_ref, rows_ref, packed_ref):
    core = lax.rem(me_ref[0], 2)
    part = jnp.zeros((128, 384), f32)
    for z in range(4):
        weights = []
        for g in range(8 * z, 8 * z + 8):
            place = g // 2 % 4 * 4 + z
            a, b = own_ref[place, 288:336, :], other_ref[place, 288:336, :]
            few = jnp.where(core == g % 2, a, b)
            weights.append(jnp.concatenate([few[0:16], few[16:32], few[32:48]], axis=1))
            rest = rest_ref[g]
            tail = rest[128:160]
            tail = jnp.concatenate([tail, swap_halves(tail.astype(f32)).astype(bf16)], axis=0)
            weights.append(jnp.concatenate([rest[0:64], rest[64:128], tail], axis=1))
        part = part + jnp.dot(
            mixed_ref[:, 640 * z : 640 * z + 640],
            jnp.concatenate(weights, axis=0),
            preferred_element_type=f32,
        )
    rows = (x_ref[...].astype(f32) + part[:, :320]).astype(bf16)
    rows_ref[...] = rows
    packed_ref[0:128, :] = rows[:, 0:128]
    packed_ref[128:256, :] = rows[:, 128:256]
    tail = rows[:, 256:320].astype(f32)
    packed_ref[256:320, :] = jnp.concatenate([tail[0:64], tail[64:128]], axis=1).astype(bf16)


def attend_kernel(parts_ref, cache_ref, lengths_ref, cos_ref, sin_ref, mixed_ref, entry_ref):
    total = parts_ref[0].astype(f32)
    for t in range(1, TP):
        total = total + parts_ref[t].astype(f32)
    squares = total[:, QKV : QKV + 1] + total[:, QKV + 1 : QKV + 2]
    total = total[:, :QKV] * lax.rsqrt(squares / D + epsilon)
    cosine, sine = cos_ref[...], sin_ref[...]

    def head(index):
        return total[:, index * HEAD_SIZE : (index + 1) * HEAD_SIZE]

    def rotated(index):
        vec = head(index)
        swapped = jnp.concatenate([vec[:, HEAD_SIZE // 2 :], vec[:, : HEAD_SIZE // 2]], axis=1)
        return vec * cosine + swapped * sine

    rows = 8 * GROUP
    row = lax.rem(lax.broadcasted_iota(i32, (8, OWN * PLACES), 0), OWN)
    lane = lax.broadcasted_iota(i32, (8, OWN * PLACES), 1)
    old_ok = jnp.logical_and(lane // PLACES == row, lax.rem(lane, PLACES) < lengths_ref[:, :1])
    old_bias = jnp.tile(jnp.where(old_ok, 0.0, -jnp.inf), (GROUP, 1))
    slot = lax.broadcasted_iota(i32, (8, 8), 1)
    fresh = lax.broadcasted_iota(i32, (8, 8), 0)
    new_ok = jnp.logical_and(lax.rem(slot, OWN) == lax.rem(fresh, OWN), slot // OWN <= fresh // OWN)
    new_bias = jnp.tile(jnp.where(new_ok, 0.0, -jnp.inf), (GROUP, 1))
    scale = HEAD_SIZE ** (-0.5)
    width = KEY_VALUE_HEADS * HEAD_SIZE
    for k in range(KEY_VALUE_HEADS):
        at = k * HEAD_SIZE
        new_k = rotated(QUERY_HEADS + k).astype(bf16)
        new_v = head(QUERY_HEADS + KEY_VALUE_HEADS + k).astype(bf16)
        entry_ref[:, at : at + HEAD_SIZE] = new_k
        entry_ref[:, width + at : width + at + HEAD_SIZE] = new_v
        query = jnp.concatenate([rotated(k * GROUP + h) for h in range(GROUP)], axis=0).astype(bf16)
        old_k = cache_ref[:, :, at : at + HEAD_SIZE].reshape(OWN * PLACES, HEAD_SIZE)
        old_v = cache_ref[:, :, width + at : width + at + HEAD_SIZE].reshape(OWN * PLACES, HEAD_SIZE)
        old_s = nt_dot(query, old_k) * scale + old_bias
        new_s = nt_dot(query, new_k) * scale + new_bias
        peak = jnp.maximum(
            jnp.max(old_s, axis=1, keepdims=True), jnp.max(new_s, axis=1, keepdims=True)
        )
        old_e, new_e = jnp.exp(old_s - peak), jnp.exp(new_s - peak)
        whole = jnp.sum(old_e, axis=1, keepdims=True) + jnp.sum(new_e, axis=1, keepdims=True)
        old_w, new_w = (old_e / whole).astype(bf16), (new_e / whole).astype(bf16)
        mixed = jnp.dot(old_w, old_v, preferred_element_type=f32)
        mixed = mixed + jnp.dot(new_w, new_v, preferred_element_type=f32)
        for h in range(GROUP):
            to = (k * GROUP + h) * HEAD_SIZE
            mixed_ref[:, to : to + HEAD_SIZE] = mixed[8 * h : 8 * h + 8].astype(bf16)


def select_kernel(layer_ref, spot_ref, out_ref):
    owners = out_ref.shape[0]
    lane = lax.broadcasted_iota(i32, (16 * owners, 256), 1)
    low = lax.broadcasted_iota(i32, (256, 128), 1) < 64
    tails = jnp.zeros((16 * owners, 128), f32)
    for half in range(2):
        pieces = [layer_ref[2 * half], layer_ref[2 * half + 1]]
        sides = [jnp.concatenate([p[256:], swap_halves(p[256:].astype(f32)).astype(bf16)], axis=0) for p in pieces]
        tail = jnp.concatenate(sides, axis=0).astype(f32)
        if half:
            tail = swap_halves(tail)
        tail = jnp.where(low if half == 0 else jnp.logical_not(low), tail, 0.0).astype(bf16)
        pick = (spot_ref[:, half : half + 1] == lane).astype(f32).astype(bf16)
        for part in range(2):
            rows = jnp.concatenate([p[128 * part : 128 * part + 128] for p in pieces], axis=0)
            taken = jnp.dot(pick, rows, preferred_element_type=f32).astype(bf16)
            at = 32 * part + 16 * half
            out_ref[:, at : at + 16, :] = taken.reshape(owners, 16, 128)
        tails = tails + jnp.dot(pick, tail, preferred_element_type=f32)
    out_ref[:, 64:80, :] = tails.astype(bf16).reshape(owners, 16, 128)


def logits_kernel(rows_ref, gain_ref, head_ref, offset_ref, out_ref):
    def piece(t):
        tail = rows_ref[:, t, 64:80, :].reshape(128, 128).astype(f32)
        tail = [tail.reshape(8, 16, 128), swap_halves(tail).reshape(8, 16, 128)]
        parts = [rows_ref[:, t, 0:32, :].reshape(256, 128), rows_ref[:, t, 32:64, :].reshape(256, 128)]
        wide = [p.astype(f32) for p in parts]
        return wide + [jnp.concatenate(tail, axis=1).reshape(256, 128)[:, :64]]

    squares = jnp.zeros((256, 128), f32)
    tails = jnp.zeros((256, 64), f32)
    for t in range(TP):
        a, b, c = piece(t)
        squares = squares + (a * a + b * b)
        tails = tails + c * c
    total = jnp.sum(squares, axis=1, keepdims=True) + jnp.sum(tails, axis=1, keepdims=True)
    factor = lax.rsqrt(total / D + epsilon)
    logits = jnp.zeros((256, 2 * BLOCK), f32)
    for t in range(TP):
        at = t * 320
        for value, width in zip(piece(t), (128, 128, 64)):
            normed = (value * factor * gain_ref[:, at : at + width].astype(f32)).astype(bf16)
            weights = head_ref[at : at + width, :]
            logits = logits + jnp.dot(normed, weights, preferred_element_type=f32)
            at += width
    pair = lax.broadcasted_iota(i32, (256, BLOCK), 0)
    logits = jnp.where(lax.rem(pair // 4, 2) == 0, logits[:, :BLOCK], logits[:, BLOCK:])
    token = lax.broadcasted_iota(i32, (BLOCK, 128), 0)
    line = lax.broadcasted_iota(i32, (8, 128), 0)
    for half in range(2):
        side = logits[128 * half : 128 * half + 128].T
        peak = jnp.max(side, axis=0, keepdims=True)
        mass = jnp.sum(jnp.exp(side - peak), axis=0, keepdims=True)
        target = offset_ref[:, 128 * half : 128 * half + 128] - 1
        picked = jnp.sum(jnp.where(token == target, side, 0.0), axis=0, keepdims=True)
        out = jnp.where(line == 0, peak, jnp.where(line == 1, mass, picked))
        out_ref[:, 128 * half : 128 * half + 128] = out


def rows_kernel(stats_ref, row_ref, out_ref):
    mine = lax.broadcasted_iota(i32, (ROWS, GEN), 0)
    lane = lax.broadcasted_iota(i32, (ROWS, 128), 1)
    out = jnp.zeros((ROWS, 128), f32)
    for s in range(STEPS):
        best = jnp.full((ROWS, 1), -jnp.inf, f32)
        combos = [(j, slot) for j in range(2) for slot in range(2)]
        masks = [row_ref[2 * j + slot : 2 * j + slot + 1, :] == mine for j, slot in combos]

        def stat(which, j, slot):
            at = which * 8 + j * 4 + slot * 2 + s
            return stats_ref[at : at + 1, :]

        for mask, (j, slot) in zip(masks, combos):
            peak = jnp.where(mask, stat(0, j, slot), -jnp.inf)
            best = jnp.maximum(best, jnp.max(peak, axis=1, keepdims=True))
        mass = jnp.zeros((ROWS, 1), f32)
        picked = jnp.zeros((ROWS, 1), f32)
        for mask, (j, slot) in zip(masks, combos):
            grown = stat(1, j, slot) * jnp.exp(jnp.where(mask, stat(0, j, slot), best) - best)
            mass = mass + jnp.sum(jnp.where(mask, grown, 0.0), axis=1, keepdims=True)
            picked = picked + jnp.sum(
                jnp.where(mask, stat(2, j, slot), 0.0), axis=1, keepdims=True
            )
        for at, value in enumerate((best, mass, picked)):
            out = jnp.where(lane == 3 * s + at, value, out)
    out_ref[...] = out


def gen_index(z, x, core):
    return (z * 4 + x) * 2 + core


Z_GROUPS = [[gen_index(z, x, c) for z in range(4)] for x in range(4) for c in range(2)]
X_GROUPS = [[gen_index(z, x, c) for x in range(4)] for z in range(4) for c in range(2)]


LAYERS = [[z * 128 + i for i in range(128)] for z in range(4)]


def gather_gen(piece):
    along_z = spread(piece, "gen", 4, Z_GROUPS)
    along_x = spread(along_z, "gen", 4, X_GROUPS)
    own = along_x.reshape((16,) + piece.shape)
    return own, lax.ppermute(own, "gen", [(g, g ^ 1) for g in range(GEN)])


def all_to_all(value, axis, groups=None):
    return lax.all_to_all(
        value, axis, split_axis=0, concat_axis=0, tiled=True, axis_index_groups=groups
    )


def spread(value, axis, count, groups=None):
    return all_to_all(jnp.broadcast_to(value[None], (count,) + value.shape), axis, groups)


def rotary_tables(lengths):
    half = HEAD_SIZE // 2
    exponent = jnp.arange(half, dtype=f32) * (2.0 / HEAD_SIZE)
    inverse = jnp.power(f32(rope_base), -exponent)
    positions = (jnp.arange(STEPS, dtype=i32)[:, None] + lengths[None, :]).reshape(-1)
    angles = positions.astype(f32)[:, None] * inverse[None, :]
    cosine, sine = jnp.cos(angles), jnp.sin(angles)
    return (
        jnp.concatenate([cosine, cosine], axis=1),
        jnp.concatenate([-sine, sine], axis=1),
    )


def row_table(kept):
    row = jnp.arange(ROWS, dtype=i32)[:, None]
    match = jnp.any(kept[:, :, None] == jnp.arange(ROWS, dtype=i32), axis=1)
    first = jnp.min(jnp.where(match, row, ROWS - 1), axis=0)
    last = jnp.max(jnp.where(match, row, 0), axis=0)
    return jnp.stack([first, last], axis=1)


def body(embeddings, cache, lengths, attn_gain, wqkv, wout, final_gain, head, kept, chosen):
    rank = lax.axis_index("tp").astype(i32)
    me = lax.axis_index("gen").astype(i32)
    features = D // TP

    table = jnp.concatenate([kept[0], chosen.T], axis=1)
    piece, rest = call(
        pack_kernel,
        (shape((336, 128), bf16), shape((160, 128), bf16)),
        rank.reshape(1),
        wqkv,
        table,
        wout,
        scalars=1,
    )
    rest = lax.all_gather(rest, "gen")
    own_w, other_w = gather_gen(piece)

    x = embeddings.reshape(STEPS, TP, OWN, features).transpose(1, 0, 2, 3).reshape(128, features)
    parts, meta = call(
        project_kernel,
        (shape((128, QKV + 128), bf16), shape((32, 128), f32)),
        me.reshape(1),
        x,
        attn_gain.reshape(1, features),
        own_w,
        other_w,
        scalars=1,
    )
    parts, rest = lax.optimization_barrier((parts, rest))
    parts = all_to_all(parts.reshape(TP, 8, QKV + 128), "tp")

    meta = meta.reshape(2, 16, 128)[:, :6, 32:64].astype(i32).reshape(2, 3, 2, GEN)
    offset = meta[:, 1:].reshape(2, 2, 2, 4, 8).transpose(4, 3, 0, 2, 1).reshape(1, 256)
    routes = lax.dynamic_slice_in_dim(parts[:, :, QKV + 64 :], me // 8 * 16, 16, 2)
    row = routes.astype(f32).astype(i32).reshape(TP, 2, 2, 2, 8, 2).transpose(4, 0, 2, 5, 3, 1)
    spot = jnp.arange(2, dtype=i32)[:, None, None, None] * 128 + row // OWN * 8 + row % OWN
    spot = spot[:, :, :, :, :, None, :] + jnp.arange(STEPS, dtype=i32)[:, None] * OWN
    spot = spot.reshape(16 * 128, 2)

    cosine, sine = rotary_tables(lengths)
    wide_lengths = jnp.broadcast_to(jnp.tile(lengths, STEPS)[:, None], (8, 128))
    mixed, entries = call(
        attend_kernel,
        (shape((8, QUERY_HEADS * HEAD_SIZE), bf16), shape((8, 1024), bf16)),
        parts,
        cache,
        wide_lengths,
        cosine,
        sine,
    )
    mixed = spread(mixed, "tp", TP).reshape(128, QUERY_HEADS * HEAD_SIZE)
    layer_out, packed = call(
        output_kernel,
        (shape((128, features), bf16), shape((320, 128), bf16)),
        me.reshape(1),
        mixed,
        own_w,
        other_w,
        rest,
        x,
        scalars=1,
    )
    last_hidden = layer_out.reshape(TP, STEPS, OWN, features)[:, -1].reshape(ROWS, features)

    layers = spread(packed, "gen", 4, Z_GROUPS)
    taken = call(select_kernel, shape((128, 80, 128), bf16), layers, spot)
    taken = all_to_all(taken, ("gen", "tp"), LAYERS).reshape(8, TP, 80, 128)
    stats = call(
        logits_kernel,
        shape((8, 256), f32),
        taken,
        final_gain.reshape(1, D),
        head,
        offset,
    )
    stats = stats[:3].reshape(3, 8, 4, 8).transpose(2, 1, 0, 3).reshape(GEN, 1, 24)
    stats = all_to_all(stats, "gen").reshape(GEN, 24).T
    rows_of = row_table(kept[0]).reshape(GEN, 4).T
    row_stats = call(rows_kernel, shape((ROWS, 128), f32), stats, rows_of)
    row_stats = all_to_all(row_stats.reshape(TP, OWN, 128)[:, :, :8], "tp")
    peak, mass, picked = (row_stats[:, :, i : 3 * STEPS : 3] for i in range(3))
    best = jnp.max(peak, axis=0)
    mass = jnp.sum(mass * jnp.exp(peak - best), axis=0)
    logprobs = jnp.sum(picked, axis=0) - best - jnp.log(mass)
    return logprobs.T, last_hidden, entries.reshape(STEPS, OWN, 1024)


def solution(mesh):
    return jax.shard_map(
        body,
        mesh=mesh,
        in_specs=(
            P(None, "gen", "tp"),
            P(("gen", "tp"), None, None),
            P(("gen", "tp")),
            P("tp"),
            P("tp", "gen"),
            P("gen", "tp"),
            P(),
            P(None, ("gen", "tp")),
            P("tp", "gen", None),
            P(None, "gen"),
        ),
        out_specs=(P(None, ("gen", "tp")), P("gen", "tp"), P(None, ("gen", "tp"), None)),
        check_vma=False,
    )
```

```python
import jax
import jax.numpy as jnp
from jax import lax
from jax.experimental import pallas as pl
from jax.experimental.pallas import tpu as pltpu
from jax.sharding import PartitionSpec as P

D = 5120
QUERY_HEADS = 20
KEY_VALUE_HEADS = 4
GROUP = QUERY_HEADS // KEY_VALUE_HEADS
HEAD_SIZE = 128
BLOCK = 128
KPS = 2
STEPS = 2
QKV = 3584
GEN = 32
TP = 16
ROWS = 64
OWN = ROWS // TP
PLACES = 128

epsilon = 1e-06
rope_base = 1000000.0

bf16 = jnp.bfloat16
f32 = jnp.float32
i32 = jnp.int32
VMEM_BYTES = 48 * 1024 * 1024


def call(kernel, out_shape, *args, scalars=0, scratch=()):
    specs = [pl.BlockSpec(memory_space=pltpu.SMEM)] * scalars
    specs += [pl.BlockSpec(memory_space=pltpu.VMEM)] * (len(args) - scalars)
    return pl.pallas_call(
        kernel,
        out_shape=out_shape,
        in_specs=specs,
        out_specs=jax.tree.map(lambda _: pl.BlockSpec(memory_space=pltpu.VMEM), out_shape),
        scratch_shapes=list(scratch),
        compiler_params=pltpu.CompilerParams(vmem_limit_bytes=VMEM_BYTES),
    )(*args)


def shape(dims, dtype):
    return jax.ShapeDtypeStruct(dims, dtype)


def nt_dot(a, b):
    return lax.dot_general(a, b, (((1,), (1,)), ((), ())), preferred_element_type=f32)


def swap_halves(value):
    return jnp.concatenate([value[:, 64:], value[:, :64]], axis=1)


def unpack(piece, rows):
    tail = piece[2 * rows :]
    other = swap_halves(tail.astype(f32)).astype(bf16)
    tail = jnp.concatenate([tail, other[: rows - 64]], axis=0)
    return jnp.concatenate([piece[:rows], piece[rows : 2 * rows], tail], axis=1)


def pack_kernel(rank_ref, weights_ref, table_ref, wout_ref, out_ref):
    wide = wout_ref[...].astype(f32)
    out_ref[288:368, :] = wide[:, 0:128].astype(bf16)
    out_ref[368:448, :] = wide[:, 128:256].astype(bf16)
    tail = jnp.concatenate([wide[0:48, 256:320], wide[32:80, 256:320]], axis=1)
    out_ref[448:496, :] = tail.astype(bf16)
    turned = weights_ref[...].astype(f32).T
    out_ref[0:112, :] = turned[:, 0:128].astype(bf16)
    out_ref[112:224, :] = turned[:, 128:256].astype(bf16)
    block = lax.broadcasted_iota(i32, (ROWS, ROWS), 1)
    row = lax.broadcasted_iota(i32, (ROWS, ROWS), 0)
    named = [table_ref[:, k : k + 1] == block for k in range(KPS)]
    match = jnp.logical_or(named[0], named[1])
    first = jnp.min(jnp.where(match, row, ROWS - 1), axis=0, keepdims=True)
    last = jnp.max(jnp.where(match, row, 0), axis=0, keepdims=True)
    line = lax.broadcasted_iota(i32, (16, ROWS), 0)
    meta = jnp.where(line == 0, first, jnp.where(line == 1, last, 0))
    for s in range(STEPS):
        code = table_ref[:, KPS + s : KPS + s + 1]
        offset = jnp.zeros((ROWS, ROWS), i32)
        for k in range(KPS):
            here = jnp.logical_and(code // BLOCK == rank_ref[0] * KPS + k, named[k])
            offset = jnp.where(here, lax.rem(code, BLOCK) + 1, offset)
        for slot, target in enumerate((first, last)):
            value = jnp.sum(jnp.where(row == target, offset, 0), axis=0, keepdims=True)
            meta = jnp.where(line == 2 + 2 * s + slot, value, meta)
    side = jnp.concatenate([turned[64:112, 256:320], meta.astype(f32)], axis=0)
    out_ref[224:288, :] = jnp.concatenate([turned[0:64, 256:320], side], axis=1).astype(bf16)


def project_kernel(me_ref, x_ref, gain_ref, own_ref, other_ref, out_ref, meta_ref):
    me = me_ref[0]
    core = lax.rem(me, 2)
    wide = x_ref[...].astype(f32)
    scaled = (wide * gain_ref[...].astype(f32)).astype(bf16)
    scaled = jnp.concatenate([scaled, jnp.zeros((128, 64), bf16)], axis=1)
    lane = lax.broadcasted_iota(i32, (16, 128), 1)
    metas = [jnp.zeros((16, 128), f32), jnp.zeros((16, 128), f32)]
    line = lax.rem(lax.broadcasted_iota(i32, (TP * 8, 128), 0), 8)
    extra = jnp.zeros((TP * 8, 128), f32)
    for z in range(4):
        pieces = []
        for x in range(4):
            a = own_ref[x * 4 + z]
            b = other_ref[x * 4 + z]
            for c, piece in enumerate((jnp.where(core == 0, a, b), jnp.where(core == 0, b, a))):
                pieces.append(unpack(piece, 112))
                table = piece[272:288].astype(f32)
                for j in range(2):
                    mine = jnp.where(lane == 64 + 2 * me + j, table, 0.0)
                    column = jnp.sum(mine, axis=1, keepdims=True)
                    at = 32 + gen_index(z, x, c)
                    metas[j] = jnp.where(lane == at, column, metas[j])
        table = own_ref[lax.rem(me // 2, 4) * 4 + z][272:288].astype(f32)
        for slot in range(2):
            extra = jnp.where(line == 2 * z + slot, table[slot : slot + 1], extra)
        part = nt_dot(scaled, jnp.concatenate(pieces, axis=0))
        out_ref[:, z * 896 : (z + 1) * 896] = part.astype(bf16)
    for j in range(2):
        meta_ref[16 * j : 16 * j + 16, :] = metas[j]
    squares = jnp.sum(wide * wide, axis=1, keepdims=True)
    high = squares.astype(bf16).astype(f32)
    low = squares - high
    lane = lax.broadcasted_iota(i32, (TP * 8, 128), 1)
    extra = jnp.where(lane < 64, 0.0, extra)
    extra = jnp.where(lane == 0, high, jnp.where(lane == 1, low, extra))
    out_ref[:, QKV:] = extra.astype(bf16)


def output_kernel(mixed_ref, weights_ref, x_ref, rows_ref, packed_ref):
    part = jnp.zeros((128, 384), f32)
    for z in range(4):
        weights = []
        for g in range(8):
            piece = weights_ref[g, z]
            tail = piece[160:208]
            other = swap_halves(tail.astype(f32)).astype(bf16)
            tail = jnp.concatenate([tail, other[16:48]], axis=0)
            weights.append(jnp.concatenate([piece[0:80], piece[80:160], tail], axis=1))
        part = part + jnp.dot(
            mixed_ref[:, 640 * z : 640 * z + 640],
            jnp.concatenate(weights, axis=0),
            preferred_element_type=f32,
        )
    rows = (x_ref[...].astype(f32) + part[:, :320]).astype(bf16)
    rows_ref[...] = rows
    packed_ref[0:128, :] = rows[:, 0:128]
    packed_ref[128:256, :] = rows[:, 128:256]
    tail = rows[:, 256:320].astype(f32)
    packed_ref[256:320, :] = jnp.concatenate([tail[0:64], tail[64:128]], axis=1).astype(bf16)


def attend_kernel(parts_ref, cache_ref, lengths_ref, cos_ref, sin_ref, mixed_ref, entry_ref):
    total = parts_ref[0].astype(f32)
    for t in range(1, TP):
        total = total + parts_ref[t].astype(f32)
    squares = total[:, QKV : QKV + 1] + total[:, QKV + 1 : QKV + 2]
    total = total[:, :QKV] * lax.rsqrt(squares / D + epsilon)
    cosine, sine = cos_ref[...], sin_ref[...]

    def head(index):
        return total[:, index * HEAD_SIZE : (index + 1) * HEAD_SIZE]

    def rotated(index):
        vec = head(index)
        swapped = jnp.concatenate([vec[:, HEAD_SIZE // 2 :], vec[:, : HEAD_SIZE // 2]], axis=1)
        return vec * cosine + swapped * sine

    rows = 8 * GROUP
    row = lax.rem(lax.broadcasted_iota(i32, (8, OWN * PLACES), 0), OWN)
    lane = lax.broadcasted_iota(i32, (8, OWN * PLACES), 1)
    old_ok = jnp.logical_and(lane // PLACES == row, lax.rem(lane, PLACES) < lengths_ref[:, :1])
    old_bias = jnp.tile(jnp.where(old_ok, 0.0, -jnp.inf), (GROUP, 1))
    slot = lax.broadcasted_iota(i32, (8, 8), 1)
    fresh = lax.broadcasted_iota(i32, (8, 8), 0)
    new_ok = jnp.logical_and(lax.rem(slot, OWN) == lax.rem(fresh, OWN), slot // OWN <= fresh // OWN)
    new_bias = jnp.tile(jnp.where(new_ok, 0.0, -jnp.inf), (GROUP, 1))
    scale = HEAD_SIZE ** (-0.5)
    width = KEY_VALUE_HEADS * HEAD_SIZE
    for k in range(KEY_VALUE_HEADS):
        at = k * HEAD_SIZE
        new_k = rotated(QUERY_HEADS + k).astype(bf16)
        new_v = head(QUERY_HEADS + KEY_VALUE_HEADS + k).astype(bf16)
        entry_ref[:, at : at + HEAD_SIZE] = new_k
        entry_ref[:, width + at : width + at + HEAD_SIZE] = new_v
        query = jnp.concatenate([rotated(k * GROUP + h) for h in range(GROUP)], axis=0).astype(bf16)
        old_k = cache_ref[:, :, at : at + HEAD_SIZE].reshape(OWN * PLACES, HEAD_SIZE)
        old_v = cache_ref[:, :, width + at : width + at + HEAD_SIZE].reshape(OWN * PLACES, HEAD_SIZE)
        old_s = nt_dot(query, old_k) * scale + old_bias
        new_s = nt_dot(query, new_k) * scale + new_bias
        peak = jnp.maximum(
            jnp.max(old_s, axis=1, keepdims=True), jnp.max(new_s, axis=1, keepdims=True)
        )
        old_e, new_e = jnp.exp(old_s - peak), jnp.exp(new_s - peak)
        whole = jnp.sum(old_e, axis=1, keepdims=True) + jnp.sum(new_e, axis=1, keepdims=True)
        old_w, new_w = (old_e / whole).astype(bf16), (new_e / whole).astype(bf16)
        mixed = jnp.dot(old_w, old_v, preferred_element_type=f32)
        mixed = mixed + jnp.dot(new_w, new_v, preferred_element_type=f32)
        for h in range(GROUP):
            to = (k * GROUP + h) * HEAD_SIZE
            mixed_ref[:, to : to + HEAD_SIZE] = mixed[8 * h : 8 * h + 8].astype(bf16)


def select_kernel(layer_ref, spot_ref, out_ref):
    owners = out_ref.shape[0]
    lane = lax.broadcasted_iota(i32, (16 * owners, 256), 1)
    low = lax.broadcasted_iota(i32, (256, 128), 1) < 64
    tails = jnp.zeros((16 * owners, 128), f32)
    for half in range(2):
        pieces = [layer_ref[2 * half], layer_ref[2 * half + 1]]
        sides = [jnp.concatenate([p[256:], swap_halves(p[256:].astype(f32)).astype(bf16)], axis=0) for p in pieces]
        tail = jnp.concatenate(sides, axis=0).astype(f32)
        if half:
            tail = swap_halves(tail)
        tail = jnp.where(low if half == 0 else jnp.logical_not(low), tail, 0.0).astype(bf16)
        pick = (spot_ref[:, half : half + 1] == lane).astype(f32).astype(bf16)
        for part in range(2):
            rows = jnp.concatenate([p[128 * part : 128 * part + 128] for p in pieces], axis=0)
            taken = jnp.dot(pick, rows, preferred_element_type=f32).astype(bf16)
            at = 32 * part + 16 * half
            out_ref[:, at : at + 16, :] = taken.reshape(owners, 16, 128)
        tails = tails + jnp.dot(pick, tail, preferred_element_type=f32)
    out_ref[:, 64:80, :] = tails.astype(bf16).reshape(owners, 16, 128)


def logits_kernel(rows_ref, gain_ref, head_ref, offset_ref, out_ref):
    def piece(t):
        tail = rows_ref[:, t, 64:80, :].reshape(128, 128).astype(f32)
        tail = [tail.reshape(8, 16, 128), swap_halves(tail).reshape(8, 16, 128)]
        parts = [rows_ref[:, t, 0:32, :].reshape(256, 128), rows_ref[:, t, 32:64, :].reshape(256, 128)]
        wide = [p.astype(f32) for p in parts]
        return wide + [jnp.concatenate(tail, axis=1).reshape(256, 128)[:, :64]]

    squares = jnp.zeros((256, 128), f32)
    tails = jnp.zeros((256, 64), f32)
    for t in range(TP):
        a, b, c = piece(t)
        squares = squares + (a * a + b * b)
        tails = tails + c * c
    total = jnp.sum(squares, axis=1, keepdims=True) + jnp.sum(tails, axis=1, keepdims=True)
    factor = lax.rsqrt(total / D + epsilon)
    logits = jnp.zeros((256, 2 * BLOCK), f32)
    for t in range(TP):
        at = t * 320
        for value, width in zip(piece(t), (128, 128, 64)):
            normed = (value * factor * gain_ref[:, at : at + width].astype(f32)).astype(bf16)
            weights = head_ref[at : at + width, :]
            logits = logits + jnp.dot(normed, weights, preferred_element_type=f32)
            at += width
    pair = lax.broadcasted_iota(i32, (256, BLOCK), 0)
    logits = jnp.where(lax.rem(pair // 4, 2) == 0, logits[:, :BLOCK], logits[:, BLOCK:])
    token = lax.broadcasted_iota(i32, (BLOCK, 128), 0)
    line = lax.broadcasted_iota(i32, (8, 128), 0)
    for half in range(2):
        side = logits[128 * half : 128 * half + 128].T
        peak = jnp.max(side, axis=0, keepdims=True)
        mass = jnp.sum(jnp.exp(side - peak), axis=0, keepdims=True)
        target = offset_ref[:, 128 * half : 128 * half + 128] - 1
        picked = jnp.sum(jnp.where(token == target, side, 0.0), axis=0, keepdims=True)
        out = jnp.where(line == 0, peak, jnp.where(line == 1, mass, picked))
        out_ref[:, 128 * half : 128 * half + 128] = out


def rows_kernel(stats_ref, row_ref, out_ref):
    mine = lax.broadcasted_iota(i32, (ROWS, GEN), 0)
    lane = lax.broadcasted_iota(i32, (ROWS, 128), 1)
    out = jnp.zeros((ROWS, 128), f32)
    for s in range(STEPS):
        best = jnp.full((ROWS, 1), -jnp.inf, f32)
        combos = [(j, slot) for j in range(2) for slot in range(2)]
        masks = [row_ref[2 * j + slot : 2 * j + slot + 1, :] == mine for j, slot in combos]

        def stat(which, j, slot):
            at = which * 8 + j * 4 + slot * 2 + s
            return stats_ref[at : at + 1, :]

        for mask, (j, slot) in zip(masks, combos):
            peak = jnp.where(mask, stat(0, j, slot), -jnp.inf)
            best = jnp.maximum(best, jnp.max(peak, axis=1, keepdims=True))
        mass = jnp.zeros((ROWS, 1), f32)
        picked = jnp.zeros((ROWS, 1), f32)
        for mask, (j, slot) in zip(masks, combos):
            grown = stat(1, j, slot) * jnp.exp(jnp.where(mask, stat(0, j, slot), best) - best)
            mass = mass + jnp.sum(jnp.where(mask, grown, 0.0), axis=1, keepdims=True)
            picked = picked + jnp.sum(
                jnp.where(mask, stat(2, j, slot), 0.0), axis=1, keepdims=True
            )
        for at, value in enumerate((best, mass, picked)):
            out = jnp.where(lane == 3 * s + at, value, out)
    out_ref[...] = out


def gen_index(z, x, core):
    return (z * 4 + x) * 2 + core


Z_GROUPS = [[gen_index(z, x, c) for z in range(4)] for x in range(4) for c in range(2)]
X_GROUPS = [[gen_index(z, x, c) for x in range(4)] for z in range(4) for c in range(2)]


LAYERS = [[z * 128 + i for i in range(128)] for z in range(4)]


XC_GROUPS = [[z * 8 + i for i in range(8)] for z in range(4)]


def all_to_all(value, axis, groups=None):
    return lax.all_to_all(
        value, axis, split_axis=0, concat_axis=0, tiled=True, axis_index_groups=groups
    )


def spread(value, axis, count, groups=None):
    return all_to_all(jnp.broadcast_to(value[None], (count,) + value.shape), axis, groups)


def rotary_tables(lengths):
    half = HEAD_SIZE // 2
    exponent = jnp.arange(half, dtype=f32) * (2.0 / HEAD_SIZE)
    inverse = jnp.power(f32(rope_base), -exponent)
    positions = (jnp.arange(STEPS, dtype=i32)[:, None] + lengths[None, :]).reshape(-1)
    angles = positions.astype(f32)[:, None] * inverse[None, :]
    cosine, sine = jnp.cos(angles), jnp.sin(angles)
    return (
        jnp.concatenate([cosine, cosine], axis=1),
        jnp.concatenate([-sine, sine], axis=1),
    )


def row_table(kept):
    row = jnp.arange(ROWS, dtype=i32)[:, None]
    match = jnp.any(kept[:, :, None] == jnp.arange(ROWS, dtype=i32), axis=1)
    first = jnp.min(jnp.where(match, row, ROWS - 1), axis=0)
    last = jnp.max(jnp.where(match, row, 0), axis=0)
    return jnp.stack([first, last], axis=1)


def body(embeddings, cache, lengths, attn_gain, wqkv, wout, final_gain, head, kept, chosen):
    rank = lax.axis_index("tp").astype(i32)
    me = lax.axis_index("gen").astype(i32)
    features = D // TP

    table = jnp.concatenate([kept[0], chosen.T], axis=1)
    piece = call(
        pack_kernel, shape((496, 128), bf16), rank.reshape(1), wqkv, table, wout, scalars=1
    )
    along_z = spread(piece, "gen", 4, Z_GROUPS)
    out_whole = lax.all_gather(along_z[:, 288:], "gen", axis_index_groups=XC_GROUPS)
    own_w = spread(along_z[:, :288], "gen", 4, X_GROUPS).reshape(16, 288, 128)
    other_w = lax.ppermute(own_w, "gen", [(g, g ^ 1) for g in range(GEN)])

    x = embeddings.reshape(STEPS, TP, OWN, features).transpose(1, 0, 2, 3).reshape(128, features)
    parts, meta = call(
        project_kernel,
        (shape((128, QKV + 128), bf16), shape((32, 128), f32)),
        me.reshape(1),
        x,
        attn_gain.reshape(1, features),
        own_w,
        other_w,
        scalars=1,
    )
    parts = all_to_all(parts.reshape(TP, 8, QKV + 128), "tp")

    meta = meta.reshape(2, 16, 128)[:, :6, 32:64].astype(i32).reshape(2, 3, 2, GEN)
    offset = meta[:, 1:].reshape(2, 2, 2, 4, 8).transpose(4, 3, 0, 2, 1).reshape(1, 256)
    routes = lax.dynamic_slice_in_dim(parts[:, :, QKV + 64 :], me // 8 * 16, 16, 2)
    row = routes.astype(f32).astype(i32).reshape(TP, 2, 2, 2, 8, 2).transpose(4, 0, 2, 5, 3, 1)
    spot = jnp.arange(2, dtype=i32)[:, None, None, None] * 128 + row // OWN * 8 + row % OWN
    spot = spot[:, :, :, :, :, None, :] + jnp.arange(STEPS, dtype=i32)[:, None] * OWN
    spot = spot.reshape(16 * 128, 2)

    cosine, sine = rotary_tables(lengths)
    wide_lengths = jnp.broadcast_to(jnp.tile(lengths, STEPS)[:, None], (8, 128))
    mixed, entries = call(
        attend_kernel,
        (shape((8, QUERY_HEADS * HEAD_SIZE), bf16), shape((8, 1024), bf16)),
        parts,
        cache,
        wide_lengths,
        cosine,
        sine,
    )
    mixed = spread(mixed, "tp", TP).reshape(128, QUERY_HEADS * HEAD_SIZE)
    layer_out, packed = call(
        output_kernel,
        (shape((128, features), bf16), shape((320, 128), bf16)),
        mixed,
        out_whole,
        x,
    )
    last_hidden = layer_out.reshape(TP, STEPS, OWN, features)[:, -1].reshape(ROWS, features)

    layers = spread(packed, "gen", 4, Z_GROUPS)
    taken = call(select_kernel, shape((128, 80, 128), bf16), layers, spot)
    taken = all_to_all(taken, ("gen", "tp"), LAYERS).reshape(8, TP, 80, 128)
    stats = call(
        logits_kernel,
        shape((8, 256), f32),
        taken,
        final_gain.reshape(1, D),
        head,
        offset,
    )
    stats = stats[:3].reshape(3, 8, 4, 8).transpose(2, 1, 0, 3).reshape(GEN, 1, 24)
    stats = all_to_all(stats, "gen").reshape(GEN, 24).T
    rows_of = row_table(kept[0]).reshape(GEN, 4).T
    row_stats = call(rows_kernel, shape((ROWS, 128), f32), stats, rows_of)
    row_stats = all_to_all(row_stats.reshape(TP, OWN, 128)[:, :, :8], "tp")
    peak, mass, picked = (row_stats[:, :, i : 3 * STEPS : 3] for i in range(3))
    best = jnp.max(peak, axis=0)
    mass = jnp.sum(mass * jnp.exp(peak - best), axis=0)
    logprobs = jnp.sum(picked, axis=0) - best - jnp.log(mass)
    return logprobs.T, last_hidden, entries.reshape(STEPS, OWN, 1024)


def solution(mesh):
    return jax.shard_map(
        body,
        mesh=mesh,
        in_specs=(
            P(None, "gen", "tp"),
            P(("gen", "tp"), None, None),
            P(("gen", "tp")),
            P("tp"),
            P("tp", "gen"),
            P("gen", "tp"),
            P(),
            P(None, ("gen", "tp")),
            P("tp", "gen", None),
            P(None, "gen"),
        ),
        out_specs=(P(None, ("gen", "tp")), P("gen", "tp"), P(None, ("gen", "tp"), None)),
        check_vma=False,
    )
```

```python
import jax
import jax.numpy as jnp
from jax import lax
from jax.experimental import pallas as pl
from jax.experimental.pallas import tpu as pltpu
from jax.sharding import PartitionSpec as P

D = 5120
QUERY_HEADS = 20
KEY_VALUE_HEADS = 4
GROUP = QUERY_HEADS // KEY_VALUE_HEADS
HEAD_SIZE = 128
BLOCK = 128
KPS = 2
STEPS = 2
QKV = 3584
GEN = 32
TP = 16
ROWS = 64
OWN = ROWS // TP
PLACES = 128

epsilon = 1e-06
rope_base = 1000000.0

bf16 = jnp.bfloat16
f32 = jnp.float32
i32 = jnp.int32
MIB = 1024 * 1024


def call(kernel, out_shape, *args, scalars=0, away=0, scratch=(), vmem=48):
    specs = [pl.BlockSpec(memory_space=pltpu.SMEM)] * scalars
    specs += [pl.BlockSpec(memory_space=pltpu.VMEM)] * (len(args) - scalars - away)
    specs += [pl.BlockSpec(memory_space=pl.ANY)] * away
    return pl.pallas_call(
        kernel,
        out_shape=out_shape,
        in_specs=specs,
        out_specs=jax.tree.map(lambda _: pl.BlockSpec(memory_space=pltpu.VMEM), out_shape),
        scratch_shapes=list(scratch),
        compiler_params=pltpu.CompilerParams(vmem_limit_bytes=vmem * MIB),
    )(*args)


def shape(dims, dtype):
    return jax.ShapeDtypeStruct(dims, dtype)


def nt_dot(a, b):
    return lax.dot_general(a, b, (((1,), (1,)), ((), ())), preferred_element_type=f32)


def swap_halves(value):
    return jnp.concatenate([value[:, 64:], value[:, :64]], axis=1)


def unpack(piece, rows):
    tail = piece[2 * rows :]
    other = swap_halves(tail.astype(f32)).astype(bf16)
    tail = jnp.concatenate([tail, other[: rows - 64]], axis=0)
    return jnp.concatenate([piece[:rows], piece[rows : 2 * rows], tail], axis=1)


def pack_out_kernel(wout_ref, out_ref):
    wide = wout_ref[...].astype(f32)
    out_ref[0:80, :] = wide[:, 0:128].astype(bf16)
    out_ref[80:160, :] = wide[:, 128:256].astype(bf16)
    tail = jnp.concatenate([wide[0:48, 256:320], wide[32:80, 256:320]], axis=1)
    out_ref[160:208, :] = tail.astype(bf16)


def pack_kernel(rank_ref, weights_ref, table_ref, out_ref):
    turned = weights_ref[...].astype(f32).T
    out_ref[0:112, :] = turned[:, 0:128].astype(bf16)
    out_ref[112:224, :] = turned[:, 128:256].astype(bf16)
    block = lax.broadcasted_iota(i32, (ROWS, ROWS), 1)
    row = lax.broadcasted_iota(i32, (ROWS, ROWS), 0)
    named = [table_ref[:, k : k + 1] == block for k in range(KPS)]
    match = jnp.logical_or(named[0], named[1])
    first = jnp.min(jnp.where(match, row, ROWS - 1), axis=0, keepdims=True)
    last = jnp.max(jnp.where(match, row, 0), axis=0, keepdims=True)
    line = lax.broadcasted_iota(i32, (16, ROWS), 0)
    meta = jnp.where(line == 0, first, jnp.where(line == 1, last, 0))
    for s in range(STEPS):
        code = table_ref[:, KPS + s : KPS + s + 1]
        offset = jnp.zeros((ROWS, ROWS), i32)
        for k in range(KPS):
            here = jnp.logical_and(code // BLOCK == rank_ref[0] * KPS + k, named[k])
            offset = jnp.where(here, lax.rem(code, BLOCK) + 1, offset)
        for slot, target in enumerate((first, last)):
            value = jnp.sum(jnp.where(row == target, offset, 0), axis=0, keepdims=True)
            meta = jnp.where(line == 2 + 2 * s + slot, value, meta)
    side = jnp.concatenate([turned[64:112, 256:320], meta.astype(f32)], axis=0)
    out_ref[224:288, :] = jnp.concatenate([turned[0:64, 256:320], side], axis=1).astype(bf16)


def project_kernel(me_ref, x_ref, gain_ref, away_ref, out_ref, meta_ref, pieces_ref, sems):
    copies = [
        pltpu.make_async_copy(away_ref.at[:, z], pieces_ref.at[z], sems.at[z]) for z in range(4)
    ]
    for copy in copies:
        copy.start()
    me = me_ref[0]
    wide = x_ref[...].astype(f32)
    scaled = (wide * gain_ref[...].astype(f32)).astype(bf16)
    scaled = jnp.concatenate([scaled, jnp.zeros((128, 64), bf16)], axis=1)
    lane = lax.broadcasted_iota(i32, (16, 128), 1)
    metas = [jnp.zeros((16, 128), f32), jnp.zeros((16, 128), f32)]
    line = lax.rem(lax.broadcasted_iota(i32, (TP * 8, 128), 0), 8)
    extra = jnp.zeros((TP * 8, 128), f32)
    for z in range(4):
        copies[z].wait()
        pieces = []
        for g in range(8):
            piece = pieces_ref[z, g]
            pieces.append(unpack(piece, 112))
            table = piece[272:288].astype(f32)
            for j in range(2):
                mine = jnp.where(lane == 64 + 2 * me + j, table, 0.0)
                column = jnp.sum(mine, axis=1, keepdims=True)
                metas[j] = jnp.where(lane == 32 + 8 * z + g, column, metas[j])
        table = pieces_ref[z, lax.rem(me, 8)][272:288].astype(f32)
        for slot in range(2):
            extra = jnp.where(line == 2 * z + slot, table[slot : slot + 1], extra)
        part = nt_dot(scaled, jnp.concatenate(pieces, axis=0))
        out_ref[:, z * 896 : (z + 1) * 896] = part.astype(bf16)
    for j in range(2):
        meta_ref[16 * j : 16 * j + 16, :] = metas[j]
    squares = jnp.sum(wide * wide, axis=1, keepdims=True)
    high = squares.astype(bf16).astype(f32)
    low = squares - high
    lane = lax.broadcasted_iota(i32, (TP * 8, 128), 1)
    extra = jnp.where(lane < 64, 0.0, extra)
    extra = jnp.where(lane == 0, high, jnp.where(lane == 1, low, extra))
    out_ref[:, QKV:] = extra.astype(bf16)


def output_kernel(mixed_ref, x_ref, away_ref, rows_ref, packed_ref, weights_ref, sems):
    copies = [
        pltpu.make_async_copy(away_ref.at[:, z], weights_ref.at[z], sems.at[z]) for z in range(4)
    ]
    for copy in copies:
        copy.start()
    part = jnp.zeros((128, 384), f32)
    for z in range(4):
        copies[z].wait()
        weights = []
        for g in range(8):
            piece = weights_ref[z, g]
            tail = piece[160:208]
            other = swap_halves(tail.astype(f32)).astype(bf16)
            tail = jnp.concatenate([tail, other[16:48]], axis=0)
            weights.append(jnp.concatenate([piece[0:80], piece[80:160], tail], axis=1))
        part = part + jnp.dot(
            mixed_ref[:, 640 * z : 640 * z + 640],
            jnp.concatenate(weights, axis=0),
            preferred_element_type=f32,
        )
    rows = (x_ref[...].astype(f32) + part[:, :320]).astype(bf16)
    rows_ref[...] = rows
    packed_ref[0:128, :] = rows[:, 0:128]
    packed_ref[128:256, :] = rows[:, 128:256]
    tail = rows[:, 256:320].astype(f32)
    packed_ref[256:320, :] = jnp.concatenate([tail[0:64], tail[64:128]], axis=1).astype(bf16)


def attend_kernel(parts_ref, cache_ref, lengths_ref, cos_ref, sin_ref, mixed_ref, entry_ref):
    total = parts_ref[0].astype(f32)
    for t in range(1, TP):
        total = total + parts_ref[t].astype(f32)
    squares = total[:, QKV : QKV + 1] + total[:, QKV + 1 : QKV + 2]
    total = total[:, :QKV] * lax.rsqrt(squares / D + epsilon)
    cosine, sine = cos_ref[...], sin_ref[...]

    def head(index):
        return total[:, index * HEAD_SIZE : (index + 1) * HEAD_SIZE]

    def rotated(index):
        vec = head(index)
        swapped = jnp.concatenate([vec[:, HEAD_SIZE // 2 :], vec[:, : HEAD_SIZE // 2]], axis=1)
        return vec * cosine + swapped * sine

    rows = 8 * GROUP
    row = lax.rem(lax.broadcasted_iota(i32, (8, OWN * PLACES), 0), OWN)
    lane = lax.broadcasted_iota(i32, (8, OWN * PLACES), 1)
    old_ok = jnp.logical_and(lane // PLACES == row, lax.rem(lane, PLACES) < lengths_ref[:, :1])
    old_bias = jnp.tile(jnp.where(old_ok, 0.0, -jnp.inf), (GROUP, 1))
    slot = lax.broadcasted_iota(i32, (8, 8), 1)
    fresh = lax.broadcasted_iota(i32, (8, 8), 0)
    new_ok = jnp.logical_and(lax.rem(slot, OWN) == lax.rem(fresh, OWN), slot // OWN <= fresh // OWN)
    new_bias = jnp.tile(jnp.where(new_ok, 0.0, -jnp.inf), (GROUP, 1))
    scale = HEAD_SIZE ** (-0.5)
    width = KEY_VALUE_HEADS * HEAD_SIZE
    for k in range(KEY_VALUE_HEADS):
        at = k * HEAD_SIZE
        new_k = rotated(QUERY_HEADS + k).astype(bf16)
        new_v = head(QUERY_HEADS + KEY_VALUE_HEADS + k).astype(bf16)
        entry_ref[:, at : at + HEAD_SIZE] = new_k
        entry_ref[:, width + at : width + at + HEAD_SIZE] = new_v
        query = jnp.concatenate([rotated(k * GROUP + h) for h in range(GROUP)], axis=0).astype(bf16)
        old_k = cache_ref[:, :, at : at + HEAD_SIZE].reshape(OWN * PLACES, HEAD_SIZE)
        old_v = cache_ref[:, :, width + at : width + at + HEAD_SIZE].reshape(OWN * PLACES, HEAD_SIZE)
        old_s = nt_dot(query, old_k) * scale + old_bias
        new_s = nt_dot(query, new_k) * scale + new_bias
        peak = jnp.maximum(
            jnp.max(old_s, axis=1, keepdims=True), jnp.max(new_s, axis=1, keepdims=True)
        )
        old_e, new_e = jnp.exp(old_s - peak), jnp.exp(new_s - peak)
        whole = jnp.sum(old_e, axis=1, keepdims=True) + jnp.sum(new_e, axis=1, keepdims=True)
        old_w, new_w = (old_e / whole).astype(bf16), (new_e / whole).astype(bf16)
        mixed = jnp.dot(old_w, old_v, preferred_element_type=f32)
        mixed = mixed + jnp.dot(new_w, new_v, preferred_element_type=f32)
        for h in range(GROUP):
            to = (k * GROUP + h) * HEAD_SIZE
            mixed_ref[:, to : to + HEAD_SIZE] = mixed[8 * h : 8 * h + 8].astype(bf16)


def select_kernel(layer_ref, spot_ref, out_ref):
    owners = out_ref.shape[0]
    lane = lax.broadcasted_iota(i32, (16 * owners, 256), 1)
    low = lax.broadcasted_iota(i32, (256, 128), 1) < 64
    tails = jnp.zeros((16 * owners, 128), f32)
    for half in range(2):
        pieces = [layer_ref[2 * half], layer_ref[2 * half + 1]]
        sides = [jnp.concatenate([p[256:], swap_halves(p[256:].astype(f32)).astype(bf16)], axis=0) for p in pieces]
        tail = jnp.concatenate(sides, axis=0).astype(f32)
        if half:
            tail = swap_halves(tail)
        tail = jnp.where(low if half == 0 else jnp.logical_not(low), tail, 0.0).astype(bf16)
        pick = (spot_ref[:, half : half + 1] == lane).astype(f32).astype(bf16)
        for part in range(2):
            rows = jnp.concatenate([p[128 * part : 128 * part + 128] for p in pieces], axis=0)
            taken = jnp.dot(pick, rows, preferred_element_type=f32).astype(bf16)
            at = 32 * part + 16 * half
            out_ref[:, at : at + 16, :] = taken.reshape(owners, 16, 128)
        tails = tails + jnp.dot(pick, tail, preferred_element_type=f32)
    out_ref[:, 64:80, :] = tails.astype(bf16).reshape(owners, 16, 128)


def logits_kernel(gain_ref, offset_ref, away_ref, weights_ref, out_ref, rows_ref, head_ref, sems, sem):
    copies = [
        pltpu.make_async_copy(away_ref.at[:, t], rows_ref.at[t], sems.at[t]) for t in range(TP)
    ]
    for copy in copies:
        copy.start()
    head_copy = pltpu.make_async_copy(weights_ref, head_ref, sem.at[0])
    head_copy.start()

    def piece(t):
        tail = rows_ref[t, :, 64:80, :].reshape(128, 128).astype(f32)
        tail = [tail.reshape(8, 16, 128), swap_halves(tail).reshape(8, 16, 128)]
        parts = [rows_ref[t, :, 0:32, :].reshape(256, 128), rows_ref[t, :, 32:64, :].reshape(256, 128)]
        wide = [p.astype(f32) for p in parts]
        return wide + [jnp.concatenate(tail, axis=1).reshape(256, 128)[:, :64]]

    squares = jnp.zeros((256, 128), f32)
    tails = jnp.zeros((256, 64), f32)
    for t in range(TP):
        copies[t].wait()
        a, b, c = piece(t)
        squares = squares + (a * a + b * b)
        tails = tails + c * c
    total = jnp.sum(squares, axis=1, keepdims=True) + jnp.sum(tails, axis=1, keepdims=True)
    factor = lax.rsqrt(total / D + epsilon)
    head_copy.wait()
    logits = jnp.zeros((256, 2 * BLOCK), f32)
    for t in range(TP):
        at = t * 320
        for value, width in zip(piece(t), (128, 128, 64)):
            normed = (value * factor * gain_ref[:, at : at + width].astype(f32)).astype(bf16)
            weights = head_ref[at : at + width, :]
            logits = logits + jnp.dot(normed, weights, preferred_element_type=f32)
            at += width
    pair = lax.broadcasted_iota(i32, (256, BLOCK), 0)
    logits = jnp.where(lax.rem(pair // 4, 2) == 0, logits[:, :BLOCK], logits[:, BLOCK:])
    token = lax.broadcasted_iota(i32, (BLOCK, 128), 0)
    line = lax.broadcasted_iota(i32, (8, 128), 0)
    for half in range(2):
        side = logits[128 * half : 128 * half + 128].T
        peak = jnp.max(side, axis=0, keepdims=True)
        mass = jnp.sum(jnp.exp(side - peak), axis=0, keepdims=True)
        target = offset_ref[:, 128 * half : 128 * half + 128] - 1
        picked = jnp.sum(jnp.where(token == target, side, 0.0), axis=0, keepdims=True)
        out = jnp.where(line == 0, peak, jnp.where(line == 1, mass, picked))
        out_ref[:, 128 * half : 128 * half + 128] = out


def rows_kernel(stats_ref, row_ref, out_ref):
    mine = lax.broadcasted_iota(i32, (ROWS, GEN), 0)
    lane = lax.broadcasted_iota(i32, (ROWS, 128), 1)
    out = jnp.zeros((ROWS, 128), f32)
    for s in range(STEPS):
        best = jnp.full((ROWS, 1), -jnp.inf, f32)
        combos = [(j, slot) for j in range(2) for slot in range(2)]
        masks = [row_ref[2 * j + slot : 2 * j + slot + 1, :] == mine for j, slot in combos]

        def stat(which, j, slot):
            at = which * 8 + j * 4 + slot * 2 + s
            return stats_ref[at : at + 1, :]

        for mask, (j, slot) in zip(masks, combos):
            peak = jnp.where(mask, stat(0, j, slot), -jnp.inf)
            best = jnp.maximum(best, jnp.max(peak, axis=1, keepdims=True))
        mass = jnp.zeros((ROWS, 1), f32)
        picked = jnp.zeros((ROWS, 1), f32)
        for mask, (j, slot) in zip(masks, combos):
            grown = stat(1, j, slot) * jnp.exp(jnp.where(mask, stat(0, j, slot), best) - best)
            mass = mass + jnp.sum(jnp.where(mask, grown, 0.0), axis=1, keepdims=True)
            picked = picked + jnp.sum(
                jnp.where(mask, stat(2, j, slot), 0.0), axis=1, keepdims=True
            )
        for at, value in enumerate((best, mass, picked)):
            out = jnp.where(lane == 3 * s + at, value, out)
    out_ref[...] = out


def gen_index(z, x, core):
    return (z * 4 + x) * 2 + core


Z_GROUPS = [[gen_index(z, x, c) for z in range(4)] for x in range(4) for c in range(2)]


LAYERS = [[z * 128 + i for i in range(128)] for z in range(4)]


XC_GROUPS = [[z * 8 + i for i in range(8)] for z in range(4)]


def all_to_all(value, axis, groups=None):
    return lax.all_to_all(
        value, axis, split_axis=0, concat_axis=0, tiled=True, axis_index_groups=groups
    )


def spread(value, axis, count, groups=None):
    return all_to_all(jnp.broadcast_to(value[None], (count,) + value.shape), axis, groups)


def rotary_tables(lengths):
    half = HEAD_SIZE // 2
    exponent = jnp.arange(half, dtype=f32) * (2.0 / HEAD_SIZE)
    inverse = jnp.power(f32(rope_base), -exponent)
    positions = (jnp.arange(STEPS, dtype=i32)[:, None] + lengths[None, :]).reshape(-1)
    angles = positions.astype(f32)[:, None] * inverse[None, :]
    cosine, sine = jnp.cos(angles), jnp.sin(angles)
    return (
        jnp.concatenate([cosine, cosine], axis=1),
        jnp.concatenate([-sine, sine], axis=1),
    )


def row_table(kept):
    row = jnp.arange(ROWS, dtype=i32)[:, None]
    match = jnp.any(kept[:, :, None] == jnp.arange(ROWS, dtype=i32), axis=1)
    first = jnp.min(jnp.where(match, row, ROWS - 1), axis=0)
    last = jnp.max(jnp.where(match, row, 0), axis=0)
    return jnp.stack([first, last], axis=1)


def body(embeddings, cache, lengths, attn_gain, wqkv, wout, final_gain, head, kept, chosen):
    rank = lax.axis_index("tp").astype(i32)
    me = lax.axis_index("gen").astype(i32)
    features = D // TP

    table = jnp.concatenate([kept[0], chosen.T], axis=1)
    piece = call(
        pack_kernel, shape((288, 128), bf16), rank.reshape(1), wqkv, table, scalars=1
    )
    along_z = spread(piece, "gen", 4, Z_GROUPS)
    out_piece = call(pack_out_kernel, shape((208, 128), bf16), wout)
    along_z, out_piece = lax.optimization_barrier((along_z, out_piece))
    pieces = lax.all_gather(along_z, "gen", axis_index_groups=XC_GROUPS)
    out_along_z = spread(out_piece, "gen", 4, Z_GROUPS)
    pieces, out_along_z = lax.optimization_barrier((pieces, out_along_z))
    out_whole = lax.all_gather(out_along_z, "gen", axis_index_groups=XC_GROUPS)

    x = embeddings.reshape(STEPS, TP, OWN, features).transpose(1, 0, 2, 3).reshape(128, features)
    parts, meta = call(
        project_kernel,
        (shape((128, QKV + 128), bf16), shape((32, 128), f32)),
        me.reshape(1),
        x,
        attn_gain.reshape(1, features),
        pieces,
        scalars=1,
        away=1,
        scratch=[pltpu.VMEM((4, 8, 288, 128), bf16), pltpu.SemaphoreType.DMA((4,))],
        vmem=59,
    )
    parts = all_to_all(parts.reshape(TP, 8, QKV + 128), "tp")

    meta = meta.reshape(2, 16, 128)[:, :6, 32:64].astype(i32).reshape(2, 3, 2, GEN)
    offset = meta[:, 1:].reshape(2, 2, 2, 4, 8).transpose(4, 3, 0, 2, 1).reshape(1, 256)
    routes = lax.dynamic_slice_in_dim(parts[:, :, QKV + 64 :], me // 8 * 16, 16, 2)
    row = routes.astype(f32).astype(i32).reshape(TP, 2, 2, 2, 8, 2).transpose(4, 0, 2, 5, 3, 1)
    spot = jnp.arange(2, dtype=i32)[:, None, None, None] * 128 + row // OWN * 8 + row % OWN
    spot = spot[:, :, :, :, :, None, :] + jnp.arange(STEPS, dtype=i32)[:, None] * OWN
    spot = spot.reshape(16 * 128, 2)

    cosine, sine = rotary_tables(lengths)
    wide_lengths = jnp.broadcast_to(jnp.tile(lengths, STEPS)[:, None], (8, 128))
    mixed, entries = call(
        attend_kernel,
        (shape((8, QUERY_HEADS * HEAD_SIZE), bf16), shape((8, 1024), bf16)),
        parts,
        cache,
        wide_lengths,
        cosine,
        sine,
    )
    mixed = spread(mixed, "tp", TP).reshape(128, QUERY_HEADS * HEAD_SIZE)
    layer_out, packed = call(
        output_kernel,
        (shape((128, features), bf16), shape((320, 128), bf16)),
        mixed,
        x,
        out_whole,
        away=1,
        scratch=[pltpu.VMEM((4, 8, 208, 128), bf16), pltpu.SemaphoreType.DMA((4,))],
        vmem=59,
    )
    last_hidden = layer_out.reshape(TP, STEPS, OWN, features)[:, -1].reshape(ROWS, features)

    layers = spread(packed, "gen", 4, Z_GROUPS)
    taken = call(select_kernel, shape((128, 80, 128), bf16), layers, spot)
    taken = all_to_all(taken, ("gen", "tp"), LAYERS).reshape(8, TP, 80, 128)
    stats = call(
        logits_kernel,
        shape((8, 256), f32),
        final_gain.reshape(1, D),
        offset,
        taken,
        head,
        away=2,
        scratch=[
            pltpu.VMEM((TP, 8, 80, 128), bf16),
            pltpu.VMEM((D, 2 * BLOCK), bf16),
            pltpu.SemaphoreType.DMA((TP,)),
            pltpu.SemaphoreType.DMA((1,)),
        ],
        vmem=57,
    )
    stats = stats[:3].reshape(3, 8, 4, 8).transpose(2, 1, 0, 3).reshape(GEN, 1, 24)
    stats = all_to_all(stats, "gen").reshape(GEN, 24).T
    rows_of = row_table(kept[0]).reshape(GEN, 4).T
    row_stats = call(rows_kernel, shape((ROWS, 128), f32), stats, rows_of)
    row_stats = all_to_all(row_stats.reshape(TP, OWN, 128)[:, :, :8], "tp")
    peak, mass, picked = (row_stats[:, :, i : 3 * STEPS : 3] for i in range(3))
    best = jnp.max(peak, axis=0)
    mass = jnp.sum(mass * jnp.exp(peak - best), axis=0)
    logprobs = jnp.sum(picked, axis=0) - best - jnp.log(mass)
    return logprobs.T, last_hidden, entries.reshape(STEPS, OWN, 1024)


def solution(mesh):
    return jax.shard_map(
        body,
        mesh=mesh,
        in_specs=(
            P(None, "gen", "tp"),
            P(("gen", "tp"), None, None),
            P(("gen", "tp")),
            P("tp"),
            P("tp", "gen"),
            P("gen", "tp"),
            P(),
            P(None, ("gen", "tp")),
            P("tp", "gen", None),
            P(None, "gen"),
        ),
        out_specs=(P(None, ("gen", "tp")), P("gen", "tp"), P(None, ("gen", "tp"), None)),
        check_vma=False,
    )
```

```python
import jax
import jax.numpy as jnp
from jax import lax
from jax.experimental import pallas as pl
from jax.experimental.pallas import tpu as pltpu
from jax.sharding import PartitionSpec as P

D = 5120
QUERY_HEADS = 20
KEY_VALUE_HEADS = 4
GROUP = QUERY_HEADS // KEY_VALUE_HEADS
HEAD_SIZE = 128
BLOCK = 128
KPS = 2
STEPS = 2
QKV = 3584
GEN = 32
TP = 16
ROWS = 64
OWN = ROWS // TP
PLACES = 128

epsilon = 1e-06
rope_base = 1000000.0

bf16 = jnp.bfloat16
f32 = jnp.float32
i32 = jnp.int32
VMEM_BYTES = 48 * 1024 * 1024


def call(kernel, out_shape, *args, scalars=0, scratch=()):
    specs = [pl.BlockSpec(memory_space=pltpu.SMEM)] * scalars
    specs += [pl.BlockSpec(memory_space=pltpu.VMEM)] * (len(args) - scalars)
    return pl.pallas_call(
        kernel,
        out_shape=out_shape,
        in_specs=specs,
        out_specs=jax.tree.map(lambda _: pl.BlockSpec(memory_space=pltpu.VMEM), out_shape),
        scratch_shapes=list(scratch),
        compiler_params=pltpu.CompilerParams(vmem_limit_bytes=VMEM_BYTES),
    )(*args)


def shape(dims, dtype):
    return jax.ShapeDtypeStruct(dims, dtype)


def nt_dot(a, b):
    return lax.dot_general(a, b, (((1,), (1,)), ((), ())), preferred_element_type=f32)


def swap_halves(value):
    return jnp.concatenate([value[:, 64:], value[:, :64]], axis=1)


def unpack(piece, rows):
    tail = piece[2 * rows :]
    other = swap_halves(tail.astype(f32)).astype(bf16)
    tail = jnp.concatenate([tail, other[: rows - 64]], axis=0)
    return jnp.concatenate([piece[:rows], piece[rows : 2 * rows], tail], axis=1)


def pack_kernel(rank_ref, weights_ref, table_ref, wout_ref, copies_ref):
    out_ref = copies_ref.at[0]
    wide = wout_ref[...].astype(f32)
    out_ref[288:368, :] = wide[:, 0:128].astype(bf16)
    out_ref[368:448, :] = wide[:, 128:256].astype(bf16)
    tail = jnp.concatenate([wide[0:48, 256:320], wide[32:80, 256:320]], axis=1)
    out_ref[448:496, :] = tail.astype(bf16)
    turned = weights_ref[...].astype(f32).T
    out_ref[0:112, :] = turned[:, 0:128].astype(bf16)
    out_ref[112:224, :] = turned[:, 128:256].astype(bf16)
    block = lax.broadcasted_iota(i32, (ROWS, ROWS), 1)
    row = lax.broadcasted_iota(i32, (ROWS, ROWS), 0)
    named = [table_ref[:, k : k + 1] == block for k in range(KPS)]
    match = jnp.logical_or(named[0], named[1])
    first = jnp.min(jnp.where(match, row, ROWS - 1), axis=0, keepdims=True)
    last = jnp.max(jnp.where(match, row, 0), axis=0, keepdims=True)
    line = lax.broadcasted_iota(i32, (16, ROWS), 0)
    meta = jnp.where(line == 0, first, jnp.where(line == 1, last, 0))
    for s in range(STEPS):
        code = table_ref[:, KPS + s : KPS + s + 1]
        offset = jnp.zeros((ROWS, ROWS), i32)
        for k in range(KPS):
            here = jnp.logical_and(code // BLOCK == rank_ref[0] * KPS + k, named[k])
            offset = jnp.where(here, lax.rem(code, BLOCK) + 1, offset)
        for slot, target in enumerate((first, last)):
            value = jnp.sum(jnp.where(row == target, offset, 0), axis=0, keepdims=True)
            meta = jnp.where(line == 2 + 2 * s + slot, value, meta)
    side = jnp.concatenate([turned[64:112, 256:320], meta.astype(f32)], axis=0)
    out_ref[224:288, :] = jnp.concatenate([turned[0:64, 256:320], side], axis=1).astype(bf16)
    for z in range(1, 4):
        copies_ref[z] = copies_ref[0]


def project_kernel(me_ref, x_ref, gain_ref, own_ref, other_ref, out_ref, meta_ref):
    me = me_ref[0]
    core = lax.rem(me, 2)
    wide = x_ref[...].astype(f32)
    scaled = (wide * gain_ref[...].astype(f32)).astype(bf16)
    scaled = jnp.concatenate([scaled, jnp.zeros((128, 64), bf16)], axis=1)
    lane = lax.broadcasted_iota(i32, (16, 128), 1)
    metas = [jnp.zeros((16, 128), f32), jnp.zeros((16, 128), f32)]
    line = lax.rem(lax.broadcasted_iota(i32, (TP * 8, 128), 0), 8)
    extra = jnp.zeros((TP * 8, 128), f32)
    for z in range(4):
        pieces = []
        for x in range(4):
            a = own_ref[x * 4 + z]
            b = other_ref[x * 4 + z]
            for c, piece in enumerate((jnp.where(core == 0, a, b), jnp.where(core == 0, b, a))):
                pieces.append(unpack(piece, 112))
                table = piece[272:288].astype(f32)
                for j in range(2):
                    mine = jnp.where(lane == 64 + 2 * me + j, table, 0.0)
                    column = jnp.sum(mine, axis=1, keepdims=True)
                    at = 32 + gen_index(z, x, c)
                    metas[j] = jnp.where(lane == at, column, metas[j])
        table = own_ref[lax.rem(me // 2, 4) * 4 + z][272:288].astype(f32)
        for slot in range(2):
            extra = jnp.where(line == 2 * z + slot, table[slot : slot + 1], extra)
        part = nt_dot(scaled, jnp.concatenate(pieces, axis=0))
        out_ref[:, z * 896 : (z + 1) * 896] = part.astype(bf16)
    for j in range(2):
        meta_ref[16 * j : 16 * j + 16, :] = metas[j]
    squares = jnp.sum(wide * wide, axis=1, keepdims=True)
    high = squares.astype(bf16).astype(f32)
    low = squares - high
    lane = lax.broadcasted_iota(i32, (TP * 8, 128), 1)
    extra = jnp.where(lane < 64, 0.0, extra)
    extra = jnp.where(lane == 0, high, jnp.where(lane == 1, low, extra))
    out_ref[:, QKV:] = extra.astype(bf16)


def output_kernel(mixed_ref, weights_ref, x_ref, rows_ref, packed_ref):
    part = jnp.zeros((128, 384), f32)
    for z in range(4):
        weights = []
        for g in range(8):
            piece = weights_ref[g, z]
            tail = piece[160:208]
            other = swap_halves(tail.astype(f32)).astype(bf16)
            tail = jnp.concatenate([tail, other[16:48]], axis=0)
            weights.append(jnp.concatenate([piece[0:80], piece[80:160], tail], axis=1))
        part = part + jnp.dot(
            mixed_ref[:, 640 * z : 640 * z + 640],
            jnp.concatenate(weights, axis=0),
            preferred_element_type=f32,
        )
    rows = (x_ref[...].astype(f32) + part[:, :320]).astype(bf16)
    rows_ref[...] = rows
    tail = rows[:, 256:320].astype(f32)
    tail = jnp.concatenate([tail[0:64], tail[64:128]], axis=1).astype(bf16)
    for z in range(4):
        packed_ref[z, 0:128, :] = rows[:, 0:128]
        packed_ref[z, 128:256, :] = rows[:, 128:256]
        packed_ref[z, 256:320, :] = tail


def attend_kernel(parts_ref, cache_ref, lengths_ref, cos_ref, sin_ref, mixed_ref, entry_ref):
    total = parts_ref[0].astype(f32)
    for t in range(1, TP):
        total = total + parts_ref[t].astype(f32)
    squares = total[:, QKV : QKV + 1] + total[:, QKV + 1 : QKV + 2]
    total = total[:, :QKV] * lax.rsqrt(squares / D + epsilon)
    cosine, sine = cos_ref[...], sin_ref[...]

    def head(index):
        return total[:, index * HEAD_SIZE : (index + 1) * HEAD_SIZE]

    def rotated(index):
        vec = head(index)
        swapped = jnp.concatenate([vec[:, HEAD_SIZE // 2 :], vec[:, : HEAD_SIZE // 2]], axis=1)
        return vec * cosine + swapped * sine

    rows = 8 * GROUP
    row = lax.rem(lax.broadcasted_iota(i32, (8, OWN * PLACES), 0), OWN)
    lane = lax.broadcasted_iota(i32, (8, OWN * PLACES), 1)
    old_ok = jnp.logical_and(lane // PLACES == row, lax.rem(lane, PLACES) < lengths_ref[:, :1])
    old_bias = jnp.tile(jnp.where(old_ok, 0.0, -jnp.inf), (GROUP, 1))
    slot = lax.broadcasted_iota(i32, (8, 8), 1)
    fresh = lax.broadcasted_iota(i32, (8, 8), 0)
    new_ok = jnp.logical_and(lax.rem(slot, OWN) == lax.rem(fresh, OWN), slot // OWN <= fresh // OWN)
    new_bias = jnp.tile(jnp.where(new_ok, 0.0, -jnp.inf), (GROUP, 1))
    scale = HEAD_SIZE ** (-0.5)
    width = KEY_VALUE_HEADS * HEAD_SIZE
    for k in range(KEY_VALUE_HEADS):
        at = k * HEAD_SIZE
        new_k = rotated(QUERY_HEADS + k).astype(bf16)
        new_v = head(QUERY_HEADS + KEY_VALUE_HEADS + k).astype(bf16)
        entry_ref[:, at : at + HEAD_SIZE] = new_k
        entry_ref[:, width + at : width + at + HEAD_SIZE] = new_v
        query = jnp.concatenate([rotated(k * GROUP + h) for h in range(GROUP)], axis=0).astype(bf16)
        old_k = cache_ref[:, :, at : at + HEAD_SIZE].reshape(OWN * PLACES, HEAD_SIZE)
        old_v = cache_ref[:, :, width + at : width + at + HEAD_SIZE].reshape(OWN * PLACES, HEAD_SIZE)
        old_s = nt_dot(query, old_k) * scale + old_bias
        new_s = nt_dot(query, new_k) * scale + new_bias
        peak = jnp.maximum(
            jnp.max(old_s, axis=1, keepdims=True), jnp.max(new_s, axis=1, keepdims=True)
        )
        old_e, new_e = jnp.exp(old_s - peak), jnp.exp(new_s - peak)
        whole = jnp.sum(old_e, axis=1, keepdims=True) + jnp.sum(new_e, axis=1, keepdims=True)
        old_w, new_w = (old_e / whole).astype(bf16), (new_e / whole).astype(bf16)
        mixed = jnp.dot(old_w, old_v, preferred_element_type=f32)
        mixed = mixed + jnp.dot(new_w, new_v, preferred_element_type=f32)
        for h in range(GROUP):
            to = (k * GROUP + h) * HEAD_SIZE
            part = mixed[8 * h : 8 * h + 8].astype(bf16)
            for t in range(TP):
                mixed_ref[t, :, to : to + HEAD_SIZE] = part


def select_kernel(layer_ref, spot_ref, out_ref):
    owners = out_ref.shape[0]
    lane = lax.broadcasted_iota(i32, (16 * owners, 256), 1)
    low = lax.broadcasted_iota(i32, (256, 128), 1) < 64
    tails = jnp.zeros((16 * owners, 128), f32)
    for half in range(2):
        pieces = [layer_ref[2 * half], layer_ref[2 * half + 1]]
        sides = [jnp.concatenate([p[256:], swap_halves(p[256:].astype(f32)).astype(bf16)], axis=0) for p in pieces]
        tail = jnp.concatenate(sides, axis=0).astype(f32)
        if half:
            tail = swap_halves(tail)
        tail = jnp.where(low if half == 0 else jnp.logical_not(low), tail, 0.0).astype(bf16)
        pick = (spot_ref[:, half : half + 1] == lane).astype(f32).astype(bf16)
        for part in range(2):
            rows = jnp.concatenate([p[128 * part : 128 * part + 128] for p in pieces], axis=0)
            taken = jnp.dot(pick, rows, preferred_element_type=f32).astype(bf16)
            at = 32 * part + 16 * half
            out_ref[:, at : at + 16, :] = taken.reshape(owners, 16, 128)
        tails = tails + jnp.dot(pick, tail, preferred_element_type=f32)
    out_ref[:, 64:80, :] = tails.astype(bf16).reshape(owners, 16, 128)


def logits_kernel(rows_ref, gain_ref, head_ref, offset_ref, out_ref):
    def piece(t):
        tail = rows_ref[:, t, 64:80, :].reshape(128, 128).astype(f32)
        tail = [tail.reshape(8, 16, 128), swap_halves(tail).reshape(8, 16, 128)]
        parts = [rows_ref[:, t, 0:32, :].reshape(256, 128), rows_ref[:, t, 32:64, :].reshape(256, 128)]
        wide = [p.astype(f32) for p in parts]
        return wide + [jnp.concatenate(tail, axis=1).reshape(256, 128)[:, :64]]

    squares = jnp.zeros((256, 128), f32)
    tails = jnp.zeros((256, 64), f32)
    for t in range(TP):
        a, b, c = piece(t)
        squares = squares + (a * a + b * b)
        tails = tails + c * c
    total = jnp.sum(squares, axis=1, keepdims=True) + jnp.sum(tails, axis=1, keepdims=True)
    factor = lax.rsqrt(total / D + epsilon)
    logits = jnp.zeros((256, 2 * BLOCK), f32)
    for t in range(TP):
        at = t * 320
        for value, width in zip(piece(t), (128, 128, 64)):
            normed = (value * factor * gain_ref[:, at : at + width].astype(f32)).astype(bf16)
            weights = head_ref[at : at + width, :]
            logits = logits + jnp.dot(normed, weights, preferred_element_type=f32)
            at += width
    pair = lax.broadcasted_iota(i32, (256, BLOCK), 0)
    logits = jnp.where(lax.rem(pair // 4, 2) == 0, logits[:, :BLOCK], logits[:, BLOCK:])
    token = lax.broadcasted_iota(i32, (BLOCK, 128), 0)
    line = lax.broadcasted_iota(i32, (8, 128), 0)
    for half in range(2):
        side = logits[128 * half : 128 * half + 128].T
        peak = jnp.max(side, axis=0, keepdims=True)
        mass = jnp.sum(jnp.exp(side - peak), axis=0, keepdims=True)
        target = offset_ref[:, 128 * half : 128 * half + 128] - 1
        picked = jnp.sum(jnp.where(token == target, side, 0.0), axis=0, keepdims=True)
        out = jnp.where(line == 0, peak, jnp.where(line == 1, mass, picked))
        out_ref[:, 128 * half : 128 * half + 128] = out


def rows_kernel(stats_ref, row_ref, out_ref):
    mine = lax.broadcasted_iota(i32, (ROWS, GEN), 0)
    lane = lax.broadcasted_iota(i32, (ROWS, 128), 1)
    out = jnp.zeros((ROWS, 128), f32)
    for s in range(STEPS):
        best = jnp.full((ROWS, 1), -jnp.inf, f32)
        combos = [(j, slot) for j in range(2) for slot in range(2)]
        masks = [row_ref[2 * j + slot : 2 * j + slot + 1, :] == mine for j, slot in combos]

        def stat(which, j, slot):
            at = which * 8 + j * 4 + slot * 2 + s
            return stats_ref[at : at + 1, :]

        for mask, (j, slot) in zip(masks, combos):
            peak = jnp.where(mask, stat(0, j, slot), -jnp.inf)
            best = jnp.maximum(best, jnp.max(peak, axis=1, keepdims=True))
        mass = jnp.zeros((ROWS, 1), f32)
        picked = jnp.zeros((ROWS, 1), f32)
        for mask, (j, slot) in zip(masks, combos):
            grown = stat(1, j, slot) * jnp.exp(jnp.where(mask, stat(0, j, slot), best) - best)
            mass = mass + jnp.sum(jnp.where(mask, grown, 0.0), axis=1, keepdims=True)
            picked = picked + jnp.sum(
                jnp.where(mask, stat(2, j, slot), 0.0), axis=1, keepdims=True
            )
        for at, value in enumerate((best, mass, picked)):
            out = jnp.where(lane == 3 * s + at, value, out)
    out_ref[...] = out


def gen_index(z, x, core):
    return (z * 4 + x) * 2 + core


Z_GROUPS = [[gen_index(z, x, c) for z in range(4)] for x in range(4) for c in range(2)]
X_GROUPS = [[gen_index(z, x, c) for x in range(4)] for z in range(4) for c in range(2)]


LAYERS = [[z * 128 + i for i in range(128)] for z in range(4)]


XC_GROUPS = [[z * 8 + i for i in range(8)] for z in range(4)]


def all_to_all(value, axis, groups=None):
    return lax.all_to_all(
        value, axis, split_axis=0, concat_axis=0, tiled=True, axis_index_groups=groups
    )


def spread(value, axis, count, groups=None):
    return all_to_all(jnp.broadcast_to(value[None], (count,) + value.shape), axis, groups)


def rotary_tables(lengths):
    half = HEAD_SIZE // 2
    exponent = jnp.arange(half, dtype=f32) * (2.0 / HEAD_SIZE)
    inverse = jnp.power(f32(rope_base), -exponent)
    positions = (jnp.arange(STEPS, dtype=i32)[:, None] + lengths[None, :]).reshape(-1)
    angles = positions.astype(f32)[:, None] * inverse[None, :]
    cosine, sine = jnp.cos(angles), jnp.sin(angles)
    return (
        jnp.concatenate([cosine, cosine], axis=1),
        jnp.concatenate([-sine, sine], axis=1),
    )


def row_table(kept):
    row = jnp.arange(ROWS, dtype=i32)[:, None]
    match = jnp.any(kept[:, :, None] == jnp.arange(ROWS, dtype=i32), axis=1)
    first = jnp.min(jnp.where(match, row, ROWS - 1), axis=0)
    last = jnp.max(jnp.where(match, row, 0), axis=0)
    return jnp.stack([first, last], axis=1)


def body(embeddings, cache, lengths, attn_gain, wqkv, wout, final_gain, head, kept, chosen):
    rank = lax.axis_index("tp").astype(i32)
    me = lax.axis_index("gen").astype(i32)
    features = D // TP

    table = jnp.concatenate([kept[0], chosen.T], axis=1)
    piece = call(
        pack_kernel, shape((4, 496, 128), bf16), rank.reshape(1), wqkv, table, wout, scalars=1
    )
    along_z = all_to_all(piece, "gen", Z_GROUPS)
    out_whole = lax.all_gather(along_z[:, 288:], "gen", axis_index_groups=XC_GROUPS)
    own_w = spread(along_z[:, :288], "gen", 4, X_GROUPS).reshape(16, 288, 128)
    other_w = lax.ppermute(own_w, "gen", [(g, g ^ 1) for g in range(GEN)])

    x = embeddings.reshape(STEPS, TP, OWN, features).transpose(1, 0, 2, 3).reshape(128, features)
    parts, meta = call(
        project_kernel,
        (shape((128, QKV + 128), bf16), shape((32, 128), f32)),
        me.reshape(1),
        x,
        attn_gain.reshape(1, features),
        own_w,
        other_w,
        scalars=1,
    )
    parts = all_to_all(parts.reshape(TP, 8, QKV + 128), "tp")

    meta = meta.reshape(2, 16, 128)[:, :6, 32:64].astype(i32).reshape(2, 3, 2, GEN)
    offset = meta[:, 1:].reshape(2, 2, 2, 4, 8).transpose(4, 3, 0, 2, 1).reshape(1, 256)
    routes = lax.dynamic_slice_in_dim(parts[:, :, QKV + 64 :], me // 8 * 16, 16, 2)
    row = routes.astype(f32).astype(i32).reshape(TP, 2, 2, 2, 8, 2).transpose(4, 0, 2, 5, 3, 1)
    spot = jnp.arange(2, dtype=i32)[:, None, None, None] * 128 + row // OWN * 8 + row % OWN
    spot = spot[:, :, :, :, :, None, :] + jnp.arange(STEPS, dtype=i32)[:, None] * OWN
    spot = spot.reshape(16 * 128, 2)

    cosine, sine = rotary_tables(lengths)
    wide_lengths = jnp.broadcast_to(jnp.tile(lengths, STEPS)[:, None], (8, 128))
    mixed, entries = call(
        attend_kernel,
        (shape((TP, 8, QUERY_HEADS * HEAD_SIZE), bf16), shape((8, 1024), bf16)),
        parts,
        cache,
        wide_lengths,
        cosine,
        sine,
    )
    mixed = all_to_all(mixed, "tp").reshape(128, QUERY_HEADS * HEAD_SIZE)
    layer_out, packed = call(
        output_kernel,
        (shape((128, features), bf16), shape((4, 320, 128), bf16)),
        mixed,
        out_whole,
        x,
    )
    last_hidden = layer_out.reshape(TP, STEPS, OWN, features)[:, -1].reshape(ROWS, features)

    layers = all_to_all(packed, "gen", Z_GROUPS)
    taken = call(select_kernel, shape((128, 80, 128), bf16), layers, spot)
    taken = all_to_all(taken, ("gen", "tp"), LAYERS).reshape(8, TP, 80, 128)
    stats = call(
        logits_kernel,
        shape((8, 256), f32),
        taken,
        final_gain.reshape(1, D),
        head,
        offset,
    )
    stats = stats[:3].reshape(3, 8, 4, 8).transpose(2, 1, 0, 3).reshape(GEN, 1, 24)
    stats = all_to_all(stats, "gen").reshape(GEN, 24).T
    rows_of = row_table(kept[0]).reshape(GEN, 4).T
    row_stats = call(rows_kernel, shape((ROWS, 128), f32), stats, rows_of)
    row_stats = all_to_all(row_stats.reshape(TP, OWN, 128)[:, :, :8], "tp")
    peak, mass, picked = (row_stats[:, :, i : 3 * STEPS : 3] for i in range(3))
    best = jnp.max(peak, axis=0)
    mass = jnp.sum(mass * jnp.exp(peak - best), axis=0)
    logprobs = jnp.sum(picked, axis=0) - best - jnp.log(mass)
    return logprobs.T, last_hidden, entries.reshape(STEPS, OWN, 1024)


def solution(mesh):
    return jax.shard_map(
        body,
        mesh=mesh,
        in_specs=(
            P(None, "gen", "tp"),
            P(("gen", "tp"), None, None),
            P(("gen", "tp")),
            P("tp"),
            P("tp", "gen"),
            P("gen", "tp"),
            P(),
            P(None, ("gen", "tp")),
            P("tp", "gen", None),
            P(None, "gen"),
        ),
        out_specs=(P(None, ("gen", "tp")), P("gen", "tp"), P(None, ("gen", "tp"), None)),
        check_vma=False,
    )
```

```python
import jax
import jax.numpy as jnp
from jax import lax
from jax.experimental import pallas as pl
from jax.experimental.pallas import tpu as pltpu
from jax.sharding import PartitionSpec as P

D = 5120
QUERY_HEADS = 20
KEY_VALUE_HEADS = 4
GROUP = QUERY_HEADS // KEY_VALUE_HEADS
HEAD_SIZE = 128
BLOCK = 128
KPS = 2
STEPS = 2
QKV = 3584
GEN = 32
TP = 16
ROWS = 64
OWN = ROWS // TP
PLACES = 128

epsilon = 1e-06
rope_base = 1000000.0

bf16 = jnp.bfloat16
f32 = jnp.float32
i32 = jnp.int32
VMEM_BYTES = 48 * 1024 * 1024


def call(kernel, out_shape, *args, scalars=0, scratch=()):
    specs = [pl.BlockSpec(memory_space=pltpu.SMEM)] * scalars
    specs += [pl.BlockSpec(memory_space=pltpu.VMEM)] * (len(args) - scalars)
    return pl.pallas_call(
        kernel,
        out_shape=out_shape,
        in_specs=specs,
        out_specs=jax.tree.map(lambda _: pl.BlockSpec(memory_space=pltpu.VMEM), out_shape),
        scratch_shapes=list(scratch),
        compiler_params=pltpu.CompilerParams(vmem_limit_bytes=VMEM_BYTES),
    )(*args)


def shape(dims, dtype):
    return jax.ShapeDtypeStruct(dims, dtype)


def nt_dot(a, b):
    return lax.dot_general(a, b, (((1,), (1,)), ((), ())), preferred_element_type=f32)


def swap_halves(value):
    return jnp.concatenate([value[:, 64:], value[:, :64]], axis=1)


def unpack(piece, rows):
    tail = piece[2 * rows :]
    other = swap_halves(tail.astype(f32)).astype(bf16)
    tail = jnp.concatenate([tail, other[: rows - 64]], axis=0)
    return jnp.concatenate([piece[:rows], piece[rows : 2 * rows], tail], axis=1)


def pack_kernel(rank_ref, weights_ref, table_ref, wout_ref, copies_ref):
    out_ref = copies_ref.at[0]
    wide = wout_ref[...].astype(f32)
    out_ref[288:368, :] = wide[:, 0:128].astype(bf16)
    out_ref[368:448, :] = wide[:, 128:256].astype(bf16)
    tail = jnp.concatenate([wide[0:48, 256:320], wide[32:80, 256:320]], axis=1)
    out_ref[448:496, :] = tail.astype(bf16)
    turned = weights_ref[...].astype(f32).T
    out_ref[0:112, :] = turned[:, 0:128].astype(bf16)
    out_ref[112:224, :] = turned[:, 128:256].astype(bf16)
    block = lax.broadcasted_iota(i32, (ROWS, ROWS), 1)
    row = lax.broadcasted_iota(i32, (ROWS, ROWS), 0)
    named = [table_ref[:, k : k + 1] == block for k in range(KPS)]
    match = jnp.logical_or(named[0], named[1])
    first = jnp.min(jnp.where(match, row, ROWS - 1), axis=0, keepdims=True)
    last = jnp.max(jnp.where(match, row, 0), axis=0, keepdims=True)
    line = lax.broadcasted_iota(i32, (16, ROWS), 0)
    meta = jnp.where(line == 0, first, jnp.where(line == 1, last, 0))
    for s in range(STEPS):
        code = table_ref[:, KPS + s : KPS + s + 1]
        offset = jnp.zeros((ROWS, ROWS), i32)
        for k in range(KPS):
            here = jnp.logical_and(code // BLOCK == rank_ref[0] * KPS + k, named[k])
            offset = jnp.where(here, lax.rem(code, BLOCK) + 1, offset)
        for slot, target in enumerate((first, last)):
            value = jnp.sum(jnp.where(row == target, offset, 0), axis=0, keepdims=True)
            meta = jnp.where(line == 2 + 2 * s + slot, value, meta)
    side = jnp.concatenate([turned[64:112, 256:320], meta.astype(f32)], axis=0)
    out_ref[224:288, :] = jnp.concatenate([turned[0:64, 256:320], side], axis=1).astype(bf16)
    for z in range(1, 4):
        copies_ref[z] = copies_ref[0]


def project_kernel(me_ref, x_ref, gain_ref, own_ref, other_ref, late_ref, out_ref, meta_ref):
    me = me_ref[0]
    core = lax.rem(me, 2)
    wide = x_ref[...].astype(f32)
    scaled = (wide * gain_ref[...].astype(f32)).astype(bf16)
    scaled = jnp.concatenate([scaled, jnp.zeros((128, 64), bf16)], axis=1)
    lane = lax.broadcasted_iota(i32, (16, 128), 1)
    metas = [jnp.zeros((16, 128), f32), jnp.zeros((16, 128), f32)]
    line = lax.rem(lax.broadcasted_iota(i32, (TP * 8, 128), 0), 8)
    extra = jnp.zeros((TP * 8, 128), f32)
    for z in range(4):
        pieces = []
        for x in range(4):
            a = own_ref[x * 4 + z]
            b = other_ref[x * 4 + z]
            for c, piece in enumerate((jnp.where(core == 0, a, b), jnp.where(core == 0, b, a))):
                piece = jnp.concatenate([piece, late_ref[2 * x + c, z]], axis=0)
                pieces.append(unpack(piece, 112))
                table = piece[272:288].astype(f32)
                for j in range(2):
                    mine = jnp.where(lane == 64 + 2 * me + j, table, 0.0)
                    column = jnp.sum(mine, axis=1, keepdims=True)
                    at = 32 + gen_index(z, x, c)
                    metas[j] = jnp.where(lane == at, column, metas[j])
        table = late_ref[lax.rem(me, 8), z][112:128].astype(f32)
        for slot in range(2):
            extra = jnp.where(line == 2 * z + slot, table[slot : slot + 1], extra)
        part = nt_dot(scaled, jnp.concatenate(pieces, axis=0))
        out_ref[:, z * 896 : (z + 1) * 896] = part.astype(bf16)
    for j in range(2):
        meta_ref[16 * j : 16 * j + 16, :] = metas[j]
    squares = jnp.sum(wide * wide, axis=1, keepdims=True)
    high = squares.astype(bf16).astype(f32)
    low = squares - high
    lane = lax.broadcasted_iota(i32, (TP * 8, 128), 1)
    extra = jnp.where(lane < 64, 0.0, extra)
    extra = jnp.where(lane == 0, high, jnp.where(lane == 1, low, extra))
    out_ref[:, QKV:] = extra.astype(bf16)


def output_kernel(mixed_ref, weights_ref, x_ref, rows_ref, packed_ref):
    part = jnp.zeros((128, 384), f32)
    for z in range(4):
        weights = []
        for g in range(8):
            piece = weights_ref[g, z]
            tail = piece[160:208]
            other = swap_halves(tail.astype(f32)).astype(bf16)
            tail = jnp.concatenate([tail, other[16:48]], axis=0)
            weights.append(jnp.concatenate([piece[0:80], piece[80:160], tail], axis=1))
        part = part + jnp.dot(
            mixed_ref[:, 640 * z : 640 * z + 640],
            jnp.concatenate(weights, axis=0),
            preferred_element_type=f32,
        )
    rows = (x_ref[...].astype(f32) + part[:, :320]).astype(bf16)
    rows_ref[...] = rows
    tail = rows[:, 256:320].astype(f32)
    tail = jnp.concatenate([tail[0:64], tail[64:128]], axis=1).astype(bf16)
    for z in range(4):
        packed_ref[z, 0:128, :] = rows[:, 0:128]
        packed_ref[z, 128:256, :] = rows[:, 128:256]
        packed_ref[z, 256:320, :] = tail


def attend_kernel(parts_ref, cache_ref, lengths_ref, cos_ref, sin_ref, mixed_ref, entry_ref):
    total = parts_ref[0].astype(f32)
    for t in range(1, TP):
        total = total + parts_ref[t].astype(f32)
    squares = total[:, QKV : QKV + 1] + total[:, QKV + 1 : QKV + 2]
    total = total[:, :QKV] * lax.rsqrt(squares / D + epsilon)
    cosine, sine = cos_ref[...], sin_ref[...]

    def head(index):
        return total[:, index * HEAD_SIZE : (index + 1) * HEAD_SIZE]

    def rotated(index):
        vec = head(index)
        swapped = jnp.concatenate([vec[:, HEAD_SIZE // 2 :], vec[:, : HEAD_SIZE // 2]], axis=1)
        return vec * cosine + swapped * sine

    rows = 8 * GROUP
    row = lax.rem(lax.broadcasted_iota(i32, (8, OWN * PLACES), 0), OWN)
    lane = lax.broadcasted_iota(i32, (8, OWN * PLACES), 1)
    old_ok = jnp.logical_and(lane // PLACES == row, lax.rem(lane, PLACES) < lengths_ref[:, :1])
    old_bias = jnp.tile(jnp.where(old_ok, 0.0, -jnp.inf), (GROUP, 1))
    slot = lax.broadcasted_iota(i32, (8, 8), 1)
    fresh = lax.broadcasted_iota(i32, (8, 8), 0)
    new_ok = jnp.logical_and(lax.rem(slot, OWN) == lax.rem(fresh, OWN), slot // OWN <= fresh // OWN)
    new_bias = jnp.tile(jnp.where(new_ok, 0.0, -jnp.inf), (GROUP, 1))
    scale = HEAD_SIZE ** (-0.5)
    width = KEY_VALUE_HEADS * HEAD_SIZE
    for k in range(KEY_VALUE_HEADS):
        at = k * HEAD_SIZE
        new_k = rotated(QUERY_HEADS + k).astype(bf16)
        new_v = head(QUERY_HEADS + KEY_VALUE_HEADS + k).astype(bf16)
        entry_ref[:, at : at + HEAD_SIZE] = new_k
        entry_ref[:, width + at : width + at + HEAD_SIZE] = new_v
        query = jnp.concatenate([rotated(k * GROUP + h) for h in range(GROUP)], axis=0).astype(bf16)
        old_k = cache_ref[:, :, at : at + HEAD_SIZE].reshape(OWN * PLACES, HEAD_SIZE)
        old_v = cache_ref[:, :, width + at : width + at + HEAD_SIZE].reshape(OWN * PLACES, HEAD_SIZE)
        old_s = nt_dot(query, old_k) * scale + old_bias
        new_s = nt_dot(query, new_k) * scale + new_bias
        peak = jnp.maximum(
            jnp.max(old_s, axis=1, keepdims=True), jnp.max(new_s, axis=1, keepdims=True)
        )
        old_e, new_e = jnp.exp(old_s - peak), jnp.exp(new_s - peak)
        whole = jnp.sum(old_e, axis=1, keepdims=True) + jnp.sum(new_e, axis=1, keepdims=True)
        old_w, new_w = (old_e / whole).astype(bf16), (new_e / whole).astype(bf16)
        mixed = jnp.dot(old_w, old_v, preferred_element_type=f32)
        mixed = mixed + jnp.dot(new_w, new_v, preferred_element_type=f32)
        for h in range(GROUP):
            to = (k * GROUP + h) * HEAD_SIZE
            part = mixed[8 * h : 8 * h + 8].astype(bf16)
            for t in range(TP):
                mixed_ref[t, :, to : to + HEAD_SIZE] = part


def select_kernel(layer_ref, spot_ref, out_ref):
    owners = out_ref.shape[0]
    lane = lax.broadcasted_iota(i32, (16 * owners, 256), 1)
    low = lax.broadcasted_iota(i32, (256, 128), 1) < 64
    tails = jnp.zeros((16 * owners, 128), f32)
    for half in range(2):
        pieces = [layer_ref[2 * half], layer_ref[2 * half + 1]]
        sides = [jnp.concatenate([p[256:], swap_halves(p[256:].astype(f32)).astype(bf16)], axis=0) for p in pieces]
        tail = jnp.concatenate(sides, axis=0).astype(f32)
        if half:
            tail = swap_halves(tail)
        tail = jnp.where(low if half == 0 else jnp.logical_not(low), tail, 0.0).astype(bf16)
        pick = (spot_ref[:, half : half + 1] == lane).astype(f32).astype(bf16)
        for part in range(2):
            rows = jnp.concatenate([p[128 * part : 128 * part + 128] for p in pieces], axis=0)
            taken = jnp.dot(pick, rows, preferred_element_type=f32).astype(bf16)
            at = 32 * part + 16 * half
            out_ref[:, at : at + 16, :] = taken.reshape(owners, 16, 128)
        tails = tails + jnp.dot(pick, tail, preferred_element_type=f32)
    out_ref[:, 64:80, :] = tails.astype(bf16).reshape(owners, 16, 128)


def logits_kernel(rows_ref, gain_ref, head_ref, offset_ref, out_ref):
    def piece(t):
        tail = rows_ref[:, t, 64:80, :].reshape(128, 128).astype(f32)
        tail = [tail.reshape(8, 16, 128), swap_halves(tail).reshape(8, 16, 128)]
        parts = [rows_ref[:, t, 0:32, :].reshape(256, 128), rows_ref[:, t, 32:64, :].reshape(256, 128)]
        wide = [p.astype(f32) for p in parts]
        return wide + [jnp.concatenate(tail, axis=1).reshape(256, 128)[:, :64]]

    squares = jnp.zeros((256, 128), f32)
    tails = jnp.zeros((256, 64), f32)
    for t in range(TP):
        a, b, c = piece(t)
        squares = squares + (a * a + b * b)
        tails = tails + c * c
    total = jnp.sum(squares, axis=1, keepdims=True) + jnp.sum(tails, axis=1, keepdims=True)
    factor = lax.rsqrt(total / D + epsilon)
    logits = jnp.zeros((256, 2 * BLOCK), f32)
    for t in range(TP):
        at = t * 320
        for value, width in zip(piece(t), (128, 128, 64)):
            normed = (value * factor * gain_ref[:, at : at + width].astype(f32)).astype(bf16)
            weights = head_ref[at : at + width, :]
            logits = logits + jnp.dot(normed, weights, preferred_element_type=f32)
            at += width
    pair = lax.broadcasted_iota(i32, (256, BLOCK), 0)
    logits = jnp.where(lax.rem(pair // 4, 2) == 0, logits[:, :BLOCK], logits[:, BLOCK:])
    token = lax.broadcasted_iota(i32, (BLOCK, 128), 0)
    line = lax.broadcasted_iota(i32, (8, 128), 0)
    for half in range(2):
        side = logits[128 * half : 128 * half + 128].T
        peak = jnp.max(side, axis=0, keepdims=True)
        mass = jnp.sum(jnp.exp(side - peak), axis=0, keepdims=True)
        target = offset_ref[:, 128 * half : 128 * half + 128] - 1
        picked = jnp.sum(jnp.where(token == target, side, 0.0), axis=0, keepdims=True)
        out = jnp.where(line == 0, peak, jnp.where(line == 1, mass, picked))
        out_ref[:, 128 * half : 128 * half + 128] = out


def rows_kernel(stats_ref, row_ref, out_ref):
    mine = lax.broadcasted_iota(i32, (ROWS, GEN), 0)
    lane = lax.broadcasted_iota(i32, (ROWS, 128), 1)
    out = jnp.zeros((ROWS, 128), f32)
    for s in range(STEPS):
        best = jnp.full((ROWS, 1), -jnp.inf, f32)
        combos = [(j, slot) for j in range(2) for slot in range(2)]
        masks = [row_ref[2 * j + slot : 2 * j + slot + 1, :] == mine for j, slot in combos]

        def stat(which, j, slot):
            at = which * 8 + j * 4 + slot * 2 + s
            return stats_ref[at : at + 1, :]

        for mask, (j, slot) in zip(masks, combos):
            peak = jnp.where(mask, stat(0, j, slot), -jnp.inf)
            best = jnp.maximum(best, jnp.max(peak, axis=1, keepdims=True))
        mass = jnp.zeros((ROWS, 1), f32)
        picked = jnp.zeros((ROWS, 1), f32)
        for mask, (j, slot) in zip(masks, combos):
            grown = stat(1, j, slot) * jnp.exp(jnp.where(mask, stat(0, j, slot), best) - best)
            mass = mass + jnp.sum(jnp.where(mask, grown, 0.0), axis=1, keepdims=True)
            picked = picked + jnp.sum(
                jnp.where(mask, stat(2, j, slot), 0.0), axis=1, keepdims=True
            )
        for at, value in enumerate((best, mass, picked)):
            out = jnp.where(lane == 3 * s + at, value, out)
    out_ref[...] = out


def gen_index(z, x, core):
    return (z * 4 + x) * 2 + core


Z_GROUPS = [[gen_index(z, x, c) for z in range(4)] for x in range(4) for c in range(2)]
X_GROUPS = [[gen_index(z, x, c) for x in range(4)] for z in range(4) for c in range(2)]


LAYERS = [[z * 128 + i for i in range(128)] for z in range(4)]


XC_GROUPS = [[z * 8 + i for i in range(8)] for z in range(4)]


def all_to_all(value, axis, groups=None):
    return lax.all_to_all(
        value, axis, split_axis=0, concat_axis=0, tiled=True, axis_index_groups=groups
    )


def spread(value, axis, count, groups=None):
    return all_to_all(jnp.broadcast_to(value[None], (count,) + value.shape), axis, groups)


def rotary_tables(lengths):
    half = HEAD_SIZE // 2
    exponent = jnp.arange(half, dtype=f32) * (2.0 / HEAD_SIZE)
    inverse = jnp.power(f32(rope_base), -exponent)
    positions = (jnp.arange(STEPS, dtype=i32)[:, None] + lengths[None, :]).reshape(-1)
    angles = positions.astype(f32)[:, None] * inverse[None, :]
    cosine, sine = jnp.cos(angles), jnp.sin(angles)
    return (
        jnp.concatenate([cosine, cosine], axis=1),
        jnp.concatenate([-sine, sine], axis=1),
    )


def row_table(kept):
    row = jnp.arange(ROWS, dtype=i32)[:, None]
    match = jnp.any(kept[:, :, None] == jnp.arange(ROWS, dtype=i32), axis=1)
    first = jnp.min(jnp.where(match, row, ROWS - 1), axis=0)
    last = jnp.max(jnp.where(match, row, 0), axis=0)
    return jnp.stack([first, last], axis=1)


def body(embeddings, cache, lengths, attn_gain, wqkv, wout, final_gain, head, kept, chosen):
    rank = lax.axis_index("tp").astype(i32)
    me = lax.axis_index("gen").astype(i32)
    features = D // TP

    table = jnp.concatenate([kept[0], chosen.T], axis=1)
    piece = call(
        pack_kernel, shape((4, 496, 128), bf16), rank.reshape(1), wqkv, table, wout, scalars=1
    )
    along_z = all_to_all(piece, "gen", Z_GROUPS)
    out_whole = lax.all_gather(along_z[:, 288:], "gen", axis_index_groups=XC_GROUPS)
    late_w = lax.all_gather(along_z[:, 160:288], "gen", axis_index_groups=XC_GROUPS)
    own_w = spread(along_z[:, :160], "gen", 4, X_GROUPS).reshape(16, 160, 128)
    other_w = lax.ppermute(own_w, "gen", [(g, g ^ 1) for g in range(GEN)])

    x = embeddings.reshape(STEPS, TP, OWN, features).transpose(1, 0, 2, 3).reshape(128, features)
    parts, meta = call(
        project_kernel,
        (shape((128, QKV + 128), bf16), shape((32, 128), f32)),
        me.reshape(1),
        x,
        attn_gain.reshape(1, features),
        own_w,
        other_w,
        late_w,
        scalars=1,
    )
    parts = all_to_all(parts.reshape(TP, 8, QKV + 128), "tp")

    meta = meta.reshape(2, 16, 128)[:, :6, 32:64].astype(i32).reshape(2, 3, 2, GEN)
    offset = meta[:, 1:].reshape(2, 2, 2, 4, 8).transpose(4, 3, 0, 2, 1).reshape(1, 256)
    routes = lax.dynamic_slice_in_dim(parts[:, :, QKV + 64 :], me // 8 * 16, 16, 2)
    row = routes.astype(f32).astype(i32).reshape(TP, 2, 2, 2, 8, 2).transpose(4, 0, 2, 5, 3, 1)
    spot = jnp.arange(2, dtype=i32)[:, None, None, None] * 128 + row // OWN * 8 + row % OWN
    spot = spot[:, :, :, :, :, None, :] + jnp.arange(STEPS, dtype=i32)[:, None] * OWN
    spot = spot.reshape(16 * 128, 2)

    cosine, sine = rotary_tables(lengths)
    wide_lengths = jnp.broadcast_to(jnp.tile(lengths, STEPS)[:, None], (8, 128))
    mixed, entries = call(
        attend_kernel,
        (shape((TP, 8, QUERY_HEADS * HEAD_SIZE), bf16), shape((8, 1024), bf16)),
        parts,
        cache,
        wide_lengths,
        cosine,
        sine,
    )
    mixed = all_to_all(mixed, "tp").reshape(128, QUERY_HEADS * HEAD_SIZE)
    layer_out, packed = call(
        output_kernel,
        (shape((128, features), bf16), shape((4, 320, 128), bf16)),
        mixed,
        out_whole,
        x,
    )
    last_hidden = layer_out.reshape(TP, STEPS, OWN, features)[:, -1].reshape(ROWS, features)

    layers = all_to_all(packed, "gen", Z_GROUPS)
    taken = call(select_kernel, shape((128, 80, 128), bf16), layers, spot)
    taken = all_to_all(taken, ("gen", "tp"), LAYERS).reshape(8, TP, 80, 128)
    stats = call(
        logits_kernel,
        shape((8, 256), f32),
        taken,
        final_gain.reshape(1, D),
        head,
        offset,
    )
    stats = stats[:3].reshape(3, 8, 4, 8).transpose(2, 1, 0, 3).reshape(GEN, 1, 24)
    stats = all_to_all(stats, "gen").reshape(GEN, 24).T
    rows_of = row_table(kept[0]).reshape(GEN, 4).T
    row_stats = call(rows_kernel, shape((ROWS, 128), f32), stats, rows_of)
    row_stats = all_to_all(row_stats.reshape(TP, OWN, 128)[:, :, :8], "tp")
    peak, mass, picked = (row_stats[:, :, i : 3 * STEPS : 3] for i in range(3))
    best = jnp.max(peak, axis=0)
    mass = jnp.sum(mass * jnp.exp(peak - best), axis=0)
    logprobs = jnp.sum(picked, axis=0) - best - jnp.log(mass)
    return logprobs.T, last_hidden, entries.reshape(STEPS, OWN, 1024)


def solution(mesh):
    return jax.shard_map(
        body,
        mesh=mesh,
        in_specs=(
            P(None, "gen", "tp"),
            P(("gen", "tp"), None, None),
            P(("gen", "tp")),
            P("tp"),
            P("tp", "gen"),
            P("gen", "tp"),
            P(),
            P(None, ("gen", "tp")),
            P("tp", "gen", None),
            P(None, "gen"),
        ),
        out_specs=(P(None, ("gen", "tp")), P("gen", "tp"), P(None, ("gen", "tp"), None)),
        check_vma=False,
    )
```

```python
import jax
import jax.numpy as jnp
from jax import lax
from jax.experimental import pallas as pl
from jax.experimental.pallas import tpu as pltpu
from jax.sharding import PartitionSpec as P

D = 5120
QUERY_HEADS = 20
KEY_VALUE_HEADS = 4
GROUP = QUERY_HEADS // KEY_VALUE_HEADS
HEAD_SIZE = 128
BLOCK = 128
KPS = 2
STEPS = 2
QKV = 3584
GEN = 32
TP = 16
ROWS = 64
OWN = ROWS // TP
PLACES = 128

epsilon = 1e-06
rope_base = 1000000.0

bf16 = jnp.bfloat16
f32 = jnp.float32
i32 = jnp.int32
MIB = 1024 * 1024


def call(kernel, out_shape, *args, scalars=0, scratch=(), vmem=48):
    specs = [pl.BlockSpec(memory_space=pltpu.SMEM)] * scalars
    specs += [pl.BlockSpec(memory_space=pltpu.VMEM)] * (len(args) - scalars)
    return pl.pallas_call(
        kernel,
        out_shape=out_shape,
        in_specs=specs,
        out_specs=jax.tree.map(lambda _: pl.BlockSpec(memory_space=pltpu.VMEM), out_shape),
        scratch_shapes=list(scratch),
        compiler_params=pltpu.CompilerParams(vmem_limit_bytes=vmem * MIB),
    )(*args)


def shape(dims, dtype):
    return jax.ShapeDtypeStruct(dims, dtype)


def nt_dot(a, b):
    return lax.dot_general(a, b, (((1,), (1,)), ((), ())), preferred_element_type=f32)


def swap_halves(value):
    return jnp.concatenate([value[:, 64:], value[:, :64]], axis=1)


def unpack(piece, rows):
    tail = piece[2 * rows :]
    other = swap_halves(tail.astype(f32)).astype(bf16)
    tail = jnp.concatenate([tail, other[: rows - 64]], axis=0)
    return jnp.concatenate([piece[:rows], piece[rows : 2 * rows], tail], axis=1)


def pack_kernel(rank_ref, weights_ref, table_ref, wout_ref, out_ref):
    wide = wout_ref[...].astype(f32)
    out_ref[288:368, :] = wide[:, 0:128].astype(bf16)
    out_ref[368:448, :] = wide[:, 128:256].astype(bf16)
    tail = jnp.concatenate([wide[0:48, 256:320], wide[32:80, 256:320]], axis=1)
    out_ref[448:496, :] = tail.astype(bf16)
    turned = weights_ref[...].astype(f32).T
    out_ref[0:112, :] = turned[:, 0:128].astype(bf16)
    out_ref[112:224, :] = turned[:, 128:256].astype(bf16)
    block = lax.broadcasted_iota(i32, (ROWS, ROWS), 1)
    row = lax.broadcasted_iota(i32, (ROWS, ROWS), 0)
    named = [table_ref[:, k : k + 1] == block for k in range(KPS)]
    match = jnp.logical_or(named[0], named[1])
    first = jnp.min(jnp.where(match, row, ROWS - 1), axis=0, keepdims=True)
    last = jnp.max(jnp.where(match, row, 0), axis=0, keepdims=True)
    line = lax.broadcasted_iota(i32, (16, ROWS), 0)
    meta = jnp.where(line == 0, first, jnp.where(line == 1, last, 0))
    for s in range(STEPS):
        code = table_ref[:, KPS + s : KPS + s + 1]
        offset = jnp.zeros((ROWS, ROWS), i32)
        for k in range(KPS):
            here = jnp.logical_and(code // BLOCK == rank_ref[0] * KPS + k, named[k])
            offset = jnp.where(here, lax.rem(code, BLOCK) + 1, offset)
        for slot, target in enumerate((first, last)):
            value = jnp.sum(jnp.where(row == target, offset, 0), axis=0, keepdims=True)
            meta = jnp.where(line == 2 + 2 * s + slot, value, meta)
    side = jnp.concatenate([turned[64:112, 256:320], meta.astype(f32)], axis=0)
    out_ref[224:288, :] = jnp.concatenate([turned[0:64, 256:320], side], axis=1).astype(bf16)


def project_kernel(me_ref, x_ref, gain_ref, own_ref, other_ref, out_ref, meta_ref):
    me = me_ref[0]
    core = lax.rem(me, 2)
    wide = x_ref[...].astype(f32)
    scaled = (wide * gain_ref[...].astype(f32)).astype(bf16)
    scaled = jnp.concatenate([scaled, jnp.zeros((128, 64), bf16)], axis=1)
    lane = lax.broadcasted_iota(i32, (16, 128), 1)
    metas = [jnp.zeros((16, 128), f32), jnp.zeros((16, 128), f32)]
    line = lax.rem(lax.broadcasted_iota(i32, (TP * 8, 128), 0), 8)
    extra = jnp.zeros((TP * 8, 128), f32)
    for z in range(4):
        pieces = []
        for x in range(4):
            a = own_ref[x * 4 + z]
            b = other_ref[x * 4 + z]
            for c, piece in enumerate((jnp.where(core == 0, a, b), jnp.where(core == 0, b, a))):
                pieces.append(unpack(piece, 112))
                table = piece[272:288].astype(f32)
                for j in range(2):
                    mine = jnp.where(lane == 64 + 2 * me + j, table, 0.0)
                    column = jnp.sum(mine, axis=1, keepdims=True)
                    at = 32 + gen_index(z, x, c)
                    metas[j] = jnp.where(lane == at, column, metas[j])
        table = own_ref[lax.rem(me // 2, 4) * 4 + z][272:288].astype(f32)
        for slot in range(2):
            extra = jnp.where(line == 2 * z + slot, table[slot : slot + 1], extra)
        part = nt_dot(scaled, jnp.concatenate(pieces, axis=0))
        out_ref[:, z * 896 : (z + 1) * 896] = part.astype(bf16)
    for j in range(2):
        meta_ref[16 * j : 16 * j + 16, :] = metas[j]
    squares = jnp.sum(wide * wide, axis=1, keepdims=True)
    high = squares.astype(bf16).astype(f32)
    low = squares - high
    lane = lax.broadcasted_iota(i32, (TP * 8, 128), 1)
    extra = jnp.where(lane < 64, 0.0, extra)
    extra = jnp.where(lane == 0, high, jnp.where(lane == 1, low, extra))
    out_ref[:, QKV:] = extra.astype(bf16)


def output_kernel(mixed_ref, weights_ref, x_ref, rows_ref, packed_ref):
    part = jnp.zeros((128, 384), f32)
    for z in range(4):
        weights = []
        for g in range(8):
            piece = weights_ref[g, z]
            tail = piece[160:208]
            other = swap_halves(tail.astype(f32)).astype(bf16)
            tail = jnp.concatenate([tail, other[16:48]], axis=0)
            weights.append(jnp.concatenate([piece[0:80], piece[80:160], tail], axis=1))
        part = part + jnp.dot(
            mixed_ref[:, 640 * z : 640 * z + 640],
            jnp.concatenate(weights, axis=0),
            preferred_element_type=f32,
        )
    rows = (x_ref[...].astype(f32) + part[:, :320]).astype(bf16)
    rows_ref[...] = rows
    packed_ref[0:128, :] = rows[:, 0:128]
    packed_ref[128:256, :] = rows[:, 128:256]
    tail = rows[:, 256:320].astype(f32)
    packed_ref[256:320, :] = jnp.concatenate([tail[0:64], tail[64:128]], axis=1).astype(bf16)


def attend_kernel(parts_ref, cache_ref, lengths_ref, cos_ref, sin_ref, mixed_ref, entry_ref):
    total = parts_ref[0].astype(f32)
    for t in range(1, TP):
        total = total + parts_ref[t].astype(f32)
    squares = total[:, QKV : QKV + 1] + total[:, QKV + 1 : QKV + 2]
    total = total[:, :QKV] * lax.rsqrt(squares / D + epsilon)
    cosine, sine = cos_ref[...], sin_ref[...]

    def head(index):
        return total[:, index * HEAD_SIZE : (index + 1) * HEAD_SIZE]

    def rotated(index):
        vec = head(index)
        swapped = jnp.concatenate([vec[:, HEAD_SIZE // 2 :], vec[:, : HEAD_SIZE // 2]], axis=1)
        return vec * cosine + swapped * sine

    rows = 8 * GROUP
    row = lax.rem(lax.broadcasted_iota(i32, (8, OWN * PLACES), 0), OWN)
    lane = lax.broadcasted_iota(i32, (8, OWN * PLACES), 1)
    old_ok = jnp.logical_and(lane // PLACES == row, lax.rem(lane, PLACES) < lengths_ref[:, :1])
    old_bias = jnp.tile(jnp.where(old_ok, 0.0, -jnp.inf), (GROUP, 1))
    slot = lax.broadcasted_iota(i32, (8, 8), 1)
    fresh = lax.broadcasted_iota(i32, (8, 8), 0)
    new_ok = jnp.logical_and(lax.rem(slot, OWN) == lax.rem(fresh, OWN), slot // OWN <= fresh // OWN)
    new_bias = jnp.tile(jnp.where(new_ok, 0.0, -jnp.inf), (GROUP, 1))
    scale = HEAD_SIZE ** (-0.5)
    width = KEY_VALUE_HEADS * HEAD_SIZE
    for k in range(KEY_VALUE_HEADS):
        at = k * HEAD_SIZE
        new_k = rotated(QUERY_HEADS + k).astype(bf16)
        new_v = head(QUERY_HEADS + KEY_VALUE_HEADS + k).astype(bf16)
        entry_ref[:, at : at + HEAD_SIZE] = new_k
        entry_ref[:, width + at : width + at + HEAD_SIZE] = new_v
        query = jnp.concatenate([rotated(k * GROUP + h) for h in range(GROUP)], axis=0).astype(bf16)
        old_k = cache_ref[:, :, at : at + HEAD_SIZE].reshape(OWN * PLACES, HEAD_SIZE)
        old_v = cache_ref[:, :, width + at : width + at + HEAD_SIZE].reshape(OWN * PLACES, HEAD_SIZE)
        old_s = nt_dot(query, old_k) * scale + old_bias
        new_s = nt_dot(query, new_k) * scale + new_bias
        peak = jnp.maximum(
            jnp.max(old_s, axis=1, keepdims=True), jnp.max(new_s, axis=1, keepdims=True)
        )
        old_e, new_e = jnp.exp(old_s - peak), jnp.exp(new_s - peak)
        whole = jnp.sum(old_e, axis=1, keepdims=True) + jnp.sum(new_e, axis=1, keepdims=True)
        old_w, new_w = (old_e / whole).astype(bf16), (new_e / whole).astype(bf16)
        mixed = jnp.dot(old_w, old_v, preferred_element_type=f32)
        mixed = mixed + jnp.dot(new_w, new_v, preferred_element_type=f32)
        for h in range(GROUP):
            to = (k * GROUP + h) * HEAD_SIZE
            mixed_ref[:, to : to + HEAD_SIZE] = mixed[8 * h : 8 * h + 8].astype(bf16)


def select_kernel(layer_ref, spot_ref, out_ref):
    owners = out_ref.shape[0]
    lane = lax.broadcasted_iota(i32, (16 * owners, 256), 1)
    low = lax.broadcasted_iota(i32, (256, 128), 1) < 64
    tails = jnp.zeros((16 * owners, 128), f32)
    for half in range(2):
        pieces = [layer_ref[2 * half], layer_ref[2 * half + 1]]
        sides = [jnp.concatenate([p[256:], swap_halves(p[256:].astype(f32)).astype(bf16)], axis=0) for p in pieces]
        tail = jnp.concatenate(sides, axis=0).astype(f32)
        if half:
            tail = swap_halves(tail)
        tail = jnp.where(low if half == 0 else jnp.logical_not(low), tail, 0.0).astype(bf16)
        pick = (spot_ref[:, half : half + 1] == lane).astype(f32).astype(bf16)
        for part in range(2):
            rows = jnp.concatenate([p[128 * part : 128 * part + 128] for p in pieces], axis=0)
            taken = jnp.dot(pick, rows, preferred_element_type=f32).astype(bf16)
            at = 32 * part + 16 * half
            out_ref[:, at : at + 16, :] = taken.reshape(owners, 16, 128)
        tails = tails + jnp.dot(pick, tail, preferred_element_type=f32)
    out_ref[:, 64:80, :] = tails.astype(bf16).reshape(owners, 16, 128)


def logits_kernel(rows_ref, gain_ref, head_ref, offset_ref, out_ref):
    def piece(t):
        tail = rows_ref[:, t, 64:80, :].reshape(128, 128).astype(f32)
        tail = [tail.reshape(8, 16, 128), swap_halves(tail).reshape(8, 16, 128)]
        parts = [rows_ref[:, t, 0:32, :].reshape(256, 128), rows_ref[:, t, 32:64, :].reshape(256, 128)]
        wide = [p.astype(f32) for p in parts]
        return wide + [jnp.concatenate(tail, axis=1).reshape(256, 128)[:, :64]]

    squares = jnp.zeros((256, 128), f32)
    tails = jnp.zeros((256, 64), f32)
    for t in range(TP):
        a, b, c = piece(t)
        squares = squares + (a * a + b * b)
        tails = tails + c * c
    total = jnp.sum(squares, axis=1, keepdims=True) + jnp.sum(tails, axis=1, keepdims=True)
    factor = lax.rsqrt(total / D + epsilon)
    logits = jnp.zeros((256, 2 * BLOCK), f32)
    for t in range(TP):
        at = t * 320
        for value, width in zip(piece(t), (128, 128, 64)):
            normed = (value * factor * gain_ref[:, at : at + width].astype(f32)).astype(bf16)
            weights = head_ref[at : at + width, :]
            logits = logits + jnp.dot(normed, weights, preferred_element_type=f32)
            at += width
    pair = lax.broadcasted_iota(i32, (256, BLOCK), 0)
    logits = jnp.where(lax.rem(pair // 4, 2) == 0, logits[:, :BLOCK], logits[:, BLOCK:])
    token = lax.broadcasted_iota(i32, (BLOCK, 128), 0)
    line = lax.broadcasted_iota(i32, (8, 128), 0)
    for half in range(2):
        side = logits[128 * half : 128 * half + 128].T
        peak = jnp.max(side, axis=0, keepdims=True)
        mass = jnp.sum(jnp.exp(side - peak), axis=0, keepdims=True)
        target = offset_ref[:, 128 * half : 128 * half + 128] - 1
        picked = jnp.sum(jnp.where(token == target, side, 0.0), axis=0, keepdims=True)
        out = jnp.where(line == 0, peak, jnp.where(line == 1, mass, picked))
        out_ref[:, 128 * half : 128 * half + 128] = out


def rows_kernel(stats_ref, row_ref, out_ref):
    mine = lax.broadcasted_iota(i32, (ROWS, GEN), 0)
    lane = lax.broadcasted_iota(i32, (ROWS, 128), 1)
    out = jnp.zeros((ROWS, 128), f32)
    for s in range(STEPS):
        best = jnp.full((ROWS, 1), -jnp.inf, f32)
        combos = [(j, slot) for j in range(2) for slot in range(2)]
        masks = [row_ref[2 * j + slot : 2 * j + slot + 1, :] == mine for j, slot in combos]

        def stat(which, j, slot):
            at = which * 8 + j * 4 + slot * 2 + s
            return stats_ref[at : at + 1, :]

        for mask, (j, slot) in zip(masks, combos):
            peak = jnp.where(mask, stat(0, j, slot), -jnp.inf)
            best = jnp.maximum(best, jnp.max(peak, axis=1, keepdims=True))
        mass = jnp.zeros((ROWS, 1), f32)
        picked = jnp.zeros((ROWS, 1), f32)
        for mask, (j, slot) in zip(masks, combos):
            grown = stat(1, j, slot) * jnp.exp(jnp.where(mask, stat(0, j, slot), best) - best)
            mass = mass + jnp.sum(jnp.where(mask, grown, 0.0), axis=1, keepdims=True)
            picked = picked + jnp.sum(
                jnp.where(mask, stat(2, j, slot), 0.0), axis=1, keepdims=True
            )
        for at, value in enumerate((best, mass, picked)):
            out = jnp.where(lane == 3 * s + at, value, out)
    out_ref[...] = out


def gen_index(z, x, core):
    return (z * 4 + x) * 2 + core


Z_GROUPS = [[gen_index(z, x, c) for z in range(4)] for x in range(4) for c in range(2)]
X_GROUPS = [[gen_index(z, x, c) for x in range(4)] for z in range(4) for c in range(2)]


LAYERS = [[z * 128 + i for i in range(128)] for z in range(4)]


XC_GROUPS = [[z * 8 + i for i in range(8)] for z in range(4)]


def all_to_all(value, axis, groups=None):
    return lax.all_to_all(
        value, axis, split_axis=0, concat_axis=0, tiled=True, axis_index_groups=groups
    )


def spread(value, axis, count, groups=None):
    return all_to_all(jnp.broadcast_to(value[None], (count,) + value.shape), axis, groups)


def rotary_tables(lengths):
    half = HEAD_SIZE // 2
    exponent = jnp.arange(half, dtype=f32) * (2.0 / HEAD_SIZE)
    inverse = jnp.power(f32(rope_base), -exponent)
    positions = (jnp.arange(STEPS, dtype=i32)[:, None] + lengths[None, :]).reshape(-1)
    angles = positions.astype(f32)[:, None] * inverse[None, :]
    cosine, sine = jnp.cos(angles), jnp.sin(angles)
    return (
        jnp.concatenate([cosine, cosine], axis=1),
        jnp.concatenate([-sine, sine], axis=1),
    )


def row_table(kept):
    row = jnp.arange(ROWS, dtype=i32)[:, None]
    match = jnp.any(kept[:, :, None] == jnp.arange(ROWS, dtype=i32), axis=1)
    first = jnp.min(jnp.where(match, row, ROWS - 1), axis=0)
    last = jnp.max(jnp.where(match, row, 0), axis=0)
    return jnp.stack([first, last], axis=1)


def body(embeddings, cache, lengths, attn_gain, wqkv, wout, final_gain, head, kept, chosen):
    rank = lax.axis_index("tp").astype(i32)
    me = lax.axis_index("gen").astype(i32)
    features = D // TP

    table = jnp.concatenate([kept[0], chosen.T], axis=1)
    piece = call(
        pack_kernel, shape((496, 128), bf16), rank.reshape(1), wqkv, table, wout, scalars=1
    )
    along_z = spread(piece, "gen", 4, Z_GROUPS)
    out_whole = lax.all_gather(along_z[:, 288:], "gen", axis_index_groups=XC_GROUPS)
    own_w = spread(along_z[:, :288], "gen", 4, X_GROUPS).reshape(16, 288, 128)
    other_w = lax.ppermute(own_w, "gen", [(g, g ^ 1) for g in range(GEN)])

    x = embeddings.reshape(STEPS, TP, OWN, features).transpose(1, 0, 2, 3).reshape(128, features)
    parts, meta = call(
        project_kernel,
        (shape((128, QKV + 128), bf16), shape((32, 128), f32)),
        me.reshape(1),
        x,
        attn_gain.reshape(1, features),
        own_w,
        other_w,
        scalars=1,
    )
    parts = all_to_all(parts.reshape(TP, 8, QKV + 128), "tp")

    meta = meta.reshape(2, 16, 128)[:, :6, 32:64].astype(i32).reshape(2, 3, 2, GEN)
    offset = meta[:, 1:].reshape(2, 2, 2, 4, 8).transpose(4, 3, 0, 2, 1).reshape(1, 256)
    routes = lax.dynamic_slice_in_dim(parts[:, :, QKV + 64 :], me // 8 * 16, 16, 2)
    row = routes.astype(f32).astype(i32).reshape(TP, 2, 2, 2, 8, 2).transpose(4, 0, 2, 5, 3, 1)
    spot = jnp.arange(2, dtype=i32)[:, None, None, None] * 128 + row // OWN * 8 + row % OWN
    spot = spot[:, :, :, :, :, None, :] + jnp.arange(STEPS, dtype=i32)[:, None] * OWN
    spot = spot.reshape(16 * 128, 2)

    cosine, sine = rotary_tables(lengths)
    wide_lengths = jnp.broadcast_to(jnp.tile(lengths, STEPS)[:, None], (8, 128))
    mixed, entries = call(
        attend_kernel,
        (shape((8, QUERY_HEADS * HEAD_SIZE), bf16), shape((8, 1024), bf16)),
        parts,
        cache,
        wide_lengths,
        cosine,
        sine,
    )
    mixed = spread(mixed, "tp", TP).reshape(128, QUERY_HEADS * HEAD_SIZE)
    layer_out, packed = call(
        output_kernel,
        (shape((128, features), bf16), shape((320, 128), bf16)),
        mixed,
        out_whole,
        x,
    )
    last_hidden = layer_out.reshape(TP, STEPS, OWN, features)[:, -1].reshape(ROWS, features)

    layers = spread(packed, "gen", 4, Z_GROUPS)
    taken = call(select_kernel, shape((128, 80, 128), bf16), layers, spot)
    taken = all_to_all(taken, ("gen", "tp"), LAYERS).reshape(8, TP, 80, 128)
    stats = call(
        logits_kernel,
        shape((8, 256), f32),
        taken,
        final_gain.reshape(1, D),
        head,
        offset,
        vmem=60,
    )
    stats = stats[:3].reshape(3, 8, 4, 8).transpose(2, 1, 0, 3).reshape(GEN, 1, 24)
    stats = all_to_all(stats, "gen").reshape(GEN, 24).T
    rows_of = row_table(kept[0]).reshape(GEN, 4).T
    row_stats = call(rows_kernel, shape((ROWS, 128), f32), stats, rows_of)
    row_stats = all_to_all(row_stats.reshape(TP, OWN, 128)[:, :, :8], "tp")
    peak, mass, picked = (row_stats[:, :, i : 3 * STEPS : 3] for i in range(3))
    best = jnp.max(peak, axis=0)
    mass = jnp.sum(mass * jnp.exp(peak - best), axis=0)
    logprobs = jnp.sum(picked, axis=0) - best - jnp.log(mass)
    return logprobs.T, last_hidden, entries.reshape(STEPS, OWN, 1024)


def solution(mesh):
    return jax.shard_map(
        body,
        mesh=mesh,
        in_specs=(
            P(None, "gen", "tp"),
            P(("gen", "tp"), None, None),
            P(("gen", "tp")),
            P("tp"),
            P("tp", "gen"),
            P("gen", "tp"),
            P(),
            P(None, ("gen", "tp")),
            P("tp", "gen", None),
            P(None, "gen"),
        ),
        out_specs=(P(None, ("gen", "tp")), P("gen", "tp"), P(None, ("gen", "tp"), None)),
        check_vma=False,
    )
```
